32 devices in a mesh: batch: 4 (over z), ctx: 4 (over y, core), heads: 2 (over x).
Axes of the slice: x: 2, y: 2, z: 4, core: 2. Of those that a mesh axis runs over, the one named last changes fastest.
Arguments:
- tokens: bfloat16 [49152, 768], P(('batch', 'ctx', 'heads')), may hold values from -6 to 6
- lengths: int32 [4, 2], P('batch'), may hold values from 1536 to 10752, as said below
- gain_one: float32 [768], replicated, may hold values from 0.25 to 1.75
- w_qkv: bfloat16 [768, 3, 768], P(None, None, 'heads'), may hold values from -0.21875 to 0.21875
- f_query: bfloat16 [12, 64, 64], P('heads'), may hold values from -1.5 to 1.5
- f_key: bfloat16 [12, 64, 64], P('heads'), may hold values from -1.5 to 1.5
- w_out: bfloat16 [768, 768], P('heads'), may hold values from -3.5 to 3.5
- gain_two: float32 [768], replicated, may hold values from 0.25 to 1.75
- w_up: bfloat16 [768, 3072], P(None, 'heads'), may hold values from -0.21875 to 0.21875
- w_down: bfloat16 [3072, 768], P('heads'), may hold values from -0.109375 to 0.109375
- d_out: bfloat16 [49152, 768], P(('batch', 'ctx', 'heads')), may hold values from -6 to 6
Outputs:
- mixed: bfloat16 [49152, 768], P(('batch', 'ctx', 'heads'))
- grad_tokens: bfloat16 [49152, 768], P(('batch', 'ctx', 'heads'))
- grad_gain_one: float32 [768], replicated
- grad_w_qkv: float32 [768, 3, 768], P(None, None, 'heads')
- grad_f_query: float32 [12, 64, 64], P('heads')
- grad_f_key: float32 [12, 64, 64], P('heads')
- grad_w_out: float32 [768, 768], P('heads')
- grad_gain_two: float32 [768], replicated
- grad_w_up: float32 [768, 3072], P(None, 'heads')
- grad_w_down: float32 [3072, 768], P('heads')
The draws below stay inside these ranges and needn't reach their ends.
Inputs may be any that keep to these rules, and one draw needn't show every extreme that they name: `lengths`: each row holds 1536 and 10752 in one of the two orders.
All inputs are finite; a program needn't handle non-finite values.
Results may differ from the reference program's by a relative error of at most 0.015.
Values may be sent and summed in bfloat16 or wider, within the bound.
No kernel may reach another device: no remote copies, remote signals or barrier semaphores. Data moves between devices by JAX's collectives and lax.ppermute only.
A program may use at most 448 MiB of HBM per device.

```python
import jax
import jax.numpy as jnp
from jax import lax

D = 768
H = 12
HEAD = 64
FF = 3072
SPAN = 64
GROUP = 12288
GROUPS = 4
TOKENS = 49152


def draw_lengths(key, part):
    key = jax.random.fold_in(key, 11)
    flips = jax.random.randint(key, (GROUPS,), 0, 2)
    shorter = GROUP // 8
    leading = jnp.where(flips == 1, GROUP - shorter, shorter)
    return jnp.stack([leading, GROUP - leading], axis=1).astype(jnp.int32)


def levels(rng, shape, cuts, least, largest):
    factor_of, own = 1.0, jax.random.fold_in(rng, 6)
    for axis_at, blocks in cuts:
        steps = jnp.exp(jax.random.uniform(jax.random.fold_in(own, axis_at), (blocks,), jnp.float32, least / len(cuts), largest / len(cuts)))
        factor_of = factor_of * jnp.repeat(steps, shape[axis_at] // blocks).reshape([-1 if axis == axis_at else 1 for axis in range(len(shape))])
    return factor_of


def bell_draw(rng, shape, deviation, limit, cuts=(), kind=jnp.bfloat16):
    gain = levels(rng, shape, cuts, -0.22, 0.18) if cuts else 1.0
    entries = jax.random.normal(rng, shape, jnp.float32) * deviation * gain
    return jnp.minimum(jnp.maximum(entries, -limit), limit).astype(kind)


def setup_inputs(seed: int = 0) -> dict:
    keys = jax.random.split(jax.random.key(seed), 12)
    return {
        "tokens": bell_draw(keys[0], (TOKENS, D), 1.0, 6.0, ((0, 32),)),
        "lengths": draw_lengths(jax.random.fold_in(keys[11], 71), 0),
        "gain_one": jnp.clip(1.0 + 0.15 * jax.random.normal(keys[2], (D,), jnp.float32), 0.25, 1.75),
        "w_qkv": bell_draw(keys[3], (D, 3, D), D ** -0.5, 0.21875, ((2, 2),)),
        "f_query": bell_draw(keys[4], (H, HEAD, HEAD), (HEAD // 4) ** -0.5, 1.5, ((0, 2),)),
        "f_key": bell_draw(keys[5], (H, HEAD, HEAD), (HEAD // 4) ** -0.5, 1.5, ((0, 2),)),
        "w_out": bell_draw(keys[6], (D, D), (max(D // 256, 1)) ** -0.5, 3.5, ((0, 2),)),
        "gain_two": jnp.clip(1.0 + 0.15 * jax.random.normal(keys[7], (D,), jnp.float32), 0.25, 1.75),
        "w_up": bell_draw(keys[8], (D, FF), D ** -0.5, 0.21875, ((1, 2),)),
        "w_down": bell_draw(keys[9], (FF, D), FF ** -0.5, 0.109375, ((0, 2),)),
        "d_out": bell_draw(keys[10], (TOKENS, D), 1.0, 6.0, ((0, 32),)),
    }


@jax.custom_vjp
def low(v):
    return lax.optimization_barrier(v.astype(jnp.bfloat16)).astype(jnp.float32)

@jax.custom_vjp
def low_back(v):
    return v

def low_keep(v):
    return (low(v), None)

def low_pass(kept, grad):
    return (grad,)

def back_keep(v):
    return (v, None)

def back_low(kept, grad):
    return (low(grad),)
low.defvjp(low_keep, low_pass)
low_back.defvjp(back_keep, back_low)
highest = lax.Precision.HIGHEST
epsilon = 1e-05

def layer_norm(values, norm_gain):
    centred = values - lax.optimization_barrier(jnp.mean(values, axis=1, keepdims=True))
    return centred * lax.rsqrt(lax.optimization_barrier(jnp.mean(centred * centred, axis=1, keepdims=True)) + epsilon) * norm_gain

def feature_map(vectors, feature_weights):
    logits = jnp.einsum('rhe,hef->rhf', vectors, feature_weights, precision=highest)
    return jnp.concatenate([jax.nn.softmax(logits, axis=-1), jax.nn.softmax(-logits, axis=-1)], axis=-1)

def block_forward(inputs, gain_one, w_qkv, f_query, f_key, w_out, gain_two, w_up, w_down, second):
    span_count = GROUP // SPAN
    h_one = low(layer_norm(inputs, gain_one))
    joined = low_back(low(jnp.dot(h_one, w_qkv.reshape(D, 3 * D), precision=highest)))
    vectors = joined.reshape(GROUP, 3, H, HEAD)
    phi_query = low(feature_map(vectors[:, 0], f_query)).reshape(span_count, SPAN, H, 2 * HEAD)
    phi_key = low(feature_map(vectors[:, 1], f_key)).reshape(span_count, SPAN, H, 2 * HEAD)
    values = vectors[:, 2].reshape(span_count, SPAN, H, HEAD)
    doc_masks = jnp.stack([1.0 - second, second]).reshape(2, span_count, SPAN)
    key_masked = doc_masks[:, :, :, None, None] * phi_key[None]
    key_state = jnp.einsum('dcjhf,cjhe->dchfe', key_masked, values, precision=highest)
    norm_state = lax.optimization_barrier(jnp.sum(key_masked, axis=2))
    key_before = jnp.concatenate([jnp.zeros_like(key_state[:, :1]), jnp.cumsum(key_state, axis=1)[:, :-1]], axis=1)
    norm_before = jnp.concatenate([jnp.zeros_like(norm_state[:, :1]), jnp.cumsum(norm_state, axis=1)[:, :-1]], axis=1)
    query_masked = doc_masks[:, :, :, None, None] * phi_query[None]
    numerator = jnp.einsum('dcihf,dchfe->cihe', query_masked, key_before, precision=highest)
    denominator = jnp.einsum('dcihf,dchf->cih', query_masked, norm_before, precision=highest)
    second_spans = second.reshape(span_count, SPAN)
    causal = jnp.tril(jnp.ones((SPAN, SPAN), second.dtype))
    allowed = jnp.where(second_spans[:, :, None] == second_spans[:, None, :], causal[None], 0.0)
    scores = jnp.einsum('cihf,cjhf->chij', phi_query, phi_key, precision=highest) * allowed[:, None]
    numerator = numerator + jnp.einsum('chij,cjhe->cihe', scores, values, precision=highest)
    denominator = denominator + jnp.einsum('chij->cih', scores)
    attended = low_back(low((numerator / denominator[..., None]).reshape(GROUP, D)))
    resid = low_back(inputs + jnp.dot(attended, w_out, precision=highest))
    h_two = low(layer_norm(resid, gain_two))
    pre_act = low_back(jnp.dot(h_two, w_up, precision=highest))
    activation = low(jax.nn.gelu(pre_act, approximate=True))
    return resid + jnp.dot(activation, w_down, precision=highest)

def reference(tokens, lengths, gain_one, w_qkv, f_query, f_key, w_out, gain_two, w_up, w_down, d_out):
    weights = (gain_one.astype(jnp.float32), w_qkv.astype(jnp.float32), f_query.astype(jnp.float32), f_key.astype(jnp.float32), w_out.astype(jnp.float32), gain_two.astype(jnp.float32), w_up.astype(jnp.float32), w_down.astype(jnp.float32))
    inputs = tokens.astype(jnp.float32).reshape(GROUPS, GROUP, D)
    cotangent = d_out.astype(jnp.float32).reshape(GROUPS, GROUP, D)
    positions = jnp.arange(GROUP, dtype=jnp.int32)

    def group_step(totals, sliced):
        group_in, group_cot, group_len = sliced
        second = (positions >= group_len[0]).astype(jnp.float32)

        def forward(values, *params):
            return block_forward(values, *params, second)
        group_out, pullback = jax.vjp(forward, group_in, *weights)
        gradients = pullback(group_cot)
        summed = jax.tree.map(jnp.add, totals, tuple(gradients[1:]))
        return (summed, (group_out, gradients[0]))
    start_sums = tuple((jnp.zeros_like(weight) for weight in weights))
    totals, (outputs, grad_in) = lax.scan(group_step, start_sums, (inputs, cotangent, lengths))
    return (outputs.reshape(TOKENS, D).astype(jnp.bfloat16), grad_in.reshape(TOKENS, D).astype(jnp.bfloat16), totals[0], totals[1], totals[2], totals[3], totals[4], totals[5], totals[6], totals[7])
```

```python
import functools

import jax
import jax.numpy as jnp
from jax import lax
from jax.experimental import pallas as pl
from jax.experimental.pallas import tpu as pltpu
from jax.sharding import PartitionSpec as P

epsilon = 1e-05
f32 = jnp.float32
bf16 = jnp.bfloat16
CHUNK = 256
VMEM_LIMIT = 60 * 1024 * 1024
GELU_A = 0.7978845608028654
GELU_B = 0.044715


def dot(left, right):
    return lax.dot_general(left, right, (((1,), (0,)), ((), ())), preferred_element_type=f32)


def dot_t(left, right):
    return lax.dot_general(left, right, (((1,), (1,)), ((), ())), preferred_element_type=f32)


def params():
    return pltpu.CompilerParams(
        dimension_semantics=("arbitrary",), vmem_limit_bytes=VMEM_LIMIT
    )


def cost(flops, bytes_accessed):
    return pl.CostEstimate(flops=int(flops), bytes_accessed=int(bytes_accessed), transcendentals=0)


def once(shape):
    zeros = (0,) * len(shape)
    return pl.BlockSpec(shape, lambda *_: zeros, pipeline_mode=pl.Buffered(1))


def first_lanes():
    return lax.broadcasted_iota(jnp.int32, (1, 128), 1) < 64


def first_sublanes():
    return lax.broadcasted_iota(jnp.int32, (128, 1), 0) < 64


def half_blocks(size):
    rows = lax.broadcasted_iota(jnp.int32, (size, size), 0) // 64
    cols = lax.broadcasted_iota(jnp.int32, (size, size), 1) // 64
    return rows, cols


def soft_halves(logits, ones_blocks):
    first = first_lanes()
    parts = []
    for h in range(2):
        own = logits[:, 128 * h : 128 * h + 128]
        low = jnp.max(jnp.where(first, own, -jnp.inf), axis=1, keepdims=True)
        high = jnp.max(jnp.where(first, -jnp.inf, own), axis=1, keepdims=True)
        parts.append(jnp.exp(own - jnp.where(first, low, high)))
    grown = jnp.concatenate(parts, axis=1)
    return grown / dot(grown.astype(bf16), ones_blocks)


def norm_parts(values):
    centred = values - jnp.mean(values, axis=1, keepdims=True)
    spread = lax.rsqrt(jnp.mean(centred * centred, axis=1, keepdims=True) + epsilon)
    return centred * spread, spread


def norm_back(gradient, normed, spread, gain):
    scaled = gradient * gain
    return spread * (
        scaled
        - jnp.mean(scaled, axis=1, keepdims=True)
        - normed * jnp.mean(scaled * normed, axis=1, keepdims=True)
    )


def norm_kernel(tokens, gain, h_out):
    normed, _ = norm_parts(tokens[...].astype(f32))
    h_out[...] = (normed * gain[...]).astype(bf16)


def norm_one(tokens, gain):
    rows, width = tokens.shape
    return pl.pallas_call(
        norm_kernel,
        grid=(rows // 512,),
        in_specs=[pl.BlockSpec((512, width), lambda c: (c, 0)), once((1, width))],
        out_specs=pl.BlockSpec((512, width), lambda c: (c, 0)),
        out_shape=jax.ShapeDtypeStruct((rows, width), bf16),
        compiler_params=params(),
        cost_estimate=cost(0, 4 * rows * width),
        name="norm_one",
    )(tokens, gain)


def keys_kernel(pairs, h, w_kv, fext, ones, k_out, v_out, phi_out, prefix_out, state_out, state):
    step = pl.program_id(0)
    wide = 128 * pairs

    @pl.when(step == 0)
    def _():
        state[...] = jnp.zeros_like(state)

    prefix_out[0] = state[...].astype(bf16)
    kv = dot(h[...], w_kv[...]).astype(bf16)
    k_out[...] = kv[:, :wide]
    v_out[...] = kv[:, wide:]
    top = first_sublanes()
    for p in range(pairs):
        k_two = kv[:, 128 * p : 128 * p + 128]
        v_two = kv[:, wide + 128 * p : wide + 128 * p + 128]
        phi = soft_halves(dot(k_two, fext[p]), ones[...]).astype(bf16)
        phi_out[:, 256 * p : 256 * p + 256] = phi
        turned = v_two.astype(f32).T
        for h_at in range(2):
            sel = top if h_at == 0 else jnp.logical_not(top)
            padded = jnp.where(sel, turned, 1.0).astype(bf16)
            state[2 * p + h_at] += dot(padded, phi[:, 128 * h_at : 128 * h_at + 128])

    @pl.when(step == pl.num_programs(0) - 1)
    def _():
        write_state(state, state_out, pairs)


def write_state(state, state_out, pairs):
    top = first_sublanes()
    sums = []
    for p in range(pairs):
        state_out[128 * p : 128 * p + 128] = jnp.where(top, state[2 * p], state[2 * p + 1])
        sums.append(state[2 * p, 64:65, :])
        sums.append(state[2 * p + 1, 0:1, :])
    tail = state_out.shape[0] - 128 * pairs
    sums.append(jnp.zeros((tail - 2 * pairs, 128), f32))
    state_out[128 * pairs :] = jnp.concatenate(sums, axis=0)


def read_state(packed, p, h_at, pairs):
    row = 128 * pairs + 2 * p + h_at
    whole = packed[128 * p : 128 * p + 128, :]
    sums = packed[row : row + 1, :]
    sel = first_sublanes() if h_at == 0 else jnp.logical_not(first_sublanes())
    return jnp.where(sel, whole, sums)


def key_pass(h, w_kv, fext, ones):
    rows, width = h.shape
    pairs = fext.shape[0]
    wide = 128 * pairs
    count = rows // CHUNK
    packed = wide + 16
    return pl.pallas_call(
        functools.partial(keys_kernel, pairs),
        grid=(count,),
        in_specs=[
            pl.BlockSpec((CHUNK, width), lambda c: (c, 0)),
            once(w_kv.shape),
            once(fext.shape),
            once(ones.shape),
        ],
        out_specs=[
            pl.BlockSpec((CHUNK, wide), lambda c: (c, 0)),
            pl.BlockSpec((CHUNK, wide), lambda c: (c, 0)),
            pl.BlockSpec((CHUNK, 2 * wide), lambda c: (c, 0)),
            pl.BlockSpec((1, 2 * pairs, 128, 128), lambda c: (c, 0, 0, 0)),
            pl.BlockSpec((packed, 128), lambda c: (0, 0)),
        ],
        out_shape=[
            jax.ShapeDtypeStruct((rows, wide), bf16),
            jax.ShapeDtypeStruct((rows, wide), bf16),
            jax.ShapeDtypeStruct((rows, 2 * wide), bf16),
            jax.ShapeDtypeStruct((count, 2 * pairs, 128, 128), bf16),
            jax.ShapeDtypeStruct((packed, 128), f32),
        ],
        scratch_shapes=[pltpu.VMEM((2 * pairs, 128, 128), f32)],
        compiler_params=params(),
        cost_estimate=cost(6 * rows * width * wide, 12 * rows * width),
        name="key_pass",
    )(h, w_kv, fext, ones)


def query_kernel(pairs, h, w_q, k_phi, v, prefix, fext, ones, q_out, phi_out, numer_out):
    q = dot(h[...], w_q[...]).astype(bf16)
    q_out[...] = q
    first = first_lanes()
    size = h.shape[0]
    past = lax.broadcasted_iota(jnp.int32, (size, size), 0) >= lax.broadcasted_iota(
        jnp.int32, (size, size), 1
    )
    for p in range(pairs):
        phi = soft_halves(dot(q[:, 128 * p : 128 * p + 128], fext[p]), ones[...]).astype(bf16)
        phi_out[:, 256 * p : 256 * p + 256] = phi
        v_two = v[:, 128 * p : 128 * p + 128].astype(f32)
        for h_at in range(2):
            at = 256 * p + 128 * h_at
            sel = first if h_at == 0 else jnp.logical_not(first)
            padded = jnp.where(sel, v_two, 1.0).astype(bf16)
            phi_q = phi[:, 128 * h_at : 128 * h_at + 128]
            scores = jnp.where(past, dot_t(phi_q, k_phi[:, at : at + 128]), 0.0).astype(bf16)
            numer_out[:, at : at + 128] = dot(scores, padded) + dot_t(
                phi_q, prefix[0, 2 * p + h_at]
            )


def query_pass(h, w_q, k_phi, v, prefix, fext, ones):
    rows, width = h.shape
    pairs = fext.shape[0]
    wide = 128 * pairs
    return pl.pallas_call(
        functools.partial(query_kernel, pairs),
        grid=(rows // CHUNK,),
        in_specs=[
            pl.BlockSpec((CHUNK, width), lambda c: (c, 0)),
            once(w_q.shape),
            pl.BlockSpec((CHUNK, 2 * wide), lambda c: (c, 0)),
            pl.BlockSpec((CHUNK, wide), lambda c: (c, 0)),
            pl.BlockSpec((1, 2 * pairs, 128, 128), lambda c: (c, 0, 0, 0)),
            once(fext.shape),
            once(ones.shape),
        ],
        out_specs=[
            pl.BlockSpec((CHUNK, wide), lambda c: (c, 0)),
            pl.BlockSpec((CHUNK, 2 * wide), lambda c: (c, 0)),
            pl.BlockSpec((CHUNK, 2 * wide), lambda c: (c, 0)),
        ],
        out_shape=[
            jax.ShapeDtypeStruct((rows, wide), bf16),
            jax.ShapeDtypeStruct((rows, 2 * wide), bf16),
            jax.ShapeDtypeStruct((rows, 2 * wide), f32),
        ],
        compiler_params=params(),
        cost_estimate=cost(5 * rows * width * wide, 16 * rows * width),
        name="query_pass",
    )(h, w_q, k_phi, v, prefix, fext, ones)


def middle_kernel(
    pairs,
    tile,
    tokens,
    d_out,
    numer_own,
    numer_oth,
    phi_own,
    phi_oth,
    incoming,
    wo_own,
    wo_oth,
    up_own,
    up_oth,
    down_own,
    down_oth,
    gain,
    cross,
    attended_out,
    act_out,
    pre_out,
    h_out,
    mixed_out,
    resid_out,
    gn_out,
    gd_out,
    state_out,
    held,
    exact,
    inverse,
    state,
):
    step = pl.program_id(0)
    first = first_lanes()
    top = first_sublanes()
    wide = 128 * pairs
    numer = (numer_own, numer_oth)
    phi = (phi_own, phi_oth)

    @pl.when(step == 0)
    def _():
        state[...] = jnp.zeros_like(state)
        for half in range(2):
            for p in range(pairs):
                for h_at in range(2):
                    held[half, 2 * p + h_at] = read_state(
                        incoming.at[half], p, h_at, pairs
                    ).astype(bf16)

    for half in range(2):
        for p in range(pairs):
            sums = []
            for h_at in range(2):
                at = 256 * p + 128 * h_at
                sums.append(
                    numer[half][:, at : at + 128]
                    + dot_t(phi[half][:, at : at + 128], held[half, 2 * p + h_at])
                )
            numerator = jnp.where(first, sums[0], sums[1])
            swapped = 1.0 / jnp.where(first, sums[1], sums[0])
            inv = pltpu.roll(swapped, 64, 1)
            value = numerator * inv
            at = wide * half + 128 * p
            exact[:, at : at + 128] = value
            inverse[:, at : at + 128] = swapped
            attended_out[:, at : at + 128] = value.astype(bf16)

    resid = (
        tokens[...].astype(f32)
        + dot(attended_out[:, :wide], wo_own[...])
        + dot(attended_out[:, wide:], wo_oth[...])
    )
    normed, spread = norm_parts(resid)
    h_two = (normed * gain[...]).astype(bf16)
    h_out[...] = h_two
    d_low = d_out[...]
    units = up_own.shape[1]
    mixed = grad_h = None
    for half in range(2):
        up = (up_own, up_oth)[half]
        down = (down_own, down_oth)[half]
        for at in range(0, units, tile):
            pre = dot(h_two, up[:, at : at + tile])
            square = pre * pre
            swing = jnp.tanh(GELU_A * pre * (1.0 + GELU_B * square))
            half_up = 0.5 + 0.5 * swing
            act = (pre * half_up).astype(bf16)
            slope = half_up + (0.5 * GELU_A) * pre * (1.0 - swing * swing) * (
                1.0 + (3.0 * GELU_B) * square
            )
            grad_act = dot_t(d_low, down[at : at + tile, :])
            grad_pre = (grad_act * slope).astype(bf16)
            act_out[:, half * units + at : half * units + at + tile] = act
            pre_out[:, half * units + at : half * units + at + tile] = grad_pre
            part = dot(act, down[at : at + tile, :])
            mixed = part if mixed is None else mixed + part
            part = dot_t(grad_pre, up[:, at : at + tile])
            grad_h = part if grad_h is None else grad_h + part
    mixed_out[...] = (resid + mixed).astype(bf16)
    grad_resid = (d_low.astype(f32) + norm_back(grad_h, normed, spread, gain[...])).astype(bf16)
    resid_out[...] = grad_resid

    for half in range(2):
        grad_att = dot_t(grad_resid, (wo_own, wo_oth)[half][...]).astype(bf16).astype(f32)
        for p in range(pairs):
            at = wide * half + 128 * p
            own = grad_att[:, 128 * p : 128 * p + 128]
            swapped = inverse[:, at : at + 128]
            grad_n = own * pltpu.roll(swapped, 64, 1)
            total = dot((own * exact[:, at : at + 128]).astype(bf16), cross[...])
            grad_d = (-1.0 / 64.0) * total * swapped
            gn_out[:, at : at + 128] = grad_n.astype(bf16)
            gd_out[:, at : at + 128] = grad_d.astype(bf16)
            turned_n = grad_n.T
            turned_d = grad_d.T
            for h_at in range(2):
                sel = top if h_at == 0 else jnp.logical_not(top)
                padded = jnp.where(sel, turned_n, turned_d).astype(bf16)
                lane = 256 * p + 128 * h_at
                state[half, 2 * p + h_at] += dot(padded, phi[half][:, lane : lane + 128])

    @pl.when(step == pl.num_programs(0) - 1)
    def _():
        for half in range(2):
            write_state(state.at[half], state_out.at[half], pairs)


def middle_pass(
    tokens, d_out, numers, phis, incoming, w_outs, w_ups, w_downs, gain, cross, block, tile
):
    rows, width = tokens.shape
    wide = w_outs[0].shape[0]
    pairs = wide // 128
    units = w_ups[0].shape[1]
    by_rows = lambda cols: pl.BlockSpec((block, cols), lambda c: (c, 0))
    out = lambda cols: jax.ShapeDtypeStruct((rows, cols), bf16)
    cols_out = [2 * wide, 2 * units, 2 * units, width, width, width, 2 * wide, 2 * wide]
    return pl.pallas_call(
        functools.partial(middle_kernel, pairs, tile),
        grid=(rows // block,),
        in_specs=[by_rows(width)] * 2
        + [by_rows(2 * wide)] * 4
        + [once(incoming.shape)]
        + [once(w.shape) for w in (*w_outs, *w_ups, *w_downs)]
        + [once(gain.shape), once(cross.shape)],
        out_specs=[by_rows(c) for c in cols_out]
        + [pl.BlockSpec(incoming.shape, lambda c: (0, 0, 0))],
        out_shape=[out(c) for c in cols_out] + [jax.ShapeDtypeStruct(incoming.shape, f32)],
        scratch_shapes=[
            pltpu.VMEM((2, 2 * pairs, 128, 128), bf16),
            pltpu.VMEM((block, 2 * wide), f32),
            pltpu.VMEM((block, 2 * wide), f32),
            pltpu.VMEM((2, 2 * pairs, 128, 128), f32),
        ],
        compiler_params=params(),
        cost_estimate=cost(
            2 * rows * width * (8 * units + 8 * wide), 20 * rows * (units + width)
        ),
        name="middle_pass",
    )(tokens, d_out, *numers, *phis, incoming, *w_outs, *w_ups, *w_downs, gain, cross)


def weight_kernel(steps, half, *refs):
    count = len(steps)
    lefts, rights = refs[:count], refs[count : 2 * count]
    outs, turned = refs[2 * count : 2 * count + 2], refs[2 * count + 2]
    step = pl.program_id(0)
    whole = sum(steps)

    @pl.when(step == 0)
    def _():
        for i in range(count):
            turned[i] = lefts[i][...].T

    start = 0
    for i in range(count):

        def product(i=i):
            return dot(turned[i], rights[i][...]).astype(bf16)

        for side in range(2):
            low = side * whole + start

            @pl.when(jnp.logical_and(step >= low, step < low + steps[i]))
            def _(product=product, side=side):
                outs[1 - side][...] = product()

        start += steps[i]


def weight_pass(half, lefts, rights, block):
    rows, width = lefts[0].shape
    part = width // 2
    count = len(lefts)
    steps = [r.shape[1] // 2 // block for r in rights]
    whole = sum(steps)

    def right_map(i):
        start = sum(steps[:i])

        def at(step, half):
            place = step % whole - start
            inside = jnp.clip(place, 0, steps[i] - 1)
            return (0, (1 - step // whole) * steps[i] + inside)

        return at

    own_map = lambda step, half: (0, jnp.maximum(step - whole, 0))
    oth_map = lambda step, half: (0, jnp.minimum(step, whole - 1))
    spec = pltpu.PrefetchScalarGridSpec(
        num_scalar_prefetch=1,
        grid=(2 * whole,),
        in_specs=[
            pl.BlockSpec((rows, part), lambda step, half: (0, half[0]), pipeline_mode=pl.Buffered(1))
            for _ in lefts
        ]
        + [pl.BlockSpec((rows, block), right_map(i)) for i in range(count)],
        out_specs=[pl.BlockSpec((part, block), own_map), pl.BlockSpec((part, block), oth_map)],
        scratch_shapes=[pltpu.VMEM((count, part, rows), bf16)],
    )
    shape = jax.ShapeDtypeStruct((part, whole * block), bf16)
    return pl.pallas_call(
        functools.partial(weight_kernel, steps),
        grid_spec=spec,
        out_shape=[shape, shape],
        compiler_params=params(),
        cost_estimate=cost(
            2 * rows * part * 2 * whole * block, 2 * rows * (part * count + 2 * whole * block)
        ),
        name="weight_pass",
    )(half, *lefts, *rights)


def back_kernel(
    pairs,
    at_pair,
    q_own,
    q_oth,
    k_own,
    k_oth,
    v_own,
    v_oth,
    pq_own,
    pq_oth,
    pk_own,
    pk_oth,
    gn_own,
    gn_oth,
    gd_own,
    gd_oth,
    prefix_own,
    prefix_oth,
    incoming,
    later,
    fq_own,
    fq_oth,
    fk_own,
    fk_oth,
    ones,
    grad_out,
    grad_f,
    held,
    state,
):
    step = pl.program_id(0)
    first = first_lanes()
    top = first_sublanes()
    size = q_own.shape[0]
    rows = lax.broadcasted_iota(jnp.int32, (size, size), 0)
    cols = lax.broadcasted_iota(jnp.int32, (size, size), 1)

    @pl.when(step == 0)
    def _():
        grad_f[...] = jnp.zeros_like(grad_f)
        for half in range(2):
            for h_at in range(2):
                held[half, h_at] = read_state(incoming.at[half], at_pair, h_at, pairs)
                state[half, h_at] = read_state(later.at[half], at_pair, h_at, pairs)

    for half in range(2):
        q_two = (q_own, q_oth)[half][...]
        k_two = (k_own, k_oth)[half][...]
        v_two = (v_own, v_oth)[half][...].astype(f32)
        phi_q = (pq_own, pq_oth)[half][...]
        phi_k = (pk_own, pk_oth)[half][...]
        gn = (gn_own, gn_oth)[half][...].astype(f32)
        gd = (gd_own, gd_oth)[half][...].astype(f32)
        prefix = (prefix_own, prefix_oth)[half]
        turned_n = gn.T
        turned_d = gd.T
        grads_q, grads_k, grads_v = [], [], []
        for h_at in range(2):
            sel = first if h_at == 0 else jnp.logical_not(first)
            sel_top = top if h_at == 0 else jnp.logical_not(top)
            padded_v = jnp.where(sel, v_two, 1.0).astype(bf16)
            padded_g = jnp.where(sel, gn, gd).astype(bf16)
            turned = jnp.where(sel_top, turned_n, turned_d).astype(bf16)
            pq = phi_q[:, 128 * h_at : 128 * h_at + 128]
            pk = phi_k[:, 128 * h_at : 128 * h_at + 128]
            before = (prefix[0, h_at].astype(f32) + held[half, h_at]).astype(bf16)
            after = state[half, h_at].astype(bf16)
            e = jnp.where(rows >= cols, dot_t(padded_g, padded_v), 0.0).astype(bf16)
            e_t = jnp.where(rows <= cols, dot_t(padded_v, padded_g), 0.0).astype(bf16)
            s_t = jnp.where(rows <= cols, dot_t(pk, pq), 0.0).astype(bf16)
            grads_q.append(dot(e, pk) + dot(padded_g, before))
            grads_k.append(dot(e_t, pq) + dot(padded_v, after))
            grads_v.append(dot(s_t, padded_g) + dot_t(pk, after))
            state[half, h_at] += dot(turned, pq)
        for kind in range(2):
            phi = (phi_q, phi_k)[kind].astype(f32)
            grad_phi = jnp.concatenate((grads_q, grads_k)[kind], axis=1)
            shared = dot((phi * grad_phi).astype(bf16), ones[...])
            grad_u = (phi * (grad_phi - shared)).astype(bf16)
            fext = ((fq_own, fq_oth), (fk_own, fk_oth))[kind][half]
            vectors = (q_two, k_two)[kind]
            grad_out[:, 384 * half + 128 * kind : 384 * half + 128 * kind + 128] = dot_t(
                grad_u, fext[0]
            ).astype(bf16)
            grad_f[kind, half] += dot(vectors.astype(f32).T.astype(bf16), grad_u)
        grad_out[:, 384 * half + 256 : 384 * half + 384] = jnp.where(
            first, grads_v[0], grads_v[1]
        ).astype(bf16)


def back_pass(at_pair, q, k, v, pq, pk, gn, gd, prefix, incoming, later, fq, fk, ones):
    rows = q[0].shape[0]
    pairs = fq[0].shape[0]
    count = rows // CHUNK
    lanes = lambda cols, at: pl.BlockSpec((CHUNK, cols), lambda c: (count - 1 - c, at))
    states = pl.BlockSpec((1, 2, 128, 128), lambda c: (count - 1 - c, at_pair, 0, 0))
    weights = pl.BlockSpec((1, 128, 256), lambda c: (at_pair, 0, 0))
    return pl.pallas_call(
        functools.partial(back_kernel, pairs, at_pair),
        grid=(count,),
        in_specs=[lanes(128, at_pair)] * 6
        + [lanes(256, at_pair)] * 4
        + [lanes(128, at_pair), lanes(128, pairs + at_pair)] * 2
        + [states] * 2
        + [once(incoming.shape)] * 2
        + [weights] * 4
        + [once(ones.shape)],
        out_specs=[
            pl.BlockSpec((CHUNK, 768), lambda c: (count - 1 - c, 0)),
            pl.BlockSpec((2, 2, 128, 256), lambda c: (0, 0, 0, 0)),
        ],
        out_shape=[
            jax.ShapeDtypeStruct((rows, 768), bf16),
            jax.ShapeDtypeStruct((2, 2, 128, 256), f32),
        ],
        scratch_shapes=[
            pltpu.VMEM((2, 2, 128, 128), f32),
            pltpu.VMEM((2, 2, 128, 128), f32),
        ],
        compiler_params=params(),
        cost_estimate=cost(rows * 4 * 2 * 2600 * 128, rows * 6000),
        name="back_pass",
    )(*q, *k, *v, *pq, *pk, gn, gn, gd, gd, *prefix, incoming, later, *fq, *fk, ones)


def tokens_kernel(pairs, tokens, resid, w_own, w_oth, gain, *refs):
    grads, out = refs[:pairs], refs[pairs]
    normed, spread = norm_parts(tokens[...].astype(f32))
    total = None
    for half in range(2):
        joined = jnp.concatenate(
            [
                g[:, 384 * half + 128 * kind : 384 * half + 128 * kind + 128]
                for kind in range(3)
                for g in grads
            ],
            axis=1,
        )
        part = dot_t(joined, (w_own, w_oth)[half][...])
        total = part if total is None else total + part
    back = norm_back(total, normed, spread, gain[...])
    out[...] = (resid[...].astype(f32) + back).astype(bf16)


def tokens_pass(tokens, resid, w_own, w_oth, gain, grads, block):
    rows, width = tokens.shape
    by_rows = lambda cols: pl.BlockSpec((block, cols), lambda c: (c, 0))
    return pl.pallas_call(
        functools.partial(tokens_kernel, len(grads)),
        grid=(rows // block,),
        in_specs=[by_rows(width)] * 2
        + [once(w_own.shape), once(w_oth.shape), once(gain.shape)]
        + [by_rows(768)] * len(grads),
        out_specs=by_rows(width),
        out_shape=jax.ShapeDtypeStruct((rows, width), bf16),
        compiler_params=params(),
        cost_estimate=cost(4 * rows * width * w_own.shape[1], 16 * rows * width),
        name="tokens_pass",
    )(tokens, resid, w_own, w_oth, gain, *grads)


def swap(value, axis, bit):
    count = lax.axis_size(axis)
    return lax.ppermute(value, axis, [(i, i ^ (1 << bit)) for i in range(count)])


def bit_of(axis, bit):
    return (lax.axis_index(axis) >> bit) & 1


def bits_of(axis):
    return lax.axis_size(axis).bit_length() - 1


def ordered(bit, mine, theirs):
    return jnp.where(
        bit == 0, jnp.concatenate([mine, theirs], 0), jnp.concatenate([theirs, mine], 0)
    )


def fetch_other(weight):
    count = weight.shape[0] // 2
    place = bit_of("ctx", 0)
    part = lax.dynamic_slice_in_dim(weight, place * count, count, 0)
    direct = swap(part, "heads", 0)
    return ordered(place, direct, swap(direct, "ctx", 0))


def add_low(left, right):
    return (left.astype(f32) + right.astype(f32)).astype(bf16)


def reduce_rows(sends, keeps):
    own, oth = keeps
    got_own, got_oth = swap(sends[0], "ctx", 0), swap(sends[1], "ctx", 0)
    from_pair = swap(add_low(oth, got_oth), "heads", 0)
    left, right = add_low(own, got_own), from_pair
    stages = [("ctx", b) for b in range(1, bits_of("ctx"))]
    stages += [("batch", b) for b in range(bits_of("batch"))]
    for axis, bit in stages:
        place = bit_of(axis, bit)
        count = left.shape[0] // 2
        cut = lambda a, at: lax.dynamic_slice_in_dim(a, at * count, count, 0)
        got = swap(add_low(cut(left, 1 - place), cut(right, 1 - place)), axis, bit)
        left, right = add_low(cut(left, place), cut(right, place)), got
    whole = add_low(left, right)
    for axis, bit in reversed([("ctx", 0)] + stages):
        whole = ordered(bit_of(axis, bit), whole, swap(whole, axis, bit))
    return whole


def scan_runs(total, boundary, rows, backward):
    place = lax.axis_index("ctx") * 2 + lax.axis_index("heads")
    sequence = lambda index: index * rows >= boundary
    steps = [("heads", 0)] + [("ctx", b) for b in range(bits_of("ctx"))]
    received = jnp.zeros_like(total)
    for level, (axis, bit) in enumerate(steps):
        got = swap(total.astype(bf16), axis, bit).astype(f32)
        if axis == "heads":
            got = jnp.flip(got, 0)
        size = 1 << level
        base = (place >> (level + 1)) << (level + 1)
        latter = ((place >> level) & 1) == 1
        if backward:
            near, far = sequence(base), sequence(base + size)
            takes = jnp.logical_and(jnp.logical_not(latter), far == sequence(place))
        else:
            near, far = sequence(base + 2 * size - 1), sequence(base + size - 1)
            takes = jnp.logical_and(latter, far == sequence(place))
        received = received + jnp.where(takes, got, 0.0)
        joins = (near == far).astype(f32)
        keeps_mine = jnp.logical_not(latter) if backward else latter
        total = jnp.where(keeps_mine, total + joins * got, got + joins * total)
    return received


def extended(maps):
    heads, size, _ = maps.shape
    both = jnp.concatenate([maps, -maps], axis=2).reshape(heads // 2, 2, size, 2 * size)
    empty = jnp.zeros_like(both[:, 0])
    return jnp.concatenate(
        [
            jnp.concatenate([both[:, 0], empty], axis=2),
            jnp.concatenate([empty, both[:, 1]], axis=2),
        ],
        axis=1,
    )


def map_gradient(raw):
    pairs = raw.shape[0]
    joined = jnp.stack(
        [
            raw[:, :64, 0:64] - raw[:, :64, 64:128],
            raw[:, 64:, 128:192] - raw[:, 64:, 192:256],
        ],
        axis=1,
    )
    return joined.reshape(2 * pairs * 64, 64)


def shards(tokens, lengths, gain_one, w_qkv, f_query, f_key, w_out, gain_two, w_up, w_down, d_out):
    rows, width = tokens.shape
    heads, size, _ = f_query.shape
    pairs = heads // 2
    wide = heads * size
    assert size == 64 and lax.axis_size("heads") == 2 and 1536 % rows == 0
    boundary = lengths[0, 0]
    place = bit_of("ctx", 0)
    gain_one_row = gain_one.reshape(1, width)
    gain_two_row = gain_two.reshape(1, width)

    low_rows, low_cols = half_blocks(256)
    ones = (low_rows == low_cols).astype(bf16)
    cross_rows, cross_cols = half_blocks(128)
    cross = (cross_rows != cross_cols).astype(bf16)

    qkv_own = w_qkv.reshape(width, 3 * wide)
    qkv_oth = fetch_other(qkv_own)
    maps = jnp.stack([f_query, f_key])
    maps_oth = swap(maps, "heads", 0)
    out_oth = fetch_other(w_out)
    up_oth = fetch_other(w_up)
    down_oth = fetch_other(w_down)

    h_one = norm_one(tokens, gain_one_row)
    fq, fk, k, v, phi_k, prefix, totals, q, phi_q, numer = ([] for _ in range(10))
    for weights, maps_here in ((qkv_own, maps), (qkv_oth, maps_oth)):
        fq.append(extended(maps_here[0]))
        fk.append(extended(maps_here[1]))
        parts = key_pass(h_one, weights[:, wide:], fk[-1], ones)
        for held, value in zip((k, v, phi_k, prefix, totals), parts):
            held.append(value)
    incoming = scan_runs(jnp.stack(totals), boundary, rows, False)
    for at, weights in enumerate((qkv_own, qkv_oth)):
        parts = query_pass(h_one, weights[:, :wide], phi_k[at], v[at], prefix[at], fq[at], ones)
        for held, value in zip((q, phi_q, numer), parts):
            held.append(value)

    attended, act, grad_pre, h_two, mixed, grad_resid, gn, gd, grad_totals = middle_pass(
        tokens,
        d_out,
        numer,
        phi_q,
        incoming,
        (w_out, out_oth),
        (w_up, up_oth),
        (w_down, down_oth),
        gain_two_row,
        cross,
        256,
        512,
    )
    later = scan_runs(grad_totals, boundary, rows, True)

    def weight_sums(lefts, rights, block):
        send = weight_pass((1 - place).reshape(1), lefts, rights, block)
        keep = weight_pass(place.reshape(1), lefts, rights, block)
        return send, keep

    feed = reduce_rows(*weight_sums([h_two, d_out], [grad_pre, act], 768))
    out_sum = reduce_rows(*weight_sums([grad_resid], [attended], 384))

    grads, raw, qkv_sums = [], [], []
    for at in range(pairs):
        grad, raw_map = back_pass(
            at, q, k, v, phi_q, phi_k, gn, gd, prefix, incoming, later, fq, fk, ones
        )
        grads.append(grad)
        raw.append(raw_map)
        qkv_sums.append(reduce_rows(*weight_sums([h_one], [grad], 384)))
    grad_tokens = tokens_pass(tokens, grad_resid, qkv_own, qkv_oth, gain_one_row, grads, 512)

    raw = jnp.stack(raw)
    maps_sum = [
        jnp.concatenate([map_gradient(raw[:, kind, half]) for kind in range(2)], axis=0).astype(bf16)
        for half in range(2)
    ]
    count = maps_sum[0].shape[0] // 2
    cut = lambda at: [lax.dynamic_slice_in_dim(m, at * count, count, 0) for m in maps_sum]
    maps_sum = reduce_rows(cut(1 - place), cut(place)).astype(f32)

    units = w_up.shape[1]
    grad_up = feed[:, :units].astype(f32)
    grad_down = feed[:, units:].astype(f32).T
    grad_out = out_sum.astype(f32).T
    grad_qkv = jnp.concatenate(
        [s.reshape(width, 3, 128) for s in qkv_sums], axis=2
    ).astype(f32)
    gains = jnp.stack(
        [
            jnp.sum(grad_qkv * w_qkv.astype(f32), axis=(1, 2)),
            jnp.sum(grad_up * w_up.astype(f32), axis=1),
        ]
    )
    gains = (gains + swap(gains, "heads", 0)) / jnp.stack([gain_one, gain_two])
    grad_maps = maps_sum.reshape(2, heads, size, size)
    return (
        mixed,
        grad_tokens,
        gains[0],
        grad_qkv,
        grad_maps[0],
        grad_maps[1],
        grad_out,
        gains[1],
        grad_up,
        grad_down,
    )


def solution(mesh):
    in_specs = (
        P(("batch", "ctx", "heads"), None),
        P("batch", None),
        P(),
        P(None, None, "heads"),
        P("heads", None, None),
        P("heads", None, None),
        P("heads", None),
        P(),
        P(None, "heads"),
        P("heads", None),
        P(("batch", "ctx", "heads"), None),
    )
    out_specs = (
        P(("batch", "ctx", "heads"), None),
        P(("batch", "ctx", "heads"), None),
        P(),
        P(None, None, "heads"),
        P("heads", None, None),
        P("heads", None, None),
        P("heads", None),
        P(),
        P(None, "heads"),
        P("heads", None),
    )
    return jax.shard_map(shards, mesh=mesh, in_specs=in_specs, out_specs=out_specs, check_vma=False)
```

```python
import functools

import jax
import jax.numpy as jnp
from jax import lax
from jax.experimental import pallas as pl
from jax.experimental.pallas import tpu as pltpu
from jax.sharding import PartitionSpec as P

epsilon = 1e-05
f32 = jnp.float32
bf16 = jnp.bfloat16
CHUNK = 256
BLOCK = 512
VMEM_LIMIT = 60 * 1024 * 1024
GELU_A = 0.7978845608028654
GELU_B = 0.044715


def dot(left, right):
    return lax.dot_general(left, right, (((1,), (0,)), ((), ())), preferred_element_type=f32)


def dot_t(left, right):
    return lax.dot_general(left, right, (((1,), (1,)), ((), ())), preferred_element_type=f32)


def params():
    return pltpu.CompilerParams(
        dimension_semantics=("arbitrary",), vmem_limit_bytes=VMEM_LIMIT
    )


def small_cost():
    return pl.CostEstimate(flops=1000, bytes_accessed=1000, transcendentals=0)


def shaped(shape, kind=bf16):
    return jax.ShapeDtypeStruct(shape, kind)


def once(shape):
    zeros = (0,) * len(shape)
    return pl.BlockSpec(shape, lambda *_: zeros, pipeline_mode=pl.Buffered(1))


def by_rows(count, cols, at=0):
    return pl.BlockSpec((count, cols), lambda c, *_: (c, at))


def by_cols(rows, count, at=0):
    return pl.BlockSpec((rows, count), lambda c, *_: (at, c))


anywhere = pl.BlockSpec(memory_space=pl.ANY)
scalars = pl.BlockSpec(memory_space=pltpu.SMEM)


def first_lanes():
    return lax.broadcasted_iota(jnp.int32, (1, 128), 1) < 64


def first_sublanes():
    return lax.broadcasted_iota(jnp.int32, (128, 1), 0) < 64


def half_blocks(size):
    rows = lax.broadcasted_iota(jnp.int32, (size, size), 0) // 64
    cols = lax.broadcasted_iota(jnp.int32, (size, size), 1) // 64
    return rows, cols


def soft_rows(logits):
    count, size = logits.shape
    groups = logits.reshape(count // 64, 64, size)
    grown = jnp.exp(groups - jnp.max(groups, axis=1, keepdims=True))
    soft = grown * (1.0 / jnp.sum(grown, axis=1, keepdims=True))
    return soft.reshape(count, size)


def norm_parts(values):
    centred = values - jnp.mean(values, axis=1, keepdims=True)
    spread = lax.rsqrt(jnp.mean(centred * centred, axis=1, keepdims=True) + epsilon)
    return centred * spread, spread


def norm_back(gradient, normed, spread, gain):
    scaled = gradient * gain
    return spread * (
        scaled
        - jnp.mean(scaled, axis=1, keepdims=True)
        - normed * jnp.mean(scaled * normed, axis=1, keepdims=True)
    )


def run_copies(copies):
    for copy in copies:
        copy.start()
    for copy in copies:
        copy.wait()


def qkv_copies(pieces, order, kinds, target, sems, first_sem):
    rows = pieces[0].shape[1]
    copies = []
    for i, piece in enumerate(pieces):
        where = 0 if len(pieces) == 1 else pl.multiple_of(order[i] * rows, 16)
        for at, kind in enumerate(kinds):
            wide = piece.shape[2]
            copies.append(
                pltpu.make_async_copy(
                    piece.at[kind],
                    target.at[pl.ds(where, rows), pl.ds(at * wide, wide)],
                    sems.at[first_sem + len(copies)],
                )
            )
    return copies


def norm_kernel(tokens, gain, h_out, turned_out):
    normed, _ = norm_parts(tokens[...].astype(f32))
    low = (normed * gain[...]).astype(bf16)
    h_out[...] = low
    turned_out[...] = low.T


def norm_one(tokens, gain):
    rows, width = tokens.shape
    return pl.pallas_call(
        norm_kernel,
        grid=(rows // BLOCK,),
        in_specs=[by_rows(BLOCK, width), once((1, width))],
        out_specs=[by_rows(BLOCK, width), by_cols(width, BLOCK)],
        out_shape=[shaped((rows, width)), shaped((width, rows))],
        compiler_params=params(),
        cost_estimate=small_cost(),
        name="norm_one",
    )(tokens, gain)


def write_state(state, state_out, pairs):
    top = first_sublanes()
    sums = []
    for p in range(pairs):
        state_out[128 * p : 128 * p + 128] = jnp.where(top, state[2 * p], state[2 * p + 1])
        sums.append(state[2 * p, 64:65, :])
        sums.append(state[2 * p + 1, 0:1, :])
    tail = state_out.shape[0] - 128 * pairs
    sums.append(jnp.zeros((tail - 2 * pairs, 128), f32))
    state_out[128 * pairs :] = jnp.concatenate(sums, axis=0)


def read_state(packed, p, h_at, pairs):
    row = 128 * pairs + 2 * p + h_at
    whole = packed[128 * p : 128 * p + 128, :]
    sums = packed[row : row + 1, :]
    sel = first_sublanes() if h_at == 0 else jnp.logical_not(first_sublanes())
    return jnp.where(sel, whole, sums)


def keys_kernel(pairs, count, order, h, fext, *refs):
    pieces = refs[:count]
    k_out, v_out, turned_v_out, phi_out, turned_phi_out, prefix_out, state_out = refs[count : count + 7]
    w_kv, state, sems = refs[count + 7 :]
    step = pl.program_id(0)
    wide = 128 * pairs

    @pl.when(step == 0)
    def _():
        run_copies(qkv_copies(pieces, order, (1, 2), w_kv, sems, 0))
        state[...] = jnp.zeros_like(state)

    kv_all = dot(h[...], w_kv[...]).astype(bf16)
    turned_k_all = kv_all[:, :wide].T
    turned_v_all = kv_all[:, wide:].T
    k_out[...] = turned_k_all
    v_out[...] = kv_all[:, wide:]
    turned_v_out[...] = turned_v_all
    top = first_sublanes()
    one = jnp.ones((1, 1), bf16)
    for sub in range(h.shape[0] // CHUNK):
        run = slice(CHUNK * sub, CHUNK * sub + CHUNK)
        turned_k, turned_v = turned_k_all[:, run], turned_v_all[:, run]
        prefix_out[sub] = state[...].astype(bf16)
        for p in range(pairs):
            turned_phi = soft_rows(dot(fext[p], turned_k[128 * p : 128 * p + 128])).astype(bf16)
            phi = turned_phi.T
            turned_phi_out[256 * p : 256 * p + 256, run] = turned_phi
            phi_out[run, 256 * p : 256 * p + 256] = phi
            values = turned_v[128 * p : 128 * p + 128]
            for h_at in range(2):
                sel = top if h_at == 0 else jnp.logical_not(top)
                padded = jnp.where(sel, values, one)
                state[2 * p + h_at] += dot(padded, phi[:, 128 * h_at : 128 * h_at + 128])

    @pl.when(step == pl.num_programs(0) - 1)
    def _():
        write_state(state, state_out, pairs)


def key_pass(h, weights, order, fext):
    rows, width = h.shape
    pairs = fext.shape[0]
    wide = 128 * pairs
    count = rows // CHUNK
    packed = wide + 16
    return list(
        pl.pallas_call(
            functools.partial(keys_kernel, pairs, len(weights)),
            grid=(rows // BLOCK,),
            in_specs=[scalars, by_rows(BLOCK, width), once(fext.shape)]
            + [anywhere] * len(weights),
            out_specs=[
                by_cols(wide, BLOCK),
                by_rows(BLOCK, wide),
                by_cols(wide, BLOCK),
                by_rows(BLOCK, 2 * wide),
                by_cols(2 * wide, BLOCK),
                pl.BlockSpec((BLOCK // CHUNK, 2 * pairs, 128, 128), lambda c: (c, 0, 0, 0)),
                pl.BlockSpec((packed, 128), lambda c: (0, 0)),
            ],
            out_shape=[
                shaped((wide, rows)),
                shaped((rows, wide)),
                shaped((wide, rows)),
                shaped((rows, 2 * wide)),
                shaped((2 * wide, rows)),
                shaped((count, 2 * pairs, 128, 128)),
                shaped((packed, 128), f32),
            ],
            scratch_shapes=[
                pltpu.VMEM((width, 2 * wide), bf16),
                pltpu.VMEM((2 * pairs, 128, 128), f32),
                pltpu.SemaphoreType.DMA((2 * len(weights),)),
            ],
            compiler_params=params(),
            cost_estimate=small_cost(),
            name="key_pass",
        )(order, h, fext, *weights)
    )


def query_kernel(pairs, count, order, h, turned_k_phi, v, prefix, fext, *refs):
    pieces = refs[:count]
    q_out, phi_out, turned_phi_out, numer_out, w_q, sems = refs[count:]

    @pl.when(pl.program_id(0) == 0)
    def _():
        run_copies(qkv_copies(pieces, order, (0,), w_q, sems, 0))

    turned_q_all = dot(h[...], w_q[...]).astype(bf16).T
    q_out[...] = turned_q_all
    first = first_lanes()
    one = jnp.ones((1, 1), bf16)
    size = CHUNK
    past = lax.broadcasted_iota(jnp.int32, (size, size), 0) >= lax.broadcasted_iota(
        jnp.int32, (size, size), 1
    )
    for sub in range(h.shape[0] // CHUNK):
        run = slice(CHUNK * sub, CHUNK * sub + CHUNK)
        turned_q = turned_q_all[:, run]
        for p in range(pairs):
            turned_phi = soft_rows(dot(fext[p], turned_q[128 * p : 128 * p + 128])).astype(bf16)
            phi = turned_phi.T
            turned_phi_out[256 * p : 256 * p + 256, run] = turned_phi
            phi_out[run, 256 * p : 256 * p + 256] = phi
            v_two = v[run, 128 * p : 128 * p + 128]
            for h_at in range(2):
                at = 256 * p + 128 * h_at
                sel = first if h_at == 0 else jnp.logical_not(first)
                padded = jnp.where(sel, v_two, one)
                phi_q = phi[:, 128 * h_at : 128 * h_at + 128]
                scores = dot(phi_q, turned_k_phi[at : at + 128, run])
                scores = jnp.where(past, scores, 0.0).astype(bf16)
                numer_out[run, at : at + 128] = dot(scores, padded) + dot_t(
                    phi_q, prefix[sub, 2 * p + h_at]
                )


def query_pass(h, weights, order, turned_k_phi, v, prefix, fext):
    rows, width = h.shape
    pairs = fext.shape[0]
    wide = 128 * pairs
    return list(
        pl.pallas_call(
            functools.partial(query_kernel, pairs, len(weights)),
            grid=(rows // BLOCK,),
            in_specs=[
                scalars,
                by_rows(BLOCK, width),
                by_cols(2 * wide, BLOCK),
                by_rows(BLOCK, wide),
                pl.BlockSpec((BLOCK // CHUNK, 2 * pairs, 128, 128), lambda c: (c, 0, 0, 0)),
                once(fext.shape),
            ]
            + [anywhere] * len(weights),
            out_specs=[
                by_cols(wide, BLOCK),
                by_rows(BLOCK, 2 * wide),
                by_cols(2 * wide, BLOCK),
                by_rows(BLOCK, 2 * wide),
            ],
            out_shape=[
                shaped((wide, rows)),
                shaped((rows, 2 * wide)),
                shaped((2 * wide, rows)),
                shaped((rows, 2 * wide), f32),
            ],
            scratch_shapes=[
                pltpu.VMEM((width, wide), bf16),
                pltpu.SemaphoreType.DMA((len(weights),)),
            ],
            compiler_params=params(),
            cost_estimate=small_cost(),
            name="query_pass",
        )(order, h, turned_k_phi, v, prefix, fext, *weights)
    )


def middle_kernel(
    pairs,
    tile,
    order,
    tokens,
    d_out,
    numer_own,
    numer_oth,
    phi_own,
    phi_oth,
    incoming,
    gain,
    cross,
    wo_any,
    up_any,
    down_any,
    up_0,
    up_1,
    up_2,
    up_3,
    down_0,
    down_1,
    down_2,
    down_3,
    act_out,
    pre_out,
    mixed_out,
    resid_out,
    gn_out,
    gd_out,
    turned_h_out,
    turned_a_out,
    turned_n_out,
    turned_d_out,
    state_out,
    gain_out,
    held,
    attended_out,
    exact,
    inverse,
    wo_own,
    up_own,
    down_own,
    up_oth,
    down_oth,
    sems,
):
    step = pl.program_id(0)
    first = first_lanes()
    top = first_sublanes()
    wide = 128 * pairs
    units = up_own.shape[1]
    numer = (numer_own, numer_oth)
    phi = (phi_own, phi_oth)

    def weight_copies():
        copies = [
            pltpu.make_async_copy(source, target, sems.at[i])
            for i, (source, target) in enumerate(
                ((wo_any, wo_own), (up_any, up_own), (down_any, down_own))
            )
        ]
        for group, target, first_at in (
            ((up_0, up_1, up_2, up_3), up_oth, 2),
            ((down_0, down_1, down_2, down_3), down_oth, 6),
        ):
            for i, piece in enumerate(group):
                count = piece.shape[0]
                where = pl.multiple_of(order[first_at + i] * count, 16)
                copies.append(
                    pltpu.make_async_copy(
                        piece, target.at[pl.ds(where, count)], sems.at[len(copies)]
                    )
                )
        return copies

    @pl.when(step == 0)
    def _():
        for copy in weight_copies():
            copy.start()
        state_out[...] = jnp.zeros_like(state_out)
        gain_out[...] = jnp.zeros_like(gain_out)
        for half in range(2):
            for p in range(pairs):
                for h_at in range(2):
                    held[half, 2 * p + h_at] = read_state(
                        incoming.at[half], p, h_at, pairs
                    ).astype(bf16)

    for half in range(2):
        for p in range(pairs):
            sums = []
            for h_at in range(2):
                at = 256 * p + 128 * h_at
                sums.append(
                    numer[half][:, at : at + 128]
                    + dot_t(phi[half][:, at : at + 128], held[half, 2 * p + h_at])
                )
            numerator = jnp.where(first, sums[0], sums[1])
            swapped = 1.0 / jnp.where(first, sums[1], sums[0])
            inv = pltpu.roll(swapped, 64, 1)
            value = numerator * inv
            at = wide * half + 128 * p
            exact[:, at : at + 128] = value
            inverse[:, at : at + 128] = swapped
            attended = value.astype(bf16)
            attended_out[:, at : at + 128] = attended
            turned_a_out[at : at + 128, :] = attended.T

    @pl.when(step == 0)
    def _():
        for copy in weight_copies():
            copy.wait()

    wo_oth = down_oth.at[pl.ds(units, wide)]
    resid = (
        tokens[...].astype(f32)
        + dot(attended_out[:, :wide], wo_own[...])
        + dot(attended_out[:, wide:], wo_oth[...])
    )
    normed, spread = norm_parts(resid)
    h_two = (normed * gain[...]).astype(bf16)
    turned_h_out[...] = h_two.T
    d_low = d_out[...]
    mixed = grad_h = None
    for half in range(2):
        up = (up_own, up_oth)[half]
        down = (down_own, down_oth)[half]
        for at in range(0, units, tile):
            pre = dot(h_two, up[:, at : at + tile])
            square = pre * pre
            swing = jnp.tanh(GELU_A * pre * (1.0 + GELU_B * square))
            half_up = 0.5 + 0.5 * swing
            act = (pre * half_up).astype(bf16)
            slope = half_up + (0.5 * GELU_A) * pre * (1.0 - swing * swing) * (
                1.0 + (3.0 * GELU_B) * square
            )
            grad_act = dot_t(d_low, down[at : at + tile, :])
            grad_pre = (grad_act * slope).astype(bf16)
            act_out[half * units + at : half * units + at + tile, :] = act.T
            for col in range(0, tile, 256):
                spot = half * units + at + col
                pre_out[spot // 768, :, spot % 768 : spot % 768 + 256] = grad_pre[
                    :, col : col + 256
                ]
            part = dot(act, down[at : at + tile, :])
            mixed = part if mixed is None else mixed + part
            part = dot_t(grad_pre, up[:, at : at + tile])
            grad_h = part if grad_h is None else grad_h + part
    mixed_out[...] = (resid + mixed).astype(bf16)
    gain_out[...] += jnp.sum(grad_h * normed, axis=0, keepdims=True)
    grad_resid = (d_low.astype(f32) + norm_back(grad_h, normed, spread, gain[...])).astype(bf16)
    resid_out[...] = grad_resid

    for half in range(2):
        grad_att = dot_t(grad_resid, (wo_own, wo_oth)[half][...]).astype(bf16).astype(f32)
        for p in range(pairs):
            at = wide * half + 128 * p
            own = grad_att[:, 128 * p : 128 * p + 128]
            swapped = inverse[:, at : at + 128]
            grad_n = (own * pltpu.roll(swapped, 64, 1)).astype(bf16)
            total = dot((own * exact[:, at : at + 128]).astype(bf16), cross[...])
            grad_d = ((-1.0 / 64.0) * total * swapped).astype(bf16)
            gn_out[:, at : at + 128] = grad_n
            gd_out[:, at : at + 128] = grad_d
            turned_n = grad_n.T
            turned_d = grad_d.T
            turned_n_out[at : at + 128, :] = turned_n
            turned_d_out[at : at + 128, :] = turned_d
            left = jnp.concatenate([turned_n, turned_d[0:16], turned_d[64:80]], axis=0)
            sums = dot(left, phi[half][:, 256 * p : 256 * p + 256])
            state_out[half, 128 * p : 128 * p + 128] += jnp.where(
                top, sums[:128, :128], sums[:128, 128:]
            )
            row = wide + 2 * p
            state_out[half, row : row + 1] += sums[144:145, :128]
            state_out[half, row + 1 : row + 2] += sums[128:129, 128:]


def middle_pass(
    order, tokens, d_out, numers, phis, incoming, gain, cross, owns, ups, downs, block, tile
):
    rows, width = tokens.shape
    wide = owns[0].shape[0]
    pairs = wide // 128
    units = owns[1].shape[1]
    cols_out = [width, width, 2 * wide, 2 * wide]
    parts = 2 * units // 768
    return pl.pallas_call(
        functools.partial(middle_kernel, pairs, tile),
        grid=(rows // block,),
        in_specs=[scalars]
        + [by_rows(block, width)] * 2
        + [by_rows(block, 2 * wide)] * 4
        + [once(incoming.shape), once(gain.shape), once(cross.shape)]
        + [anywhere] * 11,
        out_specs=[by_cols(2 * units, block), pl.BlockSpec((parts, block, 768), lambda c: (0, c, 0))]
        + [by_rows(block, c) for c in cols_out]
        + [by_cols(width, block)]
        + [by_cols(2 * wide, block)] * 3
        + [
            pl.BlockSpec(incoming.shape, lambda c: (0, 0, 0)),
            pl.BlockSpec((1, width), lambda c: (0, 0)),
        ],
        out_shape=[shaped((2 * units, rows)), shaped((parts, rows, 768))]
        + [shaped((rows, c)) for c in cols_out]
        + [shaped((width, rows))]
        + [shaped((2 * wide, rows))] * 3
        + [shaped(incoming.shape, f32), shaped((1, width), f32)],
        scratch_shapes=[
            pltpu.VMEM((2, 2 * pairs, 128, 128), bf16),
            pltpu.VMEM((block, 2 * wide), bf16),
            pltpu.VMEM((block, 2 * wide), f32),
            pltpu.VMEM((block, 2 * wide), f32),
            pltpu.VMEM((wide, width), bf16),
            pltpu.VMEM((width, units), bf16),
            pltpu.VMEM((units, width), bf16),
            pltpu.VMEM((width, units), bf16),
            pltpu.VMEM((units + wide, width), bf16),
            pltpu.SemaphoreType.DMA((11,)),
        ],
        compiler_params=params(),
        cost_estimate=small_cost(),
        name="middle_pass",
    )(order, tokens, d_out, *numers, *phis, incoming, gain, cross, *owns, *ups, *downs)


def up_kernel(side, left, right, out):
    out[0] = dot(left[...], right[0]).astype(bf16)


def up_pass(side, left, right):
    width, rows = left.shape
    count, _, part = right.shape
    half = lambda step, side: (step // (count // 2) + side[0]) % 2
    return pl.pallas_call(
        up_kernel,
        grid_spec=pltpu.PrefetchScalarGridSpec(
            num_scalar_prefetch=1,
            grid=(count,),
            in_specs=[once((width, rows)), pl.BlockSpec((1, rows, part), lambda s, c: (s, 0, 0))],
            out_specs=pl.BlockSpec((1, width, part), lambda s, c: (half(s, c), 0, s % (count // 2))),
        ),
        out_shape=shaped((2, width, count // 2 * part)),
        compiler_params=params(),
        cost_estimate=small_cost(),
        name="up_pass",
    )(side, left, right)


def down_kernel(left, right, left_more, right_more, out):
    count = left.shape[0]
    main = dot(left[...], right[...])
    rest = dot(left_more[...], right_more[...])
    out[0, :count] = main.astype(bf16)
    out[0, count:] = rest.astype(bf16)


def down_kept_kernel(left, right, left_more, right_more, got, own_out, oth_out):
    count = left.shape[0]
    main = (dot(left[...], right[...]) + got[0, :count].astype(f32)).astype(bf16)
    rest = (dot(left_more[...], right_more[...]) + got[0, count:].astype(f32)).astype(bf16)

    @pl.when(pl.program_id(0) == 0)
    def _():
        oth_out[:count] = main
        oth_out[count:] = rest

    @pl.when(pl.program_id(0) == 1)
    def _():
        own_out[:count] = main
        own_out[count:] = rest


def down_pass(half, left, right, left_more, right_more, got=()):
    rows, width = right.shape
    part = left.shape[0] // 4
    more = left_more.shape[0] // 4
    out = pl.BlockSpec((1, part + more, width), lambda side, half: (1 - side, 0, 0))
    kept = pl.BlockSpec((part + more, width), lambda side, half: (0, 0))

    def kernel(half, *refs):
        (down_kept_kernel if got else down_kernel)(*refs)

    return pl.pallas_call(
        kernel,
        grid_spec=pltpu.PrefetchScalarGridSpec(
            num_scalar_prefetch=1,
            grid=(2,),
            in_specs=[
                pl.BlockSpec((part, rows), lambda side, half: (2 - 2 * side + half[0], 0)),
                once((rows, width)),
                pl.BlockSpec((more, rows), lambda side, half: (2 - 2 * side + half[0], 0)),
                once((rows, width)),
            ]
            + [out] * len(got),
            out_specs=[kept] * 2 if got else out,
        ),
        out_shape=[shaped((part + more, width))] * 2
        if got
        else shaped((2, part + more, width)),
        compiler_params=params(),
        cost_estimate=small_cost(),
        name="down_pass",
    )(half, left, right, left_more, right_more, *got)


def back_kernel(pairs, side, at_pair, more, core, *refs):
    (q, k, v, turned_v, pq, turned_pq, pk, turned_pk, gn, gd, turned_n, turned_d) = refs[:12]
    prefix, incoming, later, fq, fk, ones, h_any = refs[12:19]
    earlier = refs[19 : 19 + more]
    grad_out, send_out, keep_out, map_out = refs[19 + more : 23 + more]
    held, state, grads, maps, turned_h, sem = refs[23 + more :]
    step = pl.program_id(0)
    last = pl.num_programs(0) - 1
    first = first_lanes()
    top = first_sublanes()
    size = CHUNK
    inner = v.shape[0] // CHUNK
    past = lax.broadcasted_iota(jnp.int32, (size, size), 0) >= lax.broadcasted_iota(
        jnp.int32, (size, size), 1
    )
    one = jnp.ones((1, 1), bf16)

    @pl.when(step == 0)
    def _():
        pltpu.make_async_copy(h_any, turned_h, sem.at[0]).start()
        maps[...] = jnp.zeros_like(maps)
        for h_at in range(2):
            held[h_at] = read_state(incoming.at[side], at_pair, h_at, pairs)
            state[h_at] = read_state(later.at[side], at_pair, h_at, pairs)

    for sub in reversed(range(inner)):
        run = slice(CHUNK * sub, CHUNK * sub + CHUNK)
        grads_q, grads_k, grads_v = [], [], []
        for h_at in range(2):
            sel = first if h_at == 0 else jnp.logical_not(first)
            sel_top = top if h_at == 0 else jnp.logical_not(top)
            lanes = slice(128 * h_at, 128 * h_at + 128)
            padded_v = jnp.where(sel, v[run, :], one)
            padded_vt = jnp.where(sel_top, turned_v[:, run], one)
            padded_g = jnp.where(sel, gn[run, :], gd[run, :])
            padded_gt = jnp.where(sel_top, turned_n[:, run], turned_d[:, run])
            before = (prefix[sub, h_at].astype(f32) + held[h_at]).astype(bf16)
            after = state[h_at].astype(bf16)
            e = jnp.where(past, dot_t(padded_g, padded_v), 0.0).astype(bf16)
            s = jnp.where(past, dot(pq[run, lanes], turned_pk[lanes, run]), 0.0).astype(bf16)
            grads_q.append(dot(e, pk[run, lanes]) + dot(padded_g, before))
            grads_k.append(dot(turned_pq[lanes, run], e) + dot(after.T, padded_vt))
            grads_v.append(dot(padded_gt, s) + dot(after, turned_pk[lanes, run]))
            state[h_at] += dot(padded_gt, pq[run, lanes])

        grad_phi = jnp.concatenate(grads_q, axis=1)
        phi = pq[run, :].astype(f32)
        shared = dot((phi * grad_phi).astype(bf16), ones[...])
        grad_u = (phi * (grad_phi - shared)).astype(bf16)
        maps[0] += dot(q[:, run], grad_u)
        grad_q = dot_t(grad_u, fq[0]).astype(bf16)

        grad_phi = jnp.concatenate(grads_k, axis=0).reshape(4, 64, size)
        phi = turned_pk[:, run].astype(f32).reshape(4, 64, size)
        shared = jnp.sum(phi * grad_phi, axis=1, keepdims=True)
        grad_u = (phi * (grad_phi - shared)).reshape(256, size).astype(bf16)
        maps[1] += dot_t(k[:, run], grad_u)
        grad_k = dot(fk[0], grad_u).astype(bf16).T
        grad_v = jnp.where(top, grads_v[0], grads_v[1]).astype(bf16).T

        joined = jnp.concatenate([grad_q, grad_k, grad_v], axis=1)
        grad_out[run, :] = joined
        where = pl.multiple_of(((last - step) * inner + sub) * size, size)
        grads[pl.ds(where, size), :] = joined

    @pl.when(step == last)
    def _():
        pltpu.make_async_copy(h_any, turned_h, sem.at[0]).wait()
        product = dot(turned_h[...], grads[...]).astype(bf16)
        part = product.shape[0] // 2
        mine = core[0] == 0
        low, high = product[:part], product[part:]
        send_out[0:part] = jnp.where(mine, high, low)
        keep_out[0:part] = jnp.where(mine, low, high)
        joins = [jnp.where(top, maps[i][:, :128], maps[i][:, 128:]) for i in range(2)]
        turns = [pltpu.roll(j, 64, 1) for j in joins]
        own_map = jnp.where(first, joins[0] - turns[0], turns[1] - joins[1]).astype(bf16)
        map_out[...] = own_map
        if more:
            whole = jnp.concatenate([m[...] for m in earlier] + [own_map], axis=1)
            low, high = whole[:64], whole[64:]
            send_out[part : part + 64] = jnp.where(mine, high, low)
            keep_out[part : part + 64] = jnp.where(mine, low, high)
            send_out[part + 64 :] = jnp.zeros_like(low)
            keep_out[part + 64 :] = jnp.zeros_like(low)


def back_pass(side, at, core, firsts, seconds, prefix, incoming, later, fq, fk, ones, turned_h, earlier):
    (q, k, v, turned_v, pq, turned_pq, pk, turned_pk) = firsts
    gn, gd, turned_n, turned_d = seconds
    rows = v.shape[0]
    pairs = fq.shape[0]
    width = turned_h.shape[0]
    count = rows // BLOCK
    both = pairs * side + at
    here = lambda cols, spot: pl.BlockSpec((BLOCK, cols), lambda c, core: (count - 1 - c, spot))
    turned = lambda cols, spot: pl.BlockSpec((cols, BLOCK), lambda c, core: (spot, count - 1 - c))
    weights = pl.BlockSpec((1, 128, 256), lambda c, core: (at, 0, 0))
    more = len(earlier)
    sums = (width // 2 + (128 if more else 0), 384)
    whole = lambda dims: pl.BlockSpec(dims, lambda c, core: (0,) * len(dims))
    return pl.pallas_call(
        functools.partial(back_kernel, pairs, side, at, more),
        grid_spec=pltpu.PrefetchScalarGridSpec(
            num_scalar_prefetch=1,
            grid=(count,),
            in_specs=[turned(128, at), turned(128, at), here(128, at), turned(128, at)]
            + [here(256, at), turned(256, at)] * 2
            + [here(128, both)] * 2
            + [turned(128, both)] * 2
            + [pl.BlockSpec((BLOCK // CHUNK, 2, 128, 128), lambda c, core: (count - 1 - c, at, 0, 0))]
            + [once(incoming.shape)] * 2
            + [weights] * 2
            + [once(ones.shape), anywhere]
            + [once((128, 128))] * more,
            out_specs=[here(384, 0), whole(sums), whole(sums), whole((128, 128))],
            scratch_shapes=[
                pltpu.VMEM((2, 128, 128), f32),
                pltpu.VMEM((2, 128, 128), f32),
                pltpu.VMEM((rows, 384), bf16),
                pltpu.VMEM((2, 128, 256), f32),
                pltpu.VMEM((width, rows), bf16),
                pltpu.SemaphoreType.DMA((1,)),
            ],
        ),
        out_shape=[shaped((rows, 384)), shaped(sums), shaped(sums), shaped((128, 128))],
        compiler_params=params(),
        cost_estimate=small_cost(),
        name="back_pass",
    )(core, *firsts, *seconds, prefix, incoming, later, fq, fk, ones, turned_h, *earlier)


def tokens_kernel(pairs, count, order, tokens, resid, gain, *refs):
    pieces = refs[: 1 + count]
    grads = refs[1 + count : 1 + count + 2 * pairs]
    out, gain_out, w_own, w_oth, sems = refs[1 + count + 2 * pairs :]

    @pl.when(pl.program_id(0) == 0)
    def _():
        copies = qkv_copies(pieces[:1], order, (0, 1, 2), w_own, sems, 0)
        copies += qkv_copies(pieces[1:], order, (0, 1, 2), w_oth, sems, 3)
        run_copies(copies)
        gain_out[...] = jnp.zeros_like(gain_out)

    normed, spread = norm_parts(tokens[...].astype(f32))
    total = None
    for half in range(2):
        joined = jnp.concatenate(
            [
                g[:, 128 * kind : 128 * kind + 128]
                for kind in range(3)
                for g in grads[half * pairs : half * pairs + pairs]
            ],
            axis=1,
        )
        part = dot_t(joined, (w_own, w_oth)[half][...])
        total = part if total is None else total + part
    gain_out[...] += jnp.sum(total * normed, axis=0, keepdims=True)
    back = norm_back(total, normed, spread, gain[...])
    out[...] = (resid[...].astype(f32) + back).astype(bf16)


def tokens_pass(order, tokens, resid, gain, w_own, pieces, grads, block):
    rows, width = tokens.shape
    pairs = len(grads) // 2
    cols = 3 * w_own.shape[2]
    count = len(pieces)
    return pl.pallas_call(
        functools.partial(tokens_kernel, pairs, count),
        grid=(rows // block,),
        in_specs=[scalars]
        + [by_rows(block, width)] * 2
        + [once(gain.shape)]
        + [anywhere] * (1 + count)
        + [by_rows(block, 384)] * len(grads),
        out_specs=[by_rows(block, width), pl.BlockSpec((1, width), lambda c: (0, 0))],
        out_shape=[shaped((rows, width)), shaped((1, width), f32)],
        scratch_shapes=[
            pltpu.VMEM((width, cols), bf16),
            pltpu.VMEM((width, cols), bf16),
            pltpu.SemaphoreType.DMA((3 + 3 * count,)),
        ],
        compiler_params=params(),
        cost_estimate=small_cost(),
        name="tokens_pass",
    )(order, tokens, resid, gain, w_own, *pieces, *grads)


def cross_to(value, axis, flip):
    count = lax.axis_size(axis)
    return lax.ppermute(value, axis, [(i, i ^ flip) for i in range(count)])


def swap(value, axis, bit):
    return cross_to(value, axis, 1 << bit)


def bit_of(axis, bit):
    return (lax.axis_index(axis) >> bit) & 1


def bits_of(axis):
    return lax.axis_size(axis).bit_length() - 1


def ordered(bit, mine, theirs, axis=0):
    return jnp.where(
        bit == 0,
        jnp.concatenate([mine, theirs], axis),
        jnp.concatenate([theirs, mine], axis),
    )


def add_low(*parts):
    total = parts[0].astype(f32)
    for part in parts[1:]:
        total = total + part.astype(f32)
    return total.astype(bf16)


class Flow:
    def __init__(self):
        self.ready = {}
        self.steps = {}
        self.done = {}

    def start(self, name, steps):
        self.steps[name] = steps
        self.ready[name] = next(steps)

    def slot(self, names, others):
        names = [n for n in names if n in self.steps]
        tied, others = lax.optimization_barrier(([self.ready[n] for n in names], others))
        for name, value in zip(names, tied):
            self.move(name, value)
        return others

    def move(self, name, value):
        try:
            self.ready[name] = self.steps[name].send(value)
        except StopIteration as end:
            self.done[name] = end.value
            del self.steps[name], self.ready[name]

    def finish(self, names):
        for name in names:
            while name in self.steps:
                self.move(name, self.ready[name])


def fetch_halves(weight, axis):
    count = weight.shape[axis] // 2
    part = yield lax.dynamic_slice_in_dim(weight, bit_of("ctx", 0) * count, count, axis)
    part = yield swap(part, "heads", 0)
    return [part, swap(part, "ctx", 0)]


def fetch_quarters(weight, across):
    count = weight.shape[0] // 4
    place = 2 * bit_of("ctx", 0) + bit_of(*across)
    part = yield lax.dynamic_slice_in_dim(weight, place * count, count, 0)
    part = yield swap(part, "heads", 0)
    part, second = yield part, swap(part, *across)
    return [part, second, swap(part, "ctx", 0), swap(second, "ctx", 0)]


def fetch_order():
    core = bit_of("ctx", 0)
    order = [core, 1 - core]
    for across in (bit_of("ctx", 1), bit_of("batch", 0)):
        order += [
            2 * core + across,
            2 * core + 1 - across,
            2 - 2 * core + across,
            3 - 2 * core - across,
        ]
    return jnp.stack(order).astype(jnp.int32)


def reduce_sums(send, keep, ways):
    send = yield send
    got = swap(send, "ctx", 0)
    return (yield from reduce_rest(add_low(keep[0], got[0]), add_low(keep[1], got[1]), ways))


def reduce_rest(left, oth, ways):
    left, oth = yield left, oth
    rights = [swap(oth, "heads", 0)]
    stages = [("ctx", b, 1) for b in range(1, bits_of("ctx"))]
    count = bits_of("batch")
    stages += [("batch", b, min(ways, count - b)) for b in range(0, count, ways)]
    for axis, low_bit, bits in stages:
        ways = 1 << bits
        place = (lax.axis_index(axis) >> low_bit) & (ways - 1)
        count = left.shape[0] // ways
        cut = lambda at: add_low(
            *[lax.dynamic_slice_in_dim(a, at * count, count, 0) for a in (left, *rights)]
        )
        sends = [cut(place ^ flip) for flip in range(1, ways)]
        left, sends = yield (cut(place), sends)
        rights = [cross_to(s, axis, (i + 1) << low_bit) for i, s in enumerate(sends)]
    whole = add_low(left, *rights)
    for axis, low_bit, bits in reversed(stages):
        whole = yield whole
        parts = [whole] + [cross_to(whole, axis, flip << low_bit) for flip in range(1, 1 << bits)]
        for b in range(bits):
            bit = bit_of(axis, low_bit + b)
            parts = [ordered(bit, parts[i], parts[i + 1]) for i in range(0, len(parts), 2)]
        whole = parts[0]
    whole = yield whole
    return whole, swap(whole, "ctx", 0)


def send_once(value, axis, bit):
    value = yield value
    return swap(value, axis, bit)


def reduce_gains(value):
    for axis in ("ctx", "heads", "batch"):
        for bit in range(bits_of(axis)):
            value = yield value
            value = value + swap(value, axis, bit)
    return value


def scan_runs(total, boundary, rows, backward):
    place, side = lax.axis_index("ctx"), lax.axis_index("heads")
    second = lambda spot, half: (2 * spot + half) * rows >= boundary
    end = 0 if backward else 1
    low = yield total.astype(bf16)
    got = jnp.flip(swap(low, "heads", 0).astype(f32), 0)
    mine = second(place, side)
    joins = second(place, 0) == second(place, 1)
    received = jnp.where(jnp.logical_and(side == end, joins), got, 0.0)
    near = jnp.where(side == end, total, got)
    far = jnp.where(side == end, got, total)
    low = yield (near + jnp.where(joins, far, 0.0)).astype(bf16)
    for flip in range(1, lax.axis_size("ctx")):
        got = cross_to(low, "ctx", flip).astype(f32)
        spot = place ^ flip
        ahead = spot > place if backward else spot < place
        takes = jnp.logical_and(ahead, second(spot, end) == mine)
        received = received + jnp.where(takes, got, 0.0)
    return received


def extended(maps):
    heads, size, _ = maps.shape
    both = jnp.concatenate([maps, -maps], axis=2).reshape(heads // 2, 2, size, 2 * size)
    empty = jnp.zeros_like(both[:, 0])
    return jnp.concatenate(
        [
            jnp.concatenate([both[:, 0], empty], axis=2),
            jnp.concatenate([empty, both[:, 1]], axis=2),
        ],
        axis=1,
    )


def shards(tokens, lengths, gain_one, w_qkv, f_query, f_key, w_out, gain_two, w_up, w_down, d_out):
    rows, width = tokens.shape
    heads, size, _ = f_query.shape
    pairs = heads // 2
    wide = heads * size
    units = w_up.shape[1]
    assert size == 64 and lax.axis_size("heads") == 2 and 1536 % rows == 0
    boundary = lengths[0, 0]
    place = bit_of("ctx", 0)
    order = fetch_order()
    gain_one_row = gain_one.reshape(1, width)
    gain_two_row = gain_two.reshape(1, width)

    low_rows, low_cols = half_blocks(256)
    ones = (low_rows == low_cols).astype(bf16)
    cross_rows, cross_cols = half_blocks(128)
    cross = (cross_rows != cross_cols).astype(bf16)

    flow = Flow()
    slot = flow.slot
    qkv_own = jnp.transpose(w_qkv, (1, 0, 2))
    flow.start("maps", send_once(jnp.stack([f_query, f_key]), "heads", 0))
    flow.start("qkv", fetch_halves(qkv_own, 1))
    flow.start("up", fetch_quarters(w_up, ("ctx", 1)))
    flow.start("down", fetch_quarters(jnp.concatenate([w_down, w_out], axis=0), ("batch", 0)))
    (tokens,) = slot(["maps", "qkv"], (tokens,))
    turn = lambda a: jnp.swapaxes(a, 1, 2)

    h_one, turned_h = norm_one(tokens, gain_one_row)
    maps_oth = flow.done["maps"]
    fq, fk = [extended(f_query)], [extended(f_key)]
    keys = [key_pass(h_one, [qkv_own], order, turn(fk[0]))]
    (keys[0][1], order, maps_oth, ones, cross) = slot(
        ["qkv", "up", "down"], (keys[0][1], order, maps_oth, ones, cross)
    )
    qkv_oth = flow.done["qkv"]
    fq.append(extended(maps_oth[0]))
    fk.append(extended(maps_oth[1]))
    keys.append(key_pass(h_one, qkv_oth, order, turn(fk[1])))
    flow.start("scan", scan_runs(jnp.stack([keys[0][6], keys[1][6]]), boundary, rows, False))
    (keys[1][1], order, fq[1]) = slot(["scan", "up"], (keys[1][1], order, fq[1]))
    queries = []
    for at, weights in enumerate(([qkv_own], qkv_oth)):
        queries.append(
            query_pass(
                h_one, weights, order, keys[at][4], keys[at][1], keys[at][5], turn(fq[at])
            )
        )
        if at == 0:
            (queries[0][0], order) = slot(["scan", "up", "down"], (queries[0][0], order))
    (queries[1][0], order) = slot(["down"], (queries[1][0], order))
    ups, downs, incoming = (flow.done[n] for n in ("up", "down", "scan"))
    q, phi_q, turned_pq, numer = zip(*queries)
    k, v, turned_v, phi_k, turned_pk, prefix, _ = zip(*keys)

    (
        act,
        grad_pre,
        mixed,
        grad_resid,
        gn,
        gd,
        turned_two,
        turned_a,
        turned_n,
        turned_gd,
        grad_totals,
        gain_two_part,
    ) = middle_pass(
        order,
        tokens,
        d_out,
        numer,
        phi_q,
        incoming,
        gain_two_row,
        cross,
        (w_out, w_up, w_down),
        ups,
        downs,
        256,
        512,
    )
    flow.start("later", scan_runs(grad_totals, boundary, rows, True))
    near = place.reshape(1)
    near, away = place.reshape(1), (1 - place).reshape(1)
    side_at = lax.axis_index("heads").reshape(1).astype(jnp.int32)
    (away, act) = slot(["later"], (away, act))
    send = down_pass(away, act, d_out, turned_a, grad_resid)
    flow.start("down_core", send_once(send, "ctx", 0))
    (side_at,) = slot(["later", "down_core"], (side_at,))
    up_sum = up_pass(side_at, turned_two, grad_pre)
    got, later = flow.done["down_core"], flow.done["later"]
    (near, up_sum, got, later) = slot([], (near, up_sum, got, later))
    up_sum = lax.psum_scatter(
        up_sum.reshape(-1, units), ("heads", "batch", "ctx"), scatter_dimension=0, tiled=True
    )
    keep = down_pass(near, act, d_out, turned_a, grad_resid, (got,))
    flow.start("down", reduce_rest(*keep, 1))
    (near, ones) = slot(["down"], (near, ones))

    grads, maps, sends, keeps = [[], []], [[], []], [], []
    plan = [[], [], ["down"], ["qkv0", "down"], ["qkv0", "down"], ["qkv0", "down", "qkv1"]]
    for at in range(pairs):
        for side in (1, 0):
            grad, send, keep, map_part = back_pass(
                side,
                at,
                near,
                [a[side] for a in (q, k, v, turned_v, phi_q, turned_pq, phi_k, turned_pk)],
                [gn, gd, turned_n, turned_gd],
                prefix[side],
                incoming,
                later,
                fq[side],
                fk[side],
                ones,
                turned_h,
                maps[side] if at == pairs - 1 else [],
            )
            grads[side].append(grad)
            maps[side].append(map_part)
            sends.append(send)
            keeps.append(keep)
            if side == 0 and at == pairs - 2:
                pair_up = lambda a: jnp.stack([jnp.concatenate(a[1::2]), jnp.concatenate(a[0::2])])
                flow.start("qkv0", reduce_sums(pair_up(sends), pair_up(keeps), 2))
                sends, keeps = [], []
            if side == 0 and at == pairs - 1:
                flow.start("qkv1", reduce_sums(pair_up(sends), pair_up(keeps), 2))
            (grads[side][at], near) = slot(plan[2 * at + 1 - side], (grads[side][at], near))
    order = order + 0 * near[0]
    grad_tokens, gain_one_part = tokens_pass(
        order, tokens, grad_resid, gain_one_row, qkv_own, qkv_oth, grads[0] + grads[1], 512
    )
    flow.start("gains", reduce_gains(jnp.concatenate([gain_one_part, gain_two_part], axis=0)))
    (near, grad_tokens, up_sum) = slot(
        ["qkv1", "qkv0", "down", "gains"], (near, grad_tokens, up_sum)
    )
    up_sum = lax.all_gather(up_sum, ("batch", "ctx"), axis=0, tiled=True)
    slot(["qkv1", "qkv0", "down", "gains"], ())
    slot(["qkv1", "gains"], ())
    slot(["qkv1", "qkv0", "gains"], ())
    slot(["qkv1", "down", "qkv0", "gains"], ())
    while flow.steps:
        slot(list(flow.steps), ())
    gains = flow.done["gains"]
    grad_up = up_sum.astype(f32)
    join = lambda mine, theirs: ordered(place, mine, theirs)
    mine, theirs = flow.done["down"]
    grad_down = join(mine[: units // 2], theirs[: units // 2]).astype(f32)
    grad_out = join(mine[units // 2 :], theirs[units // 2 :]).astype(f32)
    part = width // 2
    parts = []
    for name, count in (("qkv0", pairs - 1), ("qkv1", 1)):
        mine, theirs = flow.done[name]
        for at in range(count):
            run = slice(part * at, part * at + part)
            parts.append(join(mine[run], theirs[run]).reshape(width, 3, 128))
    grad_qkv = jnp.concatenate(parts, axis=2).astype(f32)
    maps_sum = join(mine[part : part + 64], theirs[part : part + 64]).astype(f32)
    maps_sum = maps_sum.reshape(2, 64, pairs, 2, 64).transpose(3, 2, 0, 1, 4)
    grad_maps = maps_sum.reshape(2, heads, size, size)
    return (
        mixed,
        grad_tokens,
        gains[0],
        grad_qkv,
        grad_maps[0],
        grad_maps[1],
        grad_out,
        gains[1],
        grad_up,
        grad_down,
    )


def solution(mesh):
    in_specs = (
        P(("batch", "ctx", "heads"), None),
        P("batch", None),
        P(),
        P(None, None, "heads"),
        P("heads", None, None),
        P("heads", None, None),
        P("heads", None),
        P(),
        P(None, "heads"),
        P("heads", None),
        P(("batch", "ctx", "heads"), None),
    )
    out_specs = (
        P(("batch", "ctx", "heads"), None),
        P(("batch", "ctx", "heads"), None),
        P(),
        P(None, None, "heads"),
        P("heads", None, None),
        P("heads", None, None),
        P("heads", None),
        P(),
        P(None, "heads"),
        P("heads", None),
    )
    return jax.shard_map(shards, mesh=mesh, in_specs=in_specs, out_specs=out_specs, check_vma=False)
```

```python
import functools

import jax
import jax.numpy as jnp
import numpy as np
from jax import lax
from jax.experimental import pallas as pl
from jax.experimental.pallas import tpu as pltpu
from jax.sharding import PartitionSpec as P

epsilon = 1e-05
f32 = jnp.float32
bf16 = jnp.bfloat16
CHUNK = 256
BLOCK = 512
VMEM_LIMIT = 60 * 1024 * 1024
GELU_A = 0.7978845608028654
GELU_B = 0.044715


def dot(left, right):
    return lax.dot_general(left, right, (((1,), (0,)), ((), ())), preferred_element_type=f32)


def dot_t(left, right):
    return lax.dot_general(left, right, (((1,), (1,)), ((), ())), preferred_element_type=f32)


def params():
    return pltpu.CompilerParams(
        dimension_semantics=("arbitrary",), vmem_limit_bytes=VMEM_LIMIT
    )


def cost(micros):
    return pl.CostEstimate(flops=0, bytes_accessed=micros * 3_600_000, transcendentals=0)


def shaped(shape, kind=bf16):
    return jax.ShapeDtypeStruct(shape, kind)


def once(shape):
    zeros = (0,) * len(shape)
    return pl.BlockSpec(shape, lambda *_: zeros, pipeline_mode=pl.Buffered(1))


def by_rows(count, cols, at=0):
    return pl.BlockSpec((count, cols), lambda c, *_: (c, at))


def by_cols(rows, count, at=0):
    return pl.BlockSpec((rows, count), lambda c, *_: (at, c))


anywhere = pl.BlockSpec(memory_space=pl.ANY)
scalars = pl.BlockSpec(memory_space=pltpu.SMEM)


def first_lanes():
    return lax.broadcasted_iota(jnp.int32, (1, 128), 1) < 64


def first_sublanes():
    return lax.broadcasted_iota(jnp.int32, (128, 1), 0) < 64


def build_maps(f, signs, turned_out, plain_out, pairs):
    top = first_sublanes()
    left = lax.broadcasted_iota(jnp.int32, (1, 256), 1) < 128
    for p in range(pairs):
        both = dot(f[2 * p : 2 * p + 2].reshape(128, 64), signs[...])
        plain = jnp.where(top == left, both, 0.0)
        plain_out[p] = plain.astype(bf16)
        turned_out[p] = plain.T.astype(bf16)


def soft_rows(logits):
    count, size = logits.shape
    groups = logits.reshape(count // 64, 64, size)
    grown = jnp.exp(groups - jnp.max(groups, axis=1, keepdims=True))
    soft = grown * (1.0 / jnp.sum(grown, axis=1, keepdims=True))
    return soft.reshape(count, size)


def norm_parts(values):
    centred = values - jnp.mean(values, axis=1, keepdims=True)
    spread = lax.rsqrt(jnp.mean(centred * centred, axis=1, keepdims=True) + epsilon)
    return centred * spread, spread


def norm_back(gradient, normed, spread, gain):
    scaled = gradient * gain
    return spread * (
        scaled
        - jnp.mean(scaled, axis=1, keepdims=True)
        - normed * jnp.mean(scaled * normed, axis=1, keepdims=True)
    )


def run_copies(copies):
    for copy in copies:
        copy.start()
    for copy in copies:
        copy.wait()


def qkv_copies(pieces, order, kinds, target, sems, first_sem):
    rows = pieces[0].shape[1]
    copies = []
    for i, piece in enumerate(pieces):
        where = 0 if len(pieces) == 1 else pl.multiple_of(order[i] * rows, 16)
        for at, kind in enumerate(kinds):
            wide = piece.shape[2]
            copies.append(
                pltpu.make_async_copy(
                    piece.at[kind],
                    target.at[pl.ds(where, rows), pl.ds(at * wide, wide)],
                    sems.at[first_sem + len(copies)],
                )
            )
    return copies


def norm_kernel(tokens, gain, h_out, turned_out):
    normed, _ = norm_parts(tokens[...].astype(f32))
    low = (normed * gain[...]).astype(bf16)
    h_out[...] = low
    turned_out[...] = low.T


def norm_one(tokens, gain):
    rows, width = tokens.shape
    return pl.pallas_call(
        norm_kernel,
        grid=(rows // BLOCK,),
        in_specs=[by_rows(BLOCK, width), once((1, width))],
        out_specs=[by_rows(BLOCK, width), by_cols(width, BLOCK)],
        out_shape=[shaped((rows, width)), shaped((width, rows))],
        compiler_params=params(),
        cost_estimate=cost(5),
        name="norm_one",
    )(tokens, gain)


def write_state(state, state_out, pairs):
    top = first_sublanes()
    sums = []
    for p in range(pairs):
        state_out[128 * p : 128 * p + 128] = jnp.where(
            top, state[2 * p], state[2 * p + 1]
        ).astype(bf16)
        sums.append(state[2 * p, 64:65, :])
        sums.append(state[2 * p + 1, 0:1, :])
    tail = state_out.shape[0] - 128 * pairs
    sums.append(jnp.zeros((tail - 2 * pairs, 128), f32))
    state_out[128 * pairs :] = jnp.concatenate(sums, axis=0).astype(bf16)


def read_state(packed, p, h_at, pairs):
    row = 128 * pairs + 2 * p + h_at
    whole = packed[128 * p : 128 * p + 128, :]
    sums = packed[row : row + 1, :]
    sel = first_sublanes() if h_at == 0 else jnp.logical_not(first_sublanes())
    return jnp.where(sel, whole, sums)


def keys_kernel(pairs, count, order, h, f, signs, earlier, *refs):
    pieces = refs[:count]
    (k_out, v_out, turned_v_out, phi_out, turned_phi_out, prefix_out, state_out) = refs[count : count + 7]
    fext, plain_out, w_kv, state, sems = refs[count + 7 :]
    step = pl.program_id(0)
    wide = 128 * pairs

    @pl.when(step == 0)
    def _():
        copies = qkv_copies(pieces, order, (1, 2), w_kv, sems, 0)
        for copy in copies:
            copy.start()
        build_maps(f, signs, fext, plain_out, pairs)
        state[...] = jnp.zeros_like(state)
        for copy in copies:
            copy.wait()

    kv_all = dot(h[...], w_kv[...]).astype(bf16)
    turned_k_all = kv_all[:, :wide].T
    turned_v_all = kv_all[:, wide:].T
    k_out[...] = turned_k_all
    v_out[...] = kv_all[:, wide:]
    turned_v_out[...] = turned_v_all
    top = first_sublanes()
    one = jnp.ones((1, 1), bf16)
    for sub in range(h.shape[0] // CHUNK):
        run = slice(CHUNK * sub, CHUNK * sub + CHUNK)
        turned_k, turned_v = turned_k_all[:, run], turned_v_all[:, run]
        prefix_out[sub] = state[...].astype(bf16)
        for p in range(pairs):
            turned_phi = soft_rows(dot(fext[p], turned_k[128 * p : 128 * p + 128])).astype(bf16)
            phi = turned_phi.T
            turned_phi_out[256 * p : 256 * p + 256, run] = turned_phi
            phi_out[run, 256 * p : 256 * p + 256] = phi
            values = turned_v[128 * p : 128 * p + 128]
            for h_at in range(2):
                sel = top if h_at == 0 else jnp.logical_not(top)
                padded = jnp.where(sel, values, one)
                state[2 * p + h_at] += dot(padded, phi[:, 128 * h_at : 128 * h_at + 128])

    @pl.when(step == pl.num_programs(0) - 1)
    def _():
        state_out[0] = earlier[...]
        write_state(state, state_out.at[1], pairs)


def key_pass(h, weights, order, f, signs, earlier):
    rows, width = h.shape
    pairs = f.shape[0] // 2
    wide = 128 * pairs
    count = rows // CHUNK
    packed = wide + 16
    return list(
        pl.pallas_call(
            functools.partial(keys_kernel, pairs, len(weights)),
            grid=(rows // BLOCK,),
            in_specs=[
                scalars,
                by_rows(BLOCK, width),
                once(f.shape),
                once(signs.shape),
                once((packed, 128)),
            ]
            + [anywhere] * len(weights),
            out_specs=[
                by_cols(wide, BLOCK),
                by_rows(BLOCK, wide),
                by_cols(wide, BLOCK),
                by_rows(BLOCK, 2 * wide),
                by_cols(2 * wide, BLOCK),
                pl.BlockSpec((BLOCK // CHUNK, 2 * pairs, 128, 128), lambda c: (c, 0, 0, 0)),
                once((2, packed, 128)),
                once((pairs, 256, 128)),
                once((pairs, 128, 256)),
            ],
            out_shape=[
                shaped((wide, rows)),
                shaped((rows, wide)),
                shaped((wide, rows)),
                shaped((rows, 2 * wide)),
                shaped((2 * wide, rows)),
                shaped((count, 2 * pairs, 128, 128)),
                shaped((2, packed, 128)),
                shaped((pairs, 256, 128)),
                shaped((pairs, 128, 256)),
            ],
            scratch_shapes=[
                pltpu.VMEM((width, 2 * wide), bf16),
                pltpu.VMEM((2 * pairs, 128, 128), f32),
                pltpu.SemaphoreType.DMA((2 * len(weights),)),
            ],
            compiler_params=params(),
            cost_estimate=cost(10),
            name="key_pass",
        )(order, h, f, signs, earlier, *weights)
    )


def query_kernel(pairs, count, order, h, turned_k_phi, v, prefix, f, signs, *refs):
    pieces = refs[:count]
    q_out, phi_out, turned_phi_out, numer_out, fext, plain_out, w_q, sems = refs[count:]

    @pl.when(pl.program_id(0) == 0)
    def _():
        copies = qkv_copies(pieces, order, (0,), w_q, sems, 0)
        for copy in copies:
            copy.start()
        build_maps(f, signs, fext, plain_out, pairs)
        for copy in copies:
            copy.wait()

    turned_q_all = dot(h[...], w_q[...]).astype(bf16).T
    q_out[...] = turned_q_all
    first = first_lanes()
    one = jnp.ones((1, 1), bf16)
    size = CHUNK
    past = lax.broadcasted_iota(jnp.int32, (size, size), 0) >= lax.broadcasted_iota(
        jnp.int32, (size, size), 1
    )
    for sub in range(h.shape[0] // CHUNK):
        run = slice(CHUNK * sub, CHUNK * sub + CHUNK)
        turned_q = turned_q_all[:, run]
        for p in range(pairs):
            turned_phi = soft_rows(dot(fext[p], turned_q[128 * p : 128 * p + 128])).astype(bf16)
            phi = turned_phi.T
            turned_phi_out[256 * p : 256 * p + 256, run] = turned_phi
            phi_out[run, 256 * p : 256 * p + 256] = phi
            v_two = v[run, 128 * p : 128 * p + 128]
            for h_at in range(2):
                at = 256 * p + 128 * h_at
                sel = first if h_at == 0 else jnp.logical_not(first)
                padded = jnp.where(sel, v_two, one)
                phi_q = phi[:, 128 * h_at : 128 * h_at + 128]
                scores = dot(phi_q, turned_k_phi[at : at + 128, run])
                scores = jnp.where(past, scores, 0.0).astype(bf16)
                numer_out[run, at : at + 128] = (
                    dot(scores, padded) + dot_t(phi_q, prefix[sub, 2 * p + h_at])
                ).astype(bf16)


def query_pass(h, weights, order, turned_k_phi, v, prefix, f, signs):
    rows, width = h.shape
    pairs = f.shape[0] // 2
    wide = 128 * pairs
    return list(
        pl.pallas_call(
            functools.partial(query_kernel, pairs, len(weights)),
            grid=(rows // BLOCK,),
            in_specs=[
                scalars,
                by_rows(BLOCK, width),
                by_cols(2 * wide, BLOCK),
                by_rows(BLOCK, wide),
                pl.BlockSpec((BLOCK // CHUNK, 2 * pairs, 128, 128), lambda c: (c, 0, 0, 0)),
                once(f.shape),
                once(signs.shape),
            ]
            + [anywhere] * len(weights),
            out_specs=[
                by_cols(wide, BLOCK),
                by_rows(BLOCK, 2 * wide),
                by_cols(2 * wide, BLOCK),
                by_rows(BLOCK, 2 * wide),
                once((pairs, 256, 128)),
                once((pairs, 128, 256)),
            ],
            out_shape=[
                shaped((wide, rows)),
                shaped((rows, 2 * wide)),
                shaped((2 * wide, rows)),
                shaped((rows, 2 * wide)),
                shaped((pairs, 256, 128)),
                shaped((pairs, 128, 256)),
            ],
            scratch_shapes=[
                pltpu.VMEM((width, wide), bf16),
                pltpu.SemaphoreType.DMA((len(weights),)),
            ],
            compiler_params=params(),
            cost_estimate=cost(15),
            name="query_pass",
        )(order, h, turned_k_phi, v, prefix, f, signs, *weights)
    )


def quarter_copies(pieces, order, target, first_row, rows, sems, first_sem):
    copies = []
    for i, piece in enumerate(pieces):
        where = pl.multiple_of(order[i] * rows, 16)
        copies.append(
            pltpu.make_async_copy(
                piece.at[pl.ds(first_row, rows)],
                target.at[pl.ds(where, rows)],
                sems.at[first_sem + i],
            )
        )
    return copies


def front_kernel(pairs, units, order, tokens, *refs):
    numer, phi = refs[:2], refs[2:4]
    incoming, gain, wo_any = refs[4:7]
    pieces = refs[7:11]
    attended_out, turned_a_out, inverse_out, resid_out, h_out, turned_h_out = refs[11:17]
    held, wo_own, wo_oth, sems = refs[17:]
    first = first_lanes()
    wide = 128 * pairs
    start = pl.program_id(0) == 0

    def weight_copies():
        return [pltpu.make_async_copy(wo_any, wo_own, sems.at[0])] + quarter_copies(
            pieces, order, wo_oth, units // 4, wide // 4, sems, 1
        )

    @pl.when(start)
    def _():
        for copy in weight_copies():
            copy.start()
        for half in range(2):
            for p in range(pairs):
                for h_at in range(2):
                    held[half, 2 * p + h_at] = read_state(
                        incoming.at[half], p, h_at, pairs
                    ).astype(bf16)

    for half in range(2):
        for p in range(pairs):
            sums = []
            for h_at in range(2):
                at = 256 * p + 128 * h_at
                sums.append(
                    numer[half][:, at : at + 128].astype(f32)
                    + dot_t(phi[half][:, at : at + 128], held[half, 2 * p + h_at])
                )
            numerator = jnp.where(first, sums[0], sums[1])
            swapped = 1.0 / jnp.where(first, sums[1], sums[0])
            attended = (numerator * pltpu.roll(swapped, 64, 1)).astype(bf16)
            at = wide * half + 128 * p
            inverse_out[:, at : at + 128] = swapped.astype(bf16)
            attended_out[:, at : at + 128] = attended
            turned_a_out[at : at + 128, :] = attended.T

    @pl.when(start)
    def _():
        for copy in weight_copies():
            copy.wait()

    resid = (
        tokens[...].astype(f32)
        + dot(attended_out[:, :wide], wo_own[...])
        + dot(attended_out[:, wide:], wo_oth[...])
    )
    resid_out[...] = resid.astype(bf16)
    normed, _ = norm_parts(resid)
    h_two = (normed * gain[...]).astype(bf16)
    h_out[...] = h_two
    turned_h_out[...] = h_two.T


def front_pass(order, tokens, numers, phis, incoming, gain, w_out, pieces, block):
    rows, width = tokens.shape
    wide = w_out.shape[0]
    pairs = wide // 128
    units = 4 * pieces[0].shape[0] - wide
    return pl.pallas_call(
        functools.partial(front_kernel, pairs, units),
        grid=(rows // block,),
        in_specs=[scalars, by_rows(block, width)]
        + [by_rows(block, 2 * wide)] * 4
        + [once(incoming.shape), once(gain.shape)]
        + [anywhere] * 5,
        out_specs=[
            by_rows(block, 2 * wide),
            by_cols(2 * wide, block),
            by_rows(block, 2 * wide),
            by_rows(block, width),
            by_rows(block, width),
            by_cols(width, block),
        ],
        out_shape=[
            shaped((rows, 2 * wide)),
            shaped((2 * wide, rows)),
            shaped((rows, 2 * wide)),
            shaped((rows, width)),
            shaped((rows, width)),
            shaped((width, rows)),
        ],
        scratch_shapes=[
            pltpu.VMEM((2, 2 * pairs, 128, 128), bf16),
            pltpu.VMEM((wide, width), bf16),
            pltpu.VMEM((wide, width), bf16),
            pltpu.SemaphoreType.DMA((5,)),
        ],
        compiler_params=params(),
        cost_estimate=cost(13),
        name="front_pass",
    )(order, tokens, *numers, *phis, incoming, gain, w_out, *pieces)


def feed_forward(pre):
    square = pre * pre
    swing = jnp.tanh(GELU_A * pre * (1.0 + GELU_B * square))
    half_up = 0.5 + 0.5 * swing
    slope = half_up + (0.5 * GELU_A) * pre * (1.0 - swing * swing) * (
        1.0 + (3.0 * GELU_B) * square
    )
    return (pre * half_up).astype(bf16), slope


def add_to(total, part):
    return part if total is None else total + part


def feed_kernel(tile, order, h_any, turned_any, d_any, *refs):
    ups, downs = refs[:4], refs[4:8]
    sums_out = (refs[8:10], refs[10:12])
    mixed_out, grad_out = refs[12:14]
    h, turned, d, up, down, mixed, grad_h, act, grad_pre, mixed_low, grad_low = refs[14:25]
    sums, sems, out_sems = refs[25:]
    step = pl.program_id(0)
    rows = h.shape[0]
    part = up.shape[2]
    quarter = part // 2
    block = 512
    blocks = rows // block

    def chunk_copies(at):
        run = pl.ds(block * at, block)
        return [
            pltpu.make_async_copy(h_any.at[run], h.at[run], sems.at[8 + 2 * at]),
            pltpu.make_async_copy(d_any.at[run], d.at[run], sems.at[9 + 2 * at]),
        ]

    def weight_copies(spot):
        copies = []
        for i in (2, 3) if spot == 0 else (0, 1):
            where = pl.multiple_of(order[i] % 2 * quarter, 128)
            copies.append(
                pltpu.make_async_copy(
                    ups[i], up.at[spot, :, pl.ds(where, quarter)], sems.at[2 * i]
                )
            )
            where = pl.multiple_of(order[4 + i] % 2 * quarter, 16)
            copies.append(
                pltpu.make_async_copy(
                    downs[i].at[pl.ds(0, quarter)],
                    down.at[spot, pl.ds(where, quarter)],
                    sems.at[2 * i + 1],
                )
            )
        return copies

    def turned_copy():
        return pltpu.make_async_copy(turned_any, turned, sems.at[8 + 2 * blocks])

    def part_copies(at):
        run = pl.ds(block * at, block)
        return [
            pltpu.make_async_copy(mixed_low.at[run], mixed_out.at[run], out_sems.at[2 * at]),
            pltpu.make_async_copy(grad_low.at[run], grad_out.at[run], out_sems.at[2 * at + 1]),
        ]

    def sum_copies(spot):
        return [
            pltpu.make_async_copy(
                sums.at[spot, i], sums_out[spot][i], out_sems.at[2 * blocks + 2 * spot + i]
            )
            for i in range(2)
        ]

    @pl.when(step == 0)
    def _():
        for copy in weight_copies(0) + chunk_copies(0):
            copy.start()
        for at in range(1, blocks):
            for copy in chunk_copies(at):
                copy.start()
        turned_copy().start()
        for copy in weight_copies(1):
            copy.start()
        for copy in weight_copies(0):
            copy.wait()

    @pl.when(step == 1)
    def _():
        for copy in weight_copies(1):
            copy.wait()

    for at in range(blocks):
        run = slice(block * at, block * at + block)

        @pl.when(step == 0)
        def _(at=at):
            for copy in chunk_copies(at):
                copy.wait()

        mixed_part = grad_part = None
        for sub in range(0, part, tile):
            up_tile = up[step, :, sub : sub + tile]
            down_tile = down[step, sub : sub + tile, :]
            low, slope = feed_forward(dot(h[run, :], up_tile))
            grad = (dot_t(d[run, :], down_tile) * slope).astype(bf16)
            act[sub : sub + tile, run] = low.T
            grad_pre[run, sub : sub + tile] = grad
            mixed_part = add_to(mixed_part, dot(low, down_tile))
            grad_part = add_to(grad_part, dot_t(grad, up_tile))

        @pl.when(step == 0)
        def _(run=run, mixed_part=mixed_part, grad_part=grad_part):
            mixed[run, :] = mixed_part
            grad_h[run, :] = grad_part

        @pl.when(step == 1)
        def _(at=at, run=run, mixed_part=mixed_part, grad_part=grad_part):
            mixed_low[run, :] = (mixed[run, :] + mixed_part).astype(bf16)
            grad_low[run, :] = (grad_h[run, :] + grad_part).astype(bf16)
            for copy in part_copies(at):
                copy.start()

    @pl.when(step == 0)
    def _():
        turned_copy().wait()

    sums[step, 1] = dot(act[...], d[...]).astype(bf16)
    sums[step, 0] = dot(turned[...], grad_pre[...]).astype(bf16)

    @pl.when(step == 0)
    def _():
        for copy in sum_copies(0):
            copy.start()

    @pl.when(step == 1)
    def _():
        for copy in sum_copies(1):
            copy.start()
        for at in range(blocks):
            for copy in part_copies(at):
                copy.wait()
        for copy in sum_copies(0) + sum_copies(1):
            copy.wait()


def feed_pass(order, h, turned_h, d_out, ups, downs, tile):
    rows, width = h.shape
    part = 2 * ups[0].shape[1]
    square = (width, part)
    blocks = rows // 512
    return pl.pallas_call(
        functools.partial(feed_kernel, tile),
        grid=(2,),
        in_specs=[scalars] + [anywhere] * 11,
        out_specs=[anywhere] * 6,
        out_shape=[shaped(square), shaped((part, width))] * 2 + [shaped((rows, width))] * 2,
        scratch_shapes=[
            pltpu.VMEM((rows, width), bf16),
            pltpu.VMEM((width, rows), bf16),
            pltpu.VMEM((rows, width), bf16),
            pltpu.VMEM((2, width, part), bf16),
            pltpu.VMEM((2, part, width), bf16),
            pltpu.VMEM((rows, width), f32),
            pltpu.VMEM((rows, width), f32),
            pltpu.VMEM((part, rows), bf16),
            pltpu.VMEM((rows, part), bf16),
            pltpu.VMEM((rows, width), bf16),
            pltpu.VMEM((rows, width), bf16),
            pltpu.VMEM((2, 2, width, part), bf16),
            pltpu.SemaphoreType.DMA((9 + 2 * blocks,)),
            pltpu.SemaphoreType.DMA((4 + 2 * blocks,)),
        ],
        compiler_params=params(),
        cost_estimate=cost(32),
        name="feed_pass",
    )(order, h, turned_h, d_out, *ups, *downs)


def middle_kernel(pairs, tile, order, resid, h, d_out, *refs):
    mixed_part, grad_part, attended, inverse = refs[:4]
    phi = refs[4:6]
    gain, cross, wo_any, up_any, down_any = refs[6:11]
    pieces = refs[11:15]
    (
        act_out,
        pre_out,
        mixed_out,
        resid_out,
        gn_out,
        gd_out,
        turned_n_out,
        turned_d_out,
        state_out,
    ) = refs[15:24]
    state, wo_own, up, down, wo_oth, sems = refs[24:]
    step = pl.program_id(0)
    top = first_sublanes()
    wide = 128 * pairs
    units = up.shape[1]

    def early_copies():
        return [
            pltpu.make_async_copy(up_any, up, sems.at[0]),
            pltpu.make_async_copy(down_any, down, sems.at[1]),
        ]

    def late_copies():
        return [pltpu.make_async_copy(wo_any, wo_own, sems.at[2])] + quarter_copies(
            pieces, order, wo_oth, units // 4, wide // 4, sems, 3
        )

    @pl.when(step == 0)
    def _():
        for copy in early_copies() + late_copies():
            copy.start()
        state[...] = jnp.zeros_like(state)
        for copy in early_copies():
            copy.wait()

    h_two = h[...]
    d_low = d_out[...]
    mixed = grad_h = None
    for at in range(0, units, tile):
        low, slope = feed_forward(dot(h_two, up[:, at : at + tile]))
        grad_pre = (dot_t(d_low, down[at : at + tile, :]) * slope).astype(bf16)
        act_out[at : at + tile, :] = low.T
        for col in range(at, at + tile, 256):
            pre_out[col // 768, :, col % 768 : col % 768 + 256] = grad_pre[
                :, col - at : col - at + 256
            ]
        mixed = add_to(mixed, dot(low, down[at : at + tile, :]))
        grad_h = add_to(grad_h, dot_t(grad_pre, up[:, at : at + tile]))
    summed = resid[...].astype(f32)
    normed, spread = norm_parts(summed)
    mixed_out[...] = (summed + mixed_part[...].astype(f32) + mixed).astype(bf16)
    grad_h = grad_part[...].astype(f32) + grad_h
    grad_resid = (d_low.astype(f32) + norm_back(grad_h, normed, spread, gain[...])).astype(bf16)
    resid_out[...] = grad_resid

    @pl.when(step == 0)
    def _():
        for copy in late_copies():
            copy.wait()

    for half in range(2):
        grad_att = dot_t(grad_resid, (wo_own, wo_oth)[half][...]).astype(bf16).astype(f32)
        for p in range(pairs):
            at = wide * half + 128 * p
            own = grad_att[:, 128 * p : 128 * p + 128]
            swapped = inverse[:, at : at + 128].astype(f32)
            grad_n = (own * pltpu.roll(swapped, 64, 1)).astype(bf16)
            exact = attended[:, at : at + 128].astype(f32)
            total = dot((own * exact).astype(bf16), cross[...])
            grad_d = ((-1.0 / 64.0) * total * swapped).astype(bf16)
            gn_out[:, at : at + 128] = grad_n
            gd_out[:, at : at + 128] = grad_d
            turned_n = grad_n.T
            turned_d = grad_d.T
            turned_n_out[at : at + 128, :] = turned_n
            turned_d_out[at : at + 128, :] = turned_d
            left = jnp.concatenate([turned_n, turned_d[0:16], turned_d[64:80]], axis=0)
            sums = dot(left, phi[half][:, 256 * p : 256 * p + 256])
            state[half, 128 * p : 128 * p + 128] += jnp.where(
                top, sums[:128, :128], sums[:128, 128:]
            )
            row = wide + 2 * p
            state[half, row : row + 1] += sums[144:145, :128]
            state[half, row + 1 : row + 2] += sums[128:129, 128:]

    @pl.when(step == pl.num_programs(0) - 1)
    def _():
        state_out[...] = state[...].astype(bf16)


def middle_pass(
    order, resid, h_two, d_out, parts, attended, inverse, phis, gain, cross, owns, pieces, packed, block, tile
):
    rows, width = resid.shape
    wide = owns[0].shape[0]
    pairs = wide // 128
    units = owns[1].shape[1]
    cols_out = [width, width, 2 * wide, 2 * wide]
    spots = units // 768
    return pl.pallas_call(
        functools.partial(middle_kernel, pairs, tile),
        grid=(rows // block,),
        in_specs=[scalars]
        + [by_rows(block, width)] * 5
        + [by_rows(block, 2 * wide)] * 4
        + [once(gain.shape), once(cross.shape)]
        + [anywhere] * 7,
        out_specs=[by_cols(units, block), pl.BlockSpec((spots, block, 768), lambda c: (0, c, 0))]
        + [by_rows(block, c) for c in cols_out]
        + [by_cols(2 * wide, block)] * 2
        + [once(packed)],
        out_shape=[shaped((units, rows)), shaped((spots, rows, 768))]
        + [shaped((rows, c)) for c in cols_out]
        + [shaped((2 * wide, rows))] * 2
        + [shaped(packed)],
        scratch_shapes=[
            pltpu.VMEM(packed, f32),
            pltpu.VMEM((wide, width), bf16),
            pltpu.VMEM((width, units), bf16),
            pltpu.VMEM((units, width), bf16),
            pltpu.VMEM((wide, width), bf16),
            pltpu.SemaphoreType.DMA((7,)),
        ],
        compiler_params=params(),
        cost_estimate=cost(35),
        name="middle_pass",
    )(order, resid, h_two, d_out, *parts, attended, inverse, *phis, gain, cross, *owns, *pieces)


def up_kernel(core, left, right, got, out):
    product = dot(left[...], right[0])
    mine = pl.program_id(0) == core[0]

    @pl.when(mine)
    def _():
        out[...] = (product + got[...].astype(f32)).astype(bf16)

    @pl.when(jnp.logical_not(mine))
    def _():
        out[...] = product.astype(bf16)


def up_pass(core, left, right, got):
    width, rows = left.shape
    count, _, part = right.shape
    return pl.pallas_call(
        up_kernel,
        grid_spec=pltpu.PrefetchScalarGridSpec(
            num_scalar_prefetch=1,
            grid=(count,),
            in_specs=[
                once((width, rows)),
                pl.BlockSpec((1, rows, part), lambda s, c: (s, 0, 0)),
                once((width, part)),
            ],
            out_specs=pl.BlockSpec((width, part), lambda s, c: (0, s)),
        ),
        out_shape=shaped((width, count * part)),
        compiler_params=params(),
        cost_estimate=cost(8),
        name="up_pass",
    )(core, left, right, got)


def down_kernel(core, left, right, own_left, oth_left, right_more, out, more_out):
    out[...] = dot(left[...], right[...]).astype(bf16)
    for side, rows in enumerate((own_left, oth_left)):
        more_out[side] = dot(rows[...], right_more[...]).astype(bf16)


def down_pass(half, left, right, left_more, right_more):
    rows, width = right.shape
    part = left.shape[0] // 2
    more = left_more.shape[0] // 4
    tile = width // 2
    cols = pl.BlockSpec((rows, tile), lambda s, half: (0, s))
    mine = lambda count, first: pl.BlockSpec((count, rows), lambda s, half: (first + half[0], 0))
    return pl.pallas_call(
        down_kernel,
        grid_spec=pltpu.PrefetchScalarGridSpec(
            num_scalar_prefetch=1,
            grid=(2,),
            in_specs=[mine(part, 0), cols, mine(more, 0), mine(more, 2), cols],
            out_specs=[
                pl.BlockSpec((part, tile), lambda s, half: (0, s)),
                pl.BlockSpec((2, more, tile), lambda s, half: (0, s, 0)),
            ],
        ),
        out_shape=[shaped((part, width)), shaped((2, 2 * more, tile))],
        compiler_params=params(),
        cost_estimate=cost(8),
        name="down_pass",
    )(half, left, right, left_more, left_more, right_more)


def back_kernel(pairs, at_pair, more, core, *refs):
    sides = (refs[:15], refs[15:30])
    incoming, later, ones, h_any = refs[30:34]
    earlier = refs[34 : 34 + more]
    grad_outs = refs[34 + more : 36 + more]
    send_out, keep_out, map_out = refs[36 + more : 39 + more]
    held, state, grads, maps, turned_h, sem = refs[39 + more :]
    step = pl.program_id(0)
    last = pl.num_programs(0) - 1
    first = first_lanes()
    top = first_sublanes()
    size = CHUNK
    inner = refs[2].shape[0] // CHUNK
    past = lax.broadcasted_iota(jnp.int32, (size, size), 0) >= lax.broadcasted_iota(
        jnp.int32, (size, size), 1
    )
    one = jnp.ones((1, 1), bf16)

    @pl.when(step == 0)
    def _():
        pltpu.make_async_copy(h_any, turned_h, sem.at[0]).start()
        maps[...] = jnp.zeros_like(maps)
        for side in range(2):
            for h_at in range(2):
                held[side, h_at] = read_state(incoming.at[side], at_pair, h_at, pairs)
                state[side, h_at] = read_state(later.at[side], at_pair, h_at, pairs)

    for sub in reversed(range(inner)):
        run = slice(CHUNK * sub, CHUNK * sub + CHUNK)
        for side in range(2):
            (q, k, v, turned_v, pq, turned_pq, pk, turned_pk) = sides[side][:8]
            (gn, gd, turned_n, turned_d, prefix, fq, fk) = sides[side][8:]
            grads_q, grads_k, grads_v = [], [], []
            for h_at in range(2):
                sel = first if h_at == 0 else jnp.logical_not(first)
                sel_top = top if h_at == 0 else jnp.logical_not(top)
                lanes = slice(128 * h_at, 128 * h_at + 128)
                padded_v = jnp.where(sel, v[run, :], one)
                padded_vt = jnp.where(sel_top, turned_v[:, run], one)
                padded_g = jnp.where(sel, gn[run, :], gd[run, :])
                padded_gt = jnp.where(sel_top, turned_n[:, run], turned_d[:, run])
                before = (prefix[sub, h_at].astype(f32) + held[side, h_at]).astype(bf16)
                after = state[side, h_at].astype(bf16)
                e = jnp.where(past, dot_t(padded_g, padded_v), 0.0).astype(bf16)
                s = jnp.where(past, dot(pq[run, lanes], turned_pk[lanes, run]), 0.0).astype(bf16)
                grads_q.append(dot(e, pk[run, lanes]) + dot(padded_g, before))
                grads_k.append(dot(turned_pq[lanes, run], e) + dot(after.T, padded_vt))
                grads_v.append(dot(padded_gt, s) + dot(after, turned_pk[lanes, run]))
                state[side, h_at] += dot(padded_gt, pq[run, lanes])

            grad_phi = jnp.concatenate(grads_q, axis=1)
            phi = pq[run, :].astype(f32)
            shared = dot((phi * grad_phi).astype(bf16), ones[...])
            grad_u = (phi * (grad_phi - shared)).astype(bf16)
            maps[side, 0] += dot(q[:, run], grad_u)
            grad_q = dot_t(grad_u, fq[0]).astype(bf16)

            grad_phi = jnp.concatenate(grads_k, axis=0).reshape(4, 64, size)
            phi = turned_pk[:, run].astype(f32).reshape(4, 64, size)
            shared = jnp.sum(phi * grad_phi, axis=1, keepdims=True)
            grad_u = (phi * (grad_phi - shared)).reshape(256, size).astype(bf16)
            maps[side, 1] += dot_t(k[:, run], grad_u)
            grad_k = dot(fk[0], grad_u).astype(bf16).T
            grad_v = jnp.where(top, grads_v[0], grads_v[1]).astype(bf16).T

            joined = jnp.concatenate([grad_q, grad_k, grad_v], axis=1)
            grad_outs[side][run, :] = joined
            where = pl.multiple_of(((last - step) * inner + sub) * size, size)
            grads[pl.ds(where, size), 384 * side : 384 * side + 384] = joined

    @pl.when(step == last)
    def _():
        pltpu.make_async_copy(h_any, turned_h, sem.at[0]).wait()
        product = dot(turned_h[...], grads[...]).astype(bf16)
        part = product.shape[0] // 2
        mine = core[0] == 0
        for side in range(2):
            cols = slice(384 * side, 384 * side + 384)
            low, high = product[:part, cols], product[part:, cols]
            send_out[side, 0:part] = jnp.where(mine, high, low)
            keep_out[side, 0:part] = jnp.where(mine, low, high)
            joins = [
                jnp.where(top, maps[side, i][:, :128], maps[side, i][:, 128:]) for i in range(2)
            ]
            turns = [pltpu.roll(j, 64, 1) for j in joins]
            own_map = jnp.where(first, joins[0] - turns[0], turns[1] - joins[1]).astype(bf16)
            map_out[side] = own_map
            if more:
                whole = jnp.concatenate([m[side] for m in earlier] + [own_map], axis=1)
                low, high = whole[:64], whole[64:]
                send_out[side, part : part + 64] = jnp.where(mine, high, low)
                keep_out[side, part : part + 64] = jnp.where(mine, low, high)
                send_out[side, part + 64 :] = jnp.zeros_like(low)
                keep_out[side, part + 64 :] = jnp.zeros_like(low)


def back_pass(at, core, sides, seconds, prefix, incoming, later, fq, fk, ones, turned_h, earlier):
    rows = sides[0][2].shape[0]
    pairs = fq[0].shape[0]
    width = turned_h.shape[0]
    count = rows // BLOCK
    here = lambda cols, spot: pl.BlockSpec((BLOCK, cols), lambda c, core: (count - 1 - c, spot))
    turned = lambda cols, spot: pl.BlockSpec((cols, BLOCK), lambda c, core: (spot, count - 1 - c))
    weights = pl.BlockSpec((1, 128, 256), lambda c, core: (at, 0, 0))
    states = pl.BlockSpec(
        (BLOCK // CHUNK, 2, 128, 128), lambda c, core: (count - 1 - c, at, 0, 0)
    )
    more = len(earlier)
    sums = (2, width // 2 + (128 if more else 0), 384)
    in_specs, args = [], []
    for side in range(2):
        both = pairs * side + at
        in_specs += [turned(128, at), turned(128, at), here(128, at), turned(128, at)]
        in_specs += [here(256, at), turned(256, at)] * 2
        in_specs += [here(128, both)] * 2 + [turned(128, both)] * 2
        in_specs += [states, weights, weights]
        args += [*sides[side], *seconds, prefix[side], fq[side], fk[side]]
    return pl.pallas_call(
        functools.partial(back_kernel, pairs, at, more),
        grid_spec=pltpu.PrefetchScalarGridSpec(
            num_scalar_prefetch=1,
            grid=(count,),
            in_specs=in_specs
            + [once(incoming.shape)] * 2
            + [once(ones.shape), anywhere]
            + [once((2, 128, 128))] * more,
            out_specs=[here(384, 0)] * 2 + [once(sums)] * 2 + [once((2, 128, 128))],
            scratch_shapes=[
                pltpu.VMEM((2, 2, 128, 128), f32),
                pltpu.VMEM((2, 2, 128, 128), f32),
                pltpu.VMEM((rows, 768), bf16),
                pltpu.VMEM((2, 2, 128, 256), f32),
                pltpu.VMEM((width, rows), bf16),
                pltpu.SemaphoreType.DMA((1,)),
            ],
        ),
        out_shape=[shaped((rows, 384))] * 2 + [shaped(sums)] * 2 + [shaped((2, 128, 128))],
        compiler_params=params(),
        cost_estimate=cost(17),
        name="back_pass",
    )(core, *args, incoming, later, ones, turned_h, *earlier)


def tokens_kernel(pairs, count, order, tokens, resid, gain, *refs):
    pieces = refs[: 1 + count]
    grads = refs[1 + count : 1 + count + 2 * pairs]
    out, w_own, w_oth, sems = refs[1 + count + 2 * pairs :]

    @pl.when(pl.program_id(0) == 0)
    def _():
        copies = qkv_copies(pieces[:1], order, (0, 1, 2), w_own, sems, 0)
        copies += qkv_copies(pieces[1:], order, (0, 1, 2), w_oth, sems, 3)
        run_copies(copies)

    normed, spread = norm_parts(tokens[...].astype(f32))
    total = None
    for half in range(2):
        joined = jnp.concatenate(
            [
                g[:, 128 * kind : 128 * kind + 128]
                for kind in range(3)
                for g in grads[half * pairs : half * pairs + pairs]
            ],
            axis=1,
        )
        part = dot_t(joined, (w_own, w_oth)[half][...])
        total = part if total is None else total + part
    back = norm_back(total, normed, spread, gain[...])
    out[...] = (resid[...].astype(f32) + back).astype(bf16)


def tokens_pass(order, tokens, resid, gain, w_own, pieces, grads, block):
    rows, width = tokens.shape
    pairs = len(grads) // 2
    cols = 3 * w_own.shape[2]
    count = len(pieces)
    return pl.pallas_call(
        functools.partial(tokens_kernel, pairs, count),
        grid=(rows // block,),
        in_specs=[scalars]
        + [by_rows(block, width)] * 2
        + [once(gain.shape)]
        + [anywhere] * (1 + count)
        + [by_rows(block, 384)] * len(grads),
        out_specs=by_rows(block, width),
        out_shape=shaped((rows, width)),
        scratch_shapes=[
            pltpu.VMEM((width, cols), bf16),
            pltpu.VMEM((width, cols), bf16),
            pltpu.SemaphoreType.DMA((3 + 3 * count,)),
        ],
        compiler_params=params(),
        cost_estimate=cost(14),
        name="tokens_pass",
    )(order, tokens, resid, gain, w_own, *pieces, *grads)


def cross_to(value, axis, flip):
    count = lax.axis_size(axis)
    return lax.ppermute(value, axis, [(i, i ^ flip) for i in range(count)])


def swap(value, axis, bit):
    return cross_to(value, axis, 1 << bit)


def bit_of(axis, bit):
    return (lax.axis_index(axis) >> bit) & 1


def bits_of(axis):
    return lax.axis_size(axis).bit_length() - 1


def ordered(bit, mine, theirs, axis=0):
    return jnp.where(
        bit == 0,
        jnp.concatenate([mine, theirs], axis),
        jnp.concatenate([theirs, mine], axis),
    )


def add_low(*parts):
    total = parts[0].astype(f32)
    for part in parts[1:]:
        total = total + part.astype(f32)
    return total.astype(bf16)


class Flow:
    def __init__(self):
        self.ready = {}
        self.steps = {}
        self.done = {}

    def start(self, name, steps):
        self.steps[name] = steps
        self.ready[name] = next(steps)

    def slot(self, names, others):
        names = [n for n in names if n in self.steps]
        tied, others = lax.optimization_barrier(([self.ready[n] for n in names], others))
        for name, value in zip(names, tied):
            self.move(name, value)
        return others

    def move(self, name, value):
        try:
            self.ready[name] = self.steps[name].send(value)
        except StopIteration as end:
            self.done[name] = end.value
            del self.steps[name], self.ready[name]

    def finish(self, names):
        for name in names:
            while name in self.steps:
                self.move(name, self.ready[name])


def fetch_halves(weight, axis):
    count = weight.shape[axis] // 2
    part = yield lax.dynamic_slice_in_dim(weight, bit_of("ctx", 0) * count, count, axis)
    part = yield swap(part, "heads", 0)
    return [part, swap(part, "ctx", 0)]


def fetch_quarters(weights, across, axis):
    place = 2 * bit_of("ctx", 0) + bit_of(*across)
    parts = []
    for weight in weights:
        count = weight.shape[axis] // 4
        parts.append(lax.dynamic_slice_in_dim(weight, place * count, count, axis))
    part = yield jnp.concatenate(parts, axis)
    part = yield swap(part, "heads", 0)
    part, second = yield part, swap(part, *across)
    return [part, second, swap(part, "ctx", 0), swap(second, "ctx", 0)]


def fetch_order():
    core = bit_of("ctx", 0)
    order = [core, 1 - core]
    for across in (bit_of("ctx", 1), bit_of("batch", 0)):
        order += [
            2 * core + across,
            2 * core + 1 - across,
            2 - 2 * core + across,
            3 - 2 * core - across,
        ]
    return jnp.stack(order).astype(jnp.int32)


def reduce_sums(send, keep, ways, spread=False):
    send = yield send
    got = swap(send, "ctx", 0)
    left, oth = add_low(keep[0], got[0]), add_low(keep[1], got[1])
    return (yield from reduce_tail(left, [swap(oth, "heads", 0)], ways, spread))


def send_over(send, keep):
    send = yield send
    total = yield add_low(keep, swap(send, "ctx", 0))
    return (yield swap(total, "heads", 0))


def send_over_late(send, keep):
    send = yield send
    got = swap(send, "ctx", 0)
    count = keep.shape[0] // 2
    first, rest = yield [add_low(keep[i], got[i]) for i in (slice(0, count), slice(count, None))]
    first, rest = yield swap(first, "heads", 0), rest
    rest = yield rest
    return jnp.concatenate([first, (yield swap(rest, "heads", 0))])


def reduce_tail(left, rights, ways, spread=False):
    stages = [("ctx", b, 1) for b in range(1, bits_of("ctx"))]
    count = bits_of("batch")
    along = [("batch", b, min(ways, count - b)) for b in range(0, count, ways)]
    if not spread:
        stages += along
    for axis, low_bit, bits in stages:
        ways = 1 << bits
        place = (lax.axis_index(axis) >> low_bit) & (ways - 1)
        count = left.shape[0] // ways
        cut = lambda at: add_low(
            *[lax.dynamic_slice_in_dim(a, at * count, count, 0) for a in (left, *rights)]
        )
        sends = [cut(place ^ flip) for flip in range(1, ways)]
        left, sends = yield (cut(place), sends)
        rights = [cross_to(s, axis, (i + 1) << low_bit) for i, s in enumerate(sends)]
    whole = add_low(left, *rights)
    for axis, low_bit, bits in along if spread else []:
        whole = yield whole
        got = [cross_to(whole, axis, flip << low_bit) for flip in range(1, 1 << bits)]
        whole = add_low(whole, *got)
    for axis, low_bit, bits in reversed(stages):
        whole = yield whole
        parts = [whole] + [cross_to(whole, axis, flip << low_bit) for flip in range(1, 1 << bits)]
        for b in range(bits):
            bit = bit_of(axis, low_bit + b)
            parts = [ordered(bit, parts[i], parts[i + 1]) for i in range(0, len(parts), 2)]
        whole = parts[0]
    whole = yield whole
    return (yield (whole, swap(whole, "ctx", 0)))


def send_once(value, axis, bit):
    value = yield value
    return swap(value, axis, bit)


def scan_runs(total, boundary, rows, backward):
    place, side = lax.axis_index("ctx"), lax.axis_index("heads")
    second = lambda spot, half: (2 * spot + half) * rows >= boundary
    end = 0 if backward else 1
    total = yield total
    got = jnp.flip(swap(total, "heads", 0).astype(f32), 0)
    total = total.astype(f32)
    mine = second(place, side)
    joins = second(place, 0) == second(place, 1)
    received = jnp.where(jnp.logical_and(side == end, joins), got, 0.0)
    near = jnp.where(side == end, total, got)
    far = jnp.where(side == end, got, total)
    low = yield (near + jnp.where(joins, far, 0.0)).astype(bf16)
    for flip in range(1, lax.axis_size("ctx")):
        got = cross_to(low, "ctx", flip).astype(f32)
        spot = place ^ flip
        ahead = spot > place if backward else spot < place
        takes = jnp.logical_and(ahead, second(spot, end) == mine)
        received = received + jnp.where(takes, got, 0.0)
    received = yield received
    return received


def shards(tokens, lengths, gain_one, w_qkv, f_query, f_key, w_out, gain_two, w_up, w_down, d_out):
    rows, width = tokens.shape
    heads, size, _ = f_query.shape
    pairs = heads // 2
    wide = heads * size
    units = w_up.shape[1]
    assert size == 64 and lax.axis_size("heads") == 2 and 1536 % rows == 0
    boundary = lengths[0, 0]
    place = bit_of("ctx", 0)
    order = fetch_order()
    gain_one_row = gain_one.reshape(1, width)
    gain_two_row = gain_two.reshape(1, width)

    spots = np.arange(256) // 64
    ones = jnp.asarray(spots[:, None] == spots[None, :], bf16)
    cross = jnp.asarray(spots[:128, None] != spots[None, :128], bf16)
    signs = jnp.asarray(np.kron(np.array([[1, -1, 1, -1]]), np.eye(64)), bf16)

    flow = Flow()
    slot = flow.slot
    qkv_own = jnp.transpose(w_qkv, (1, 0, 2))
    flow.start("maps", send_once(jnp.stack([f_query, f_key]), "heads", 0))
    flow.start("qkv", fetch_halves(qkv_own, 1))
    flow.start("up", fetch_quarters([w_up], ("ctx", 1), 1))
    flow.start("down", fetch_quarters([w_down, w_out], ("batch", 0), 0))
    (tokens,) = slot(["maps", "qkv"], (tokens,))

    h_one, turned_h = norm_one(tokens, gain_one_row)
    maps_oth = flow.done["maps"]
    empty = jnp.zeros((wide + 16, 128), bf16)
    keys = [key_pass(h_one, [qkv_own], order, f_key, signs, empty)]
    (keys[0][6], order, maps_oth) = slot(["qkv", "up", "down"], (keys[0][6], order, maps_oth))
    qkv_oth = flow.done["qkv"]
    keys.append(key_pass(h_one, qkv_oth, order, maps_oth[1], signs, keys[0][6][1]))
    flow.start("scan", scan_runs(keys[1][6], boundary, rows, False))
    (keys[1][1], order) = slot(["scan", "up"], (keys[1][1], order))
    queries = []
    for at, weights in enumerate(([qkv_own], qkv_oth)):
        queries.append(
            query_pass(
                h_one,
                weights,
                order,
                keys[at][4],
                keys[at][1],
                keys[at][5],
                (f_query, maps_oth[0])[at],
                signs,
            )
        )
        if at == 0:
            (queries[0][0], order) = slot(["scan", "up", "down"], (queries[0][0], order))
    (queries[1][0], order) = slot(["scan", "down"], (queries[1][0], order))
    ups, downs, incoming = (flow.done[n] for n in ("up", "down", "scan"))
    q, phi_q, turned_pq, numer, _, fq = zip(*queries)
    k, v, turned_v, phi_k, turned_pk, prefix, _, _, fk = zip(*keys)

    feed_order = order[2:]
    out_order = order[6:]
    attended, turned_a, inverse, resid, h_two, turned_two = front_pass(
        out_order, tokens, numer, phi_q, incoming, gain_two_row, w_out, downs, 512
    )
    send_up, send_down, keep_up, keep_down, *parts = feed_pass(
        feed_order, h_two, turned_two, d_out, ups, downs, 256
    )
    flow.start("oth_up", send_over(send_up, keep_up))
    flow.start("oth_down", send_over_late(send_down, keep_down))
    slot(["oth_up", "oth_down"], ())
    (out_order,) = slot(["oth_up", "oth_down"], (out_order,))
    (
        act,
        grad_pre,
        mixed,
        grad_resid,
        gn,
        gd,
        turned_n,
        turned_gd,
        grad_totals,
    ) = middle_pass(
        out_order,
        resid,
        h_two,
        d_out,
        parts,
        attended,
        inverse,
        phi_q,
        gain_two_row,
        cross,
        (w_out, w_up, w_down),
        downs,
        incoming.shape,
        256,
        512,
    )
    flow.start("later", scan_runs(grad_totals, boundary, rows, True))
    near, away = place.reshape(1), (1 - place).reshape(1)
    (near, grad_pre) = slot(["later", "oth_up", "oth_down"], (near, grad_pre))
    up_sum = up_pass(near, turned_two, grad_pre, flow.done["oth_up"])
    (away, act, up_sum) = slot(["later", "oth_down"], (away, act, up_sum))
    everyone = ("batch", "ctx")
    up_sum = lax.psum_scatter(up_sum, everyone, scatter_dimension=0, tiled=True)
    send, out_send = down_pass(away, act, d_out, turned_a, grad_resid)
    flow.start("own_down", send_once(send, "ctx", 0))
    (near, out_send) = slot(["later", "own_down", "oth_down"], (near, out_send))
    keep_down, out_keep = down_pass(near, act, d_out, turned_a, grad_resid)
    got, right = flow.done["own_down"], flow.done["oth_down"]
    flow.start("down_sum", reduce_tail(keep_down, [got, right], 2))
    (near, out_keep) = slot(["down_sum"], (near, out_keep))
    later = flow.done["later"]

    grads, maps, sends, keeps = [[], []], [], [], []
    feeds = ["down_sum"]
    plan = [feeds, ["qkv0"] + feeds, ["qkv1", "qkv0"] + feeds]
    names = (q, k, v, turned_v, phi_q, turned_pq, phi_k, turned_pk)
    for at in range(pairs):
        own, oth, send, keep, map_part = back_pass(
            at,
            near,
            [[a[side] for a in names] for side in range(2)],
            [gn, gd, turned_n, turned_gd],
            prefix,
            incoming,
            later,
            fq,
            fk,
            ones,
            turned_h,
            maps if at == pairs - 1 else [],
        )
        grads[0].append(own)
        grads[1].append(oth)
        maps.append(map_part)
        sends.append(send)
        keeps.append(keep)
        if at == pairs - 2:
            flow.start(
                "qkv0",
                reduce_sums(
                    jnp.concatenate(sends + [out_send], axis=1),
                    jnp.concatenate(keeps + [out_keep], axis=1),
                    2,
                ),
            )
        if at == pairs - 1:
            flow.start("qkv1", reduce_sums(send, keep, 2))
        (grads[0][at], near) = slot(plan[at], (own, near))
        if at == pairs - 1:
            (up_sum,) = slot([], (up_sum,))
            up_sum = lax.all_gather(up_sum, everyone, axis=0, tiled=True)
    order = order + 0 * near[0]
    grad_tokens = tokens_pass(
        order, tokens, grad_resid, gain_one_row, qkv_own, qkv_oth, grads[0] + grads[1], 512
    )
    tail = ["qkv1", "qkv0"]
    (near, grad_tokens) = slot(tail + feeds, (near, grad_tokens))
    (near,) = slot(tail + feeds, (near,))
    flow.finish(feeds)
    grad_down = ordered(place, *flow.done["down_sum"]).astype(f32)
    (grad_down,) = slot(tail, (grad_down,))
    (up_sum,) = slot(tail, (up_sum,))
    grad_up = up_sum.astype(f32)
    gain_two_part = jnp.sum(grad_up * w_up.astype(f32), axis=1)
    (grad_up, gain_two_part) = slot(tail, (grad_up, gain_two_part))
    flow.finish(list(flow.steps))
    part = width // 2
    (mine, theirs), (mine_last, theirs_last) = flow.done["qkv0"], flow.done["qkv1"]
    join = lambda mine, theirs: ordered(place, mine, theirs)
    beside = lambda a: jnp.concatenate([a[: wide // 2], a[wide // 2 :]], axis=1)
    more = part * (pairs - 1)
    grad_out = join(beside(mine[more:]), beside(theirs[more:])).astype(f32)
    parts = [
        join(mine[part * at : part * at + part], theirs[part * at : part * at + part])
        for at in range(pairs - 1)
    ]
    parts.append(join(mine_last[:part], theirs_last[:part]))
    grad_qkv = jnp.stack(
        [
            jnp.concatenate([p[:, 128 * kind : 128 * kind + 128] for p in parts], axis=1)
            for kind in range(3)
        ]
    )
    grad_qkv = grad_qkv.astype(f32)
    gain_one_part = jnp.sum(grad_qkv * qkv_own.astype(f32), axis=(0, 2))
    gains = jnp.stack([gain_one_part, gain_two_part])
    gains = (gains + swap(gains, "heads", 0)) / jnp.stack([gain_one, gain_two])
    grad_qkv = jnp.transpose(grad_qkv, (1, 0, 2))
    maps_sum = join(mine_last[part : part + 64], theirs_last[part : part + 64]).astype(f32)
    maps_sum = maps_sum.reshape(2, 64, pairs, 2, 64).transpose(3, 2, 0, 1, 4)
    grad_maps = maps_sum.reshape(2, heads, size, size)
    return (
        mixed,
        grad_tokens,
        gains[0],
        grad_qkv,
        grad_maps[0],
        grad_maps[1],
        grad_out,
        gains[1],
        grad_up,
        grad_down,
    )


def solution(mesh):
    in_specs = (
        P(("batch", "ctx", "heads"), None),
        P("batch", None),
        P(),
        P(None, None, "heads"),
        P("heads", None, None),
        P("heads", None, None),
        P("heads", None),
        P(),
        P(None, "heads"),
        P("heads", None),
        P(("batch", "ctx", "heads"), None),
    )
    out_specs = (
        P(("batch", "ctx", "heads"), None),
        P(("batch", "ctx", "heads"), None),
        P(),
        P(None, None, "heads"),
        P("heads", None, None),
        P("heads", None, None),
        P("heads", None),
        P(),
        P(None, "heads"),
        P("heads", None),
    )
    return jax.shard_map(shards, mesh=mesh, in_specs=in_specs, out_specs=out_specs, check_vma=False)
```

```python
import functools

import jax
import jax.numpy as jnp
import numpy as np
from jax import lax
from jax.experimental import pallas as pl
from jax.experimental.pallas import tpu as pltpu
from jax.sharding import PartitionSpec as P

epsilon = 1e-05
f32 = jnp.float32
bf16 = jnp.bfloat16
CHUNK = 256
BLOCK = 512
VMEM_LIMIT = 60 * 1024 * 1024
GELU_A = 0.7978845608028654
GELU_B = 0.044715


def dot(left, right):
    return lax.dot_general(left, right, (((1,), (0,)), ((), ())), preferred_element_type=f32)


def dot_t(left, right):
    return lax.dot_general(left, right, (((1,), (1,)), ((), ())), preferred_element_type=f32)


def params():
    return pltpu.CompilerParams(
        dimension_semantics=("arbitrary",), vmem_limit_bytes=VMEM_LIMIT
    )


def cost(micros):
    return pl.CostEstimate(flops=0, bytes_accessed=micros * 3_600_000, transcendentals=0)


def shaped(shape, kind=bf16):
    return jax.ShapeDtypeStruct(shape, kind)


def once(shape):
    zeros = (0,) * len(shape)
    return pl.BlockSpec(shape, lambda *_: zeros, pipeline_mode=pl.Buffered(1))


def by_rows(count, cols, at=0):
    return pl.BlockSpec((count, cols), lambda c, *_: (c, at))


def by_cols(rows, count, at=0):
    return pl.BlockSpec((rows, count), lambda c, *_: (at, c))


anywhere = pl.BlockSpec(memory_space=pl.ANY)
scalars = pl.BlockSpec(memory_space=pltpu.SMEM)


def first_lanes():
    return lax.broadcasted_iota(jnp.int32, (1, 128), 1) < 64


def first_sublanes():
    return lax.broadcasted_iota(jnp.int32, (128, 1), 0) < 64


def build_maps(f, signs, turned_out, plain_out, pairs):
    top = first_sublanes()
    left = lax.broadcasted_iota(jnp.int32, (1, 256), 1) < 128
    for p in range(pairs):
        both = dot(f[2 * p : 2 * p + 2].reshape(128, 64), signs[...])
        plain = jnp.where(top == left, both, 0.0)
        plain_out[p] = plain.astype(bf16)
        turned_out[p] = plain.T.astype(bf16)


def soft_rows(logits):
    count, size = logits.shape
    groups = logits.reshape(count // 64, 64, size)
    grown = jnp.exp(groups - jnp.max(groups, axis=1, keepdims=True))
    soft = grown * (1.0 / jnp.sum(grown, axis=1, keepdims=True))
    return soft.reshape(count, size)


def norm_parts(values):
    centred = values - jnp.mean(values, axis=1, keepdims=True)
    spread = lax.rsqrt(jnp.mean(centred * centred, axis=1, keepdims=True) + epsilon)
    return centred * spread, spread


def norm_back(gradient, normed, spread, gain):
    scaled = gradient * gain
    return spread * (
        scaled
        - jnp.mean(scaled, axis=1, keepdims=True)
        - normed * jnp.mean(scaled * normed, axis=1, keepdims=True)
    )


def run_copies(copies):
    for copy in copies:
        copy.start()
    for copy in copies:
        copy.wait()


def qkv_copies(pieces, order, kinds, target, sems, first_sem):
    rows = pieces[0].shape[1]
    copies = []
    for i, piece in enumerate(pieces):
        where = 0 if len(pieces) == 1 else pl.multiple_of(order[i] * rows, 16)
        for at, kind in enumerate(kinds):
            wide = piece.shape[2]
            copies.append(
                pltpu.make_async_copy(
                    piece.at[kind],
                    target.at[pl.ds(where, rows), pl.ds(at * wide, wide)],
                    sems.at[first_sem + len(copies)],
                )
            )
    return copies


def norm_kernel(tokens, gain, h_out, turned_out):
    normed, _ = norm_parts(tokens[...].astype(f32))
    low = (normed * gain[...]).astype(bf16)
    h_out[...] = low
    turned_out[...] = low.T


def norm_one(tokens, gain):
    rows, width = tokens.shape
    return pl.pallas_call(
        norm_kernel,
        grid=(rows // BLOCK,),
        in_specs=[by_rows(BLOCK, width), once((1, width))],
        out_specs=[by_rows(BLOCK, width), by_cols(width, BLOCK)],
        out_shape=[shaped((rows, width)), shaped((width, rows))],
        compiler_params=params(),
        cost_estimate=cost(5),
        name="norm_one",
    )(tokens, gain)


def write_state(state, state_out, pairs):
    top = first_sublanes()
    sums = []
    for p in range(pairs):
        state_out[128 * p : 128 * p + 128] = jnp.where(
            top, state[2 * p], state[2 * p + 1]
        ).astype(bf16)
        sums.append(state[2 * p, 64:65, :])
        sums.append(state[2 * p + 1, 0:1, :])
    tail = state_out.shape[0] - 128 * pairs
    sums.append(jnp.zeros((tail - 2 * pairs, 128), f32))
    state_out[128 * pairs :] = jnp.concatenate(sums, axis=0).astype(bf16)


def read_state(packed, p, h_at, pairs):
    row = 128 * pairs + 2 * p + h_at
    whole = packed[128 * p : 128 * p + 128, :]
    sums = packed[row : row + 1, :]
    sel = first_sublanes() if h_at == 0 else jnp.logical_not(first_sublanes())
    return jnp.where(sel, whole, sums)


def keys_kernel(pairs, count, order, h, f, signs, earlier, *refs):
    pieces = refs[:count]
    (k_out, v_out, turned_v_out, phi_out, turned_phi_out, prefix_out, state_out) = refs[count : count + 7]
    fext, plain_out, w_kv, state, sems = refs[count + 7 :]
    step = pl.program_id(0)
    wide = 128 * pairs

    @pl.when(step == 0)
    def _():
        copies = qkv_copies(pieces, order, (1, 2), w_kv, sems, 0)
        for copy in copies:
            copy.start()
        build_maps(f, signs, fext, plain_out, pairs)
        state[...] = jnp.zeros_like(state)
        for copy in copies:
            copy.wait()

    kv_all = dot(h[...], w_kv[...]).astype(bf16)
    turned_k_all = kv_all[:, :wide].T
    turned_v_all = kv_all[:, wide:].T
    k_out[...] = turned_k_all
    v_out[...] = kv_all[:, wide:]
    turned_v_out[...] = turned_v_all
    top = first_sublanes()
    one = jnp.ones((1, 1), bf16)
    for sub in range(h.shape[0] // CHUNK):
        run = slice(CHUNK * sub, CHUNK * sub + CHUNK)
        turned_k, turned_v = turned_k_all[:, run], turned_v_all[:, run]
        prefix_out[sub] = state[...].astype(bf16)
        for p in range(pairs):
            turned_phi = soft_rows(dot(fext[p], turned_k[128 * p : 128 * p + 128])).astype(bf16)
            phi = turned_phi.T
            turned_phi_out[256 * p : 256 * p + 256, run] = turned_phi
            phi_out[run, 256 * p : 256 * p + 256] = phi
            values = turned_v[128 * p : 128 * p + 128]
            for h_at in range(2):
                sel = top if h_at == 0 else jnp.logical_not(top)
                padded = jnp.where(sel, values, one)
                state[2 * p + h_at] += dot(padded, phi[:, 128 * h_at : 128 * h_at + 128])

    @pl.when(step == pl.num_programs(0) - 1)
    def _():
        state_out[0] = earlier[...]
        write_state(state, state_out.at[1], pairs)


def key_pass(h, weights, order, f, signs, earlier):
    rows, width = h.shape
    pairs = f.shape[0] // 2
    wide = 128 * pairs
    count = rows // CHUNK
    packed = wide + 16
    return list(
        pl.pallas_call(
            functools.partial(keys_kernel, pairs, len(weights)),
            grid=(rows // BLOCK,),
            in_specs=[
                scalars,
                by_rows(BLOCK, width),
                once(f.shape),
                once(signs.shape),
                once((packed, 128)),
            ]
            + [anywhere] * len(weights),
            out_specs=[
                by_cols(wide, BLOCK),
                by_rows(BLOCK, wide),
                by_cols(wide, BLOCK),
                by_rows(BLOCK, 2 * wide),
                by_cols(2 * wide, BLOCK),
                pl.BlockSpec((BLOCK // CHUNK, 2 * pairs, 128, 128), lambda c: (c, 0, 0, 0)),
                once((2, packed, 128)),
                once((pairs, 256, 128)),
                once((pairs, 128, 256)),
            ],
            out_shape=[
                shaped((wide, rows)),
                shaped((rows, wide)),
                shaped((wide, rows)),
                shaped((rows, 2 * wide)),
                shaped((2 * wide, rows)),
                shaped((count, 2 * pairs, 128, 128)),
                shaped((2, packed, 128)),
                shaped((pairs, 256, 128)),
                shaped((pairs, 128, 256)),
            ],
            scratch_shapes=[
                pltpu.VMEM((width, 2 * wide), bf16),
                pltpu.VMEM((2 * pairs, 128, 128), f32),
                pltpu.SemaphoreType.DMA((2 * len(weights),)),
            ],
            compiler_params=params(),
            cost_estimate=cost(10),
            name="key_pass",
        )(order, h, f, signs, earlier, *weights)
    )


def query_kernel(pairs, count, order, h, turned_k_phi, v, prefix, f, signs, *refs):
    pieces = refs[:count]
    q_out, phi_out, turned_phi_out, numer_out, fext, plain_out, w_q, sems = refs[count:]

    @pl.when(pl.program_id(0) == 0)
    def _():
        copies = qkv_copies(pieces, order, (0,), w_q, sems, 0)
        for copy in copies:
            copy.start()
        build_maps(f, signs, fext, plain_out, pairs)
        for copy in copies:
            copy.wait()

    turned_q_all = dot(h[...], w_q[...]).astype(bf16).T
    q_out[...] = turned_q_all
    first = first_lanes()
    one = jnp.ones((1, 1), bf16)
    size = CHUNK
    past = lax.broadcasted_iota(jnp.int32, (size, size), 0) >= lax.broadcasted_iota(
        jnp.int32, (size, size), 1
    )
    for sub in range(h.shape[0] // CHUNK):
        run = slice(CHUNK * sub, CHUNK * sub + CHUNK)
        turned_q = turned_q_all[:, run]
        for p in range(pairs):
            turned_phi = soft_rows(dot(fext[p], turned_q[128 * p : 128 * p + 128])).astype(bf16)
            phi = turned_phi.T
            turned_phi_out[256 * p : 256 * p + 256, run] = turned_phi
            phi_out[run, 256 * p : 256 * p + 256] = phi
            v_two = v[run, 128 * p : 128 * p + 128]
            for h_at in range(2):
                at = 256 * p + 128 * h_at
                sel = first if h_at == 0 else jnp.logical_not(first)
                padded = jnp.where(sel, v_two, one)
                phi_q = phi[:, 128 * h_at : 128 * h_at + 128]
                scores = dot(phi_q, turned_k_phi[at : at + 128, run])
                scores = jnp.where(past, scores, 0.0).astype(bf16)
                numer_out[run, at : at + 128] = (
                    dot(scores, padded) + dot_t(phi_q, prefix[sub, 2 * p + h_at])
                ).astype(bf16)


def query_pass(h, weights, order, turned_k_phi, v, prefix, f, signs):
    rows, width = h.shape
    pairs = f.shape[0] // 2
    wide = 128 * pairs
    return list(
        pl.pallas_call(
            functools.partial(query_kernel, pairs, len(weights)),
            grid=(rows // BLOCK,),
            in_specs=[
                scalars,
                by_rows(BLOCK, width),
                by_cols(2 * wide, BLOCK),
                by_rows(BLOCK, wide),
                pl.BlockSpec((BLOCK // CHUNK, 2 * pairs, 128, 128), lambda c: (c, 0, 0, 0)),
                once(f.shape),
                once(signs.shape),
            ]
            + [anywhere] * len(weights),
            out_specs=[
                by_cols(wide, BLOCK),
                by_rows(BLOCK, 2 * wide),
                by_cols(2 * wide, BLOCK),
                by_rows(BLOCK, 2 * wide),
                once((pairs, 256, 128)),
                once((pairs, 128, 256)),
            ],
            out_shape=[
                shaped((wide, rows)),
                shaped((rows, 2 * wide)),
                shaped((2 * wide, rows)),
                shaped((rows, 2 * wide)),
                shaped((pairs, 256, 128)),
                shaped((pairs, 128, 256)),
            ],
            scratch_shapes=[
                pltpu.VMEM((width, wide), bf16),
                pltpu.SemaphoreType.DMA((len(weights),)),
            ],
            compiler_params=params(),
            cost_estimate=cost(15),
            name="query_pass",
        )(order, h, turned_k_phi, v, prefix, f, signs, *weights)
    )


def quarter_copies(pieces, order, target, first_row, rows, sems, first_sem):
    copies = []
    for i, piece in enumerate(pieces):
        where = pl.multiple_of(order[i] * rows, 16)
        copies.append(
            pltpu.make_async_copy(
                piece.at[pl.ds(first_row, rows)],
                target.at[pl.ds(where, rows)],
                sems.at[first_sem + i],
            )
        )
    return copies


def front_kernel(pairs, units, order, tokens, *refs):
    numer, phi = refs[:2], refs[2:4]
    incoming, gain, wo_any = refs[4:7]
    pieces = refs[7:11]
    attended_out, turned_a_out, inverse_out, resid_out, h_out, turned_h_out = refs[11:17]
    held, wo_own, wo_oth, sems = refs[17:]
    first = first_lanes()
    wide = 128 * pairs
    start = pl.program_id(0) == 0

    def weight_copies():
        return [pltpu.make_async_copy(wo_any, wo_own, sems.at[0])] + quarter_copies(
            pieces, order, wo_oth, units // 4, wide // 4, sems, 1
        )

    @pl.when(start)
    def _():
        for copy in weight_copies():
            copy.start()
        for half in range(2):
            for p in range(pairs):
                for h_at in range(2):
                    held[half, 2 * p + h_at] = read_state(
                        incoming.at[half], p, h_at, pairs
                    ).astype(bf16)

    for half in range(2):
        for p in range(pairs):
            sums = []
            for h_at in range(2):
                at = 256 * p + 128 * h_at
                sums.append(
                    numer[half][:, at : at + 128].astype(f32)
                    + dot_t(phi[half][:, at : at + 128], held[half, 2 * p + h_at])
                )
            numerator = jnp.where(first, sums[0], sums[1])
            swapped = 1.0 / jnp.where(first, sums[1], sums[0])
            inv = pltpu.roll(swapped, 64, 1)
            attended = (numerator * inv).astype(bf16)
            at = wide * half + 128 * p
            inverse_out[:, at : at + 128] = inv.astype(bf16)
            attended_out[:, at : at + 128] = attended
            turned_a_out[at : at + 128, :] = attended.T

    @pl.when(start)
    def _():
        for copy in weight_copies():
            copy.wait()

    resid = (
        tokens[...].astype(f32)
        + dot(attended_out[:, :wide], wo_own[...])
        + dot(attended_out[:, wide:], wo_oth[...])
    )
    resid_out[...] = resid.astype(bf16)
    normed, _ = norm_parts(resid)
    h_two = (normed * gain[...]).astype(bf16)
    h_out[...] = h_two
    turned_h_out[...] = h_two.T


def front_pass(order, tokens, numers, phis, incoming, gain, w_out, pieces, block):
    rows, width = tokens.shape
    wide = w_out.shape[0]
    pairs = wide // 128
    units = 4 * pieces[0].shape[0] - wide
    return pl.pallas_call(
        functools.partial(front_kernel, pairs, units),
        grid=(rows // block,),
        in_specs=[scalars, by_rows(block, width)]
        + [by_rows(block, 2 * wide)] * 4
        + [once(incoming.shape), once(gain.shape)]
        + [anywhere] * 5,
        out_specs=[
            by_rows(block, 2 * wide),
            by_cols(2 * wide, block),
            by_rows(block, 2 * wide),
            by_rows(block, width),
            by_rows(block, width),
            by_cols(width, block),
        ],
        out_shape=[
            shaped((rows, 2 * wide)),
            shaped((2 * wide, rows)),
            shaped((rows, 2 * wide)),
            shaped((rows, width)),
            shaped((rows, width)),
            shaped((width, rows)),
        ],
        scratch_shapes=[
            pltpu.VMEM((2, 2 * pairs, 128, 128), bf16),
            pltpu.VMEM((wide, width), bf16),
            pltpu.VMEM((wide, width), bf16),
            pltpu.SemaphoreType.DMA((5,)),
        ],
        compiler_params=params(),
        cost_estimate=cost(13),
        name="front_pass",
    )(order, tokens, *numers, *phis, incoming, gain, w_out, *pieces)


def feed_forward(pre):
    square = pre * pre
    swing = jnp.tanh(GELU_A * pre * (1.0 + GELU_B * square))
    half_up = 0.5 + 0.5 * swing
    slope = half_up + (0.5 * GELU_A) * pre * (1.0 - swing * swing) * (
        1.0 + (3.0 * GELU_B) * square
    )
    return (pre * half_up).astype(bf16), slope


def add_to(total, part):
    return part if total is None else total + part


def feed_kernel(tile, order, h_any, turned_any, d_any, *refs):
    ups, downs = refs[:4], refs[4:8]
    sums_out = (refs[8:10], refs[10:12])
    mixed_out, grad_out = refs[12:14]
    h, turned, d, up, down, mixed, grad_h, act, grad_pre, mixed_low, grad_low = refs[14:25]
    sums, sems, out_sems = refs[25:]
    step = pl.program_id(0)
    rows = h.shape[0]
    part = up.shape[2]
    quarter = part // 2
    block = 512
    blocks = rows // block

    def chunk_copies(at):
        run = pl.ds(block * at, block)
        return [
            pltpu.make_async_copy(h_any.at[run], h.at[run], sems.at[8 + 2 * at]),
            pltpu.make_async_copy(d_any.at[run], d.at[run], sems.at[9 + 2 * at]),
        ]

    def weight_copies(spot):
        copies = []
        for i in (2, 3) if spot == 0 else (0, 1):
            where = pl.multiple_of(order[i] % 2 * quarter, 128)
            copies.append(
                pltpu.make_async_copy(
                    ups[i], up.at[spot, :, pl.ds(where, quarter)], sems.at[2 * i]
                )
            )
            where = pl.multiple_of(order[4 + i] % 2 * quarter, 16)
            copies.append(
                pltpu.make_async_copy(
                    downs[i].at[pl.ds(0, quarter)],
                    down.at[spot, pl.ds(where, quarter)],
                    sems.at[2 * i + 1],
                )
            )
        return copies

    def turned_copy():
        return pltpu.make_async_copy(turned_any, turned, sems.at[8 + 2 * blocks])

    def part_copies(at):
        run = pl.ds(block * at, block)
        return [
            pltpu.make_async_copy(mixed_low.at[run], mixed_out.at[run], out_sems.at[2 * at]),
            pltpu.make_async_copy(grad_low.at[run], grad_out.at[run], out_sems.at[2 * at + 1]),
        ]

    def sum_copies(spot):
        return [
            pltpu.make_async_copy(
                sums.at[spot, i], sums_out[spot][i], out_sems.at[2 * blocks + 2 * spot + i]
            )
            for i in range(2)
        ]

    @pl.when(step == 0)
    def _():
        for copy in weight_copies(0) + chunk_copies(0):
            copy.start()
        for at in range(1, blocks):
            for copy in chunk_copies(at):
                copy.start()
        turned_copy().start()
        for copy in weight_copies(1):
            copy.start()
        for copy in weight_copies(0):
            copy.wait()

    @pl.when(step == 1)
    def _():
        for copy in weight_copies(1):
            copy.wait()

    for at in range(blocks):
        run = slice(block * at, block * at + block)

        @pl.when(step == 0)
        def _(at=at):
            for copy in chunk_copies(at):
                copy.wait()

        mixed_part = grad_part = None
        for sub in range(0, part, tile):
            up_tile = up[step, :, sub : sub + tile]
            down_tile = down[step, sub : sub + tile, :]
            low, slope = feed_forward(dot(h[run, :], up_tile))
            grad = (dot_t(d[run, :], down_tile) * slope).astype(bf16)
            act[sub : sub + tile, run] = low.T
            grad_pre[run, sub : sub + tile] = grad
            mixed_part = add_to(mixed_part, dot(low, down_tile))
            grad_part = add_to(grad_part, dot_t(grad, up_tile))

        @pl.when(step == 0)
        def _(run=run, mixed_part=mixed_part, grad_part=grad_part):
            mixed[run, :] = mixed_part
            grad_h[run, :] = grad_part

        @pl.when(step == 1)
        def _(at=at, run=run, mixed_part=mixed_part, grad_part=grad_part):
            mixed_low[run, :] = (mixed[run, :] + mixed_part).astype(bf16)
            grad_low[run, :] = (grad_h[run, :] + grad_part).astype(bf16)
            for copy in part_copies(at):
                copy.start()

    @pl.when(step == 0)
    def _():
        turned_copy().wait()

    sums[step, 1] = dot(act[...], d[...]).astype(bf16)
    sums[step, 0] = dot(turned[...], grad_pre[...]).astype(bf16)

    @pl.when(step == 0)
    def _():
        for copy in sum_copies(0):
            copy.start()

    @pl.when(step == 1)
    def _():
        for copy in sum_copies(1):
            copy.start()
        for at in range(blocks):
            for copy in part_copies(at):
                copy.wait()
        for copy in sum_copies(0) + sum_copies(1):
            copy.wait()


def feed_pass(order, h, turned_h, d_out, ups, downs, tile):
    rows, width = h.shape
    part = 2 * ups[0].shape[1]
    square = (width, part)
    blocks = rows // 512
    return pl.pallas_call(
        functools.partial(feed_kernel, tile),
        grid=(2,),
        in_specs=[scalars] + [anywhere] * 11,
        out_specs=[anywhere] * 6,
        out_shape=[shaped(square), shaped((part, width))] * 2 + [shaped((rows, width))] * 2,
        scratch_shapes=[
            pltpu.VMEM((rows, width), bf16),
            pltpu.VMEM((width, rows), bf16),
            pltpu.VMEM((rows, width), bf16),
            pltpu.VMEM((2, width, part), bf16),
            pltpu.VMEM((2, part, width), bf16),
            pltpu.VMEM((rows, width), f32),
            pltpu.VMEM((rows, width), f32),
            pltpu.VMEM((part, rows), bf16),
            pltpu.VMEM((rows, part), bf16),
            pltpu.VMEM((rows, width), bf16),
            pltpu.VMEM((rows, width), bf16),
            pltpu.VMEM((2, 2, width, part), bf16),
            pltpu.SemaphoreType.DMA((9 + 2 * blocks,)),
            pltpu.SemaphoreType.DMA((4 + 2 * blocks,)),
        ],
        compiler_params=params(),
        cost_estimate=cost(32),
        name="feed_pass",
    )(order, h, turned_h, d_out, *ups, *downs)


def middle_kernel(pairs, tile, order, resid, h, d_out, *refs):
    mixed_part, grad_part, attended, inverse = refs[:4]
    phi = refs[4:6]
    gain, cross, wo_any, up_any, down_any = refs[6:11]
    pieces = refs[11:15]
    (
        act_out,
        pre_out,
        mixed_out,
        resid_out,
        gn_out,
        gd_out,
        turned_n_out,
        turned_d_out,
        state_out,
    ) = refs[15:24]
    state, wo_own, up, down, wo_oth, sems = refs[24:]
    step = pl.program_id(0)
    top = first_sublanes()
    wide = 128 * pairs
    units = up.shape[1]

    def early_copies():
        return [
            pltpu.make_async_copy(up_any, up, sems.at[0]),
            pltpu.make_async_copy(down_any, down, sems.at[1]),
        ]

    def late_copies():
        return [pltpu.make_async_copy(wo_any, wo_own, sems.at[2])] + quarter_copies(
            pieces, order, wo_oth, units // 4, wide // 4, sems, 3
        )

    @pl.when(step == 0)
    def _():
        for copy in early_copies() + late_copies():
            copy.start()
        state[...] = jnp.zeros_like(state)
        for copy in early_copies():
            copy.wait()

    h_two = h[...]
    d_low = d_out[...]
    mixed = grad_h = None
    for at in range(0, units, tile):
        low, slope = feed_forward(dot(h_two, up[:, at : at + tile]))
        grad_pre = (dot_t(d_low, down[at : at + tile, :]) * slope).astype(bf16)
        act_out[at : at + tile, :] = low.T
        for col in range(at, at + tile, 256):
            pre_out[col // 768, :, col % 768 : col % 768 + 256] = grad_pre[
                :, col - at : col - at + 256
            ]
        mixed = add_to(mixed, dot(low, down[at : at + tile, :]))
        grad_h = add_to(grad_h, dot_t(grad_pre, up[:, at : at + tile]))
    summed = resid[...].astype(f32)
    normed, spread = norm_parts(summed)
    mixed_out[...] = (summed + mixed_part[...].astype(f32) + mixed).astype(bf16)
    grad_h = grad_part[...].astype(f32) + grad_h
    grad_resid = (d_low.astype(f32) + norm_back(grad_h, normed, spread, gain[...])).astype(bf16)
    resid_out[...] = grad_resid

    @pl.when(step == 0)
    def _():
        for copy in late_copies():
            copy.wait()

    for half in range(2):
        grad_att = dot_t(grad_resid, (wo_own, wo_oth)[half][...]).astype(bf16).astype(f32)
        for p in range(pairs):
            at = wide * half + 128 * p
            own = grad_att[:, 128 * p : 128 * p + 128]
            scaled = own * inverse[:, at : at + 128].astype(f32)
            grad_n = scaled.astype(bf16)
            exact = attended[:, at : at + 128].astype(f32)
            grad_d = dot((scaled * exact).astype(bf16), cross[...]).astype(bf16)
            gn_out[:, at : at + 128] = grad_n
            gd_out[:, at : at + 128] = grad_d
            turned_n = grad_n.T
            turned_d = grad_d.T
            turned_n_out[at : at + 128, :] = turned_n
            turned_d_out[at : at + 128, :] = turned_d
            left = jnp.concatenate([turned_n, turned_d[0:16], turned_d[64:80]], axis=0)
            sums = dot(left, phi[half][:, 256 * p : 256 * p + 256])
            state[half, 128 * p : 128 * p + 128] += jnp.where(
                top, sums[:128, :128], sums[:128, 128:]
            )
            row = wide + 2 * p
            state[half, row : row + 1] += sums[144:145, :128]
            state[half, row + 1 : row + 2] += sums[128:129, 128:]

    @pl.when(step == pl.num_programs(0) - 1)
    def _():
        state_out[...] = state[...].astype(bf16)


def middle_pass(
    order, resid, h_two, d_out, parts, attended, inverse, phis, gain, cross, owns, pieces, packed, block, tile
):
    rows, width = resid.shape
    wide = owns[0].shape[0]
    pairs = wide // 128
    units = owns[1].shape[1]
    cols_out = [width, width, 2 * wide, 2 * wide]
    spots = units // 768
    return pl.pallas_call(
        functools.partial(middle_kernel, pairs, tile),
        grid=(rows // block,),
        in_specs=[scalars]
        + [by_rows(block, width)] * 5
        + [by_rows(block, 2 * wide)] * 4
        + [once(gain.shape), once(cross.shape)]
        + [anywhere] * 7,
        out_specs=[by_cols(units, block), pl.BlockSpec((spots, block, 768), lambda c: (0, c, 0))]
        + [by_rows(block, c) for c in cols_out]
        + [by_cols(2 * wide, block)] * 2
        + [once(packed)],
        out_shape=[shaped((units, rows)), shaped((spots, rows, 768))]
        + [shaped((rows, c)) for c in cols_out]
        + [shaped((2 * wide, rows))] * 2
        + [shaped(packed)],
        scratch_shapes=[
            pltpu.VMEM(packed, f32),
            pltpu.VMEM((wide, width), bf16),
            pltpu.VMEM((width, units), bf16),
            pltpu.VMEM((units, width), bf16),
            pltpu.VMEM((wide, width), bf16),
            pltpu.SemaphoreType.DMA((7,)),
        ],
        compiler_params=params(),
        cost_estimate=cost(35),
        name="middle_pass",
    )(order, resid, h_two, d_out, *parts, attended, inverse, *phis, gain, cross, *owns, *pieces)


def up_kernel(core, left, right, got, out):
    product = dot(left[...], right[0])
    mine = pl.program_id(0) == core[0]

    @pl.when(mine)
    def _():
        out[...] = (product + got[...].astype(f32)).astype(bf16)

    @pl.when(jnp.logical_not(mine))
    def _():
        out[...] = product.astype(bf16)


def up_pass(core, left, right, got):
    width, rows = left.shape
    count, _, part = right.shape
    return pl.pallas_call(
        up_kernel,
        grid_spec=pltpu.PrefetchScalarGridSpec(
            num_scalar_prefetch=1,
            grid=(count,),
            in_specs=[
                once((width, rows)),
                pl.BlockSpec((1, rows, part), lambda s, c: (s, 0, 0)),
                once((width, part)),
            ],
            out_specs=pl.BlockSpec((width, part), lambda s, c: (0, s)),
        ),
        out_shape=shaped((width, count * part)),
        compiler_params=params(),
        cost_estimate=cost(8),
        name="up_pass",
    )(core, left, right, got)


def down_kernel(core, left, right, own_left, oth_left, right_more, out, more_out):
    out[...] = dot(left[...], right[...]).astype(bf16)
    for side, rows in enumerate((own_left, oth_left)):
        more_out[side] = dot(rows[...], right_more[...]).astype(bf16)


def down_pass(half, left, right, left_more, right_more):
    rows, width = right.shape
    part = left.shape[0] // 2
    more = left_more.shape[0] // 4
    tile = width // 2
    cols = pl.BlockSpec((rows, tile), lambda s, half: (0, s))
    mine = lambda count, first: pl.BlockSpec((count, rows), lambda s, half: (first + half[0], 0))
    return pl.pallas_call(
        down_kernel,
        grid_spec=pltpu.PrefetchScalarGridSpec(
            num_scalar_prefetch=1,
            grid=(2,),
            in_specs=[mine(part, 0), cols, mine(more, 0), mine(more, 2), cols],
            out_specs=[
                pl.BlockSpec((part, tile), lambda s, half: (0, s)),
                pl.BlockSpec((2, more, tile), lambda s, half: (0, s, 0)),
            ],
        ),
        out_shape=[shaped((part, width)), shaped((2, 2 * more, tile))],
        compiler_params=params(),
        cost_estimate=cost(8),
        name="down_pass",
    )(half, left, right, left_more, left_more, right_more)


def back_kernel(pairs, at_pair, more, core, *refs):
    sides = (refs[:15], refs[15:30])
    incoming, later, ones, h_any = refs[30:34]
    earlier = refs[34 : 34 + more]
    grad_outs = refs[34 + more : 36 + more]
    send_out, keep_out, map_out = refs[36 + more : 39 + more]
    held, state, grads, maps, turned_h, sem = refs[39 + more :]
    step = pl.program_id(0)
    last = pl.num_programs(0) - 1
    first = first_lanes()
    top = first_sublanes()
    size = CHUNK
    inner = refs[2].shape[0] // CHUNK
    past = lax.broadcasted_iota(jnp.int32, (size, size), 0) >= lax.broadcasted_iota(
        jnp.int32, (size, size), 1
    )
    one = jnp.ones((1, 1), bf16)

    @pl.when(step == 0)
    def _():
        pltpu.make_async_copy(h_any, turned_h, sem.at[0]).start()
        maps[...] = jnp.zeros_like(maps)
        for side in range(2):
            for h_at in range(2):
                held[side, h_at] = read_state(incoming.at[side], at_pair, h_at, pairs)
                state[side, h_at] = read_state(later.at[side], at_pair, h_at, pairs)

    for sub in reversed(range(inner)):
        run = slice(CHUNK * sub, CHUNK * sub + CHUNK)
        for side in range(2):
            (q, k, v, turned_v, pq, turned_pq, pk, turned_pk) = sides[side][:8]
            (gn, gd, turned_n, turned_d, prefix, fq, fk) = sides[side][8:]
            grads_q, grads_k, grads_v = [], [], []
            for h_at in range(2):
                sel = first if h_at == 0 else jnp.logical_not(first)
                sel_top = top if h_at == 0 else jnp.logical_not(top)
                lanes = slice(128 * h_at, 128 * h_at + 128)
                padded_v = jnp.where(sel, v[run, :], one)
                padded_vt = jnp.where(sel_top, turned_v[:, run], one)
                padded_g = jnp.where(sel, gn[run, :], gd[run, :])
                padded_gt = jnp.where(sel_top, turned_n[:, run], turned_d[:, run])
                before = (prefix[sub, h_at].astype(f32) + held[side, h_at]).astype(bf16)
                after = state[side, h_at].astype(bf16)
                e = jnp.where(past, dot_t(padded_g, padded_v), 0.0).astype(bf16)
                s = jnp.where(past, dot(pq[run, lanes], turned_pk[lanes, run]), 0.0).astype(bf16)
                grads_q.append(dot(e, pk[run, lanes]) + dot(padded_g, before))
                grads_k.append(dot(turned_pq[lanes, run], e) + dot(after.T, padded_vt))
                grads_v.append(dot(padded_gt, s) + dot(after, turned_pk[lanes, run]))
                state[side, h_at] += dot(padded_gt, pq[run, lanes])

            grad_phi = jnp.concatenate(grads_q, axis=1)
            phi = pq[run, :].astype(f32)
            shared = dot((phi * grad_phi).astype(bf16), ones[...])
            grad_u = (phi * (grad_phi - shared)).astype(bf16)
            maps[side, 0] += dot(q[:, run], grad_u)
            grad_q = dot_t(grad_u, fq[0]).astype(bf16)

            grad_phi = jnp.concatenate(grads_k, axis=0).reshape(4, 64, size)
            phi = turned_pk[:, run].astype(f32).reshape(4, 64, size)
            shared = jnp.sum(phi * grad_phi, axis=1, keepdims=True)
            grad_u = (phi * (grad_phi - shared)).reshape(256, size).astype(bf16)
            maps[side, 1] += dot_t(k[:, run], grad_u)
            grad_k = dot(fk[0], grad_u).astype(bf16).T
            grad_v = jnp.where(top, grads_v[0], grads_v[1]).astype(bf16).T

            joined = jnp.concatenate([grad_q, grad_k, grad_v], axis=1)
            grad_outs[side][run, :] = joined
            where = pl.multiple_of(((last - step) * inner + sub) * size, size)
            grads[pl.ds(where, size), 384 * side : 384 * side + 384] = joined

    @pl.when(step == last)
    def _():
        pltpu.make_async_copy(h_any, turned_h, sem.at[0]).wait()
        product = dot(turned_h[...], grads[...]).astype(bf16)
        part = product.shape[0] // 2
        mine = core[0] == 0
        for side in range(2):
            cols = slice(384 * side, 384 * side + 384)
            low, high = product[:part, cols], product[part:, cols]
            send_out[side, 0:part] = jnp.where(mine, high, low)
            keep_out[side, 0:part] = jnp.where(mine, low, high)
            joins = [
                jnp.where(top, maps[side, i][:, :128], maps[side, i][:, 128:]) for i in range(2)
            ]
            turns = [pltpu.roll(j, 64, 1) for j in joins]
            own_map = jnp.where(first, joins[0] - turns[0], turns[1] - joins[1]).astype(bf16)
            map_out[side] = own_map
            if more:
                whole = jnp.concatenate([m[side] for m in earlier] + [own_map], axis=1)
                low, high = whole[:64], whole[64:]
                send_out[side, part : part + 64] = jnp.where(mine, high, low)
                keep_out[side, part : part + 64] = jnp.where(mine, low, high)
                send_out[side, part + 64 :] = jnp.zeros_like(low)
                keep_out[side, part + 64 :] = jnp.zeros_like(low)


def back_pass(at, core, sides, seconds, prefix, incoming, later, fq, fk, ones, turned_h, earlier):
    rows = sides[0][2].shape[0]
    pairs = fq[0].shape[0]
    width = turned_h.shape[0]
    count = rows // BLOCK
    here = lambda cols, spot: pl.BlockSpec((BLOCK, cols), lambda c, core: (count - 1 - c, spot))
    turned = lambda cols, spot: pl.BlockSpec((cols, BLOCK), lambda c, core: (spot, count - 1 - c))
    weights = pl.BlockSpec((1, 128, 256), lambda c, core: (at, 0, 0))
    states = pl.BlockSpec(
        (BLOCK // CHUNK, 2, 128, 128), lambda c, core: (count - 1 - c, at, 0, 0)
    )
    more = len(earlier)
    sums = (2, width // 2 + (128 if more else 0), 384)
    in_specs, args = [], []
    for side in range(2):
        both = pairs * side + at
        in_specs += [turned(128, at), turned(128, at), here(128, at), turned(128, at)]
        in_specs += [here(256, at), turned(256, at)] * 2
        in_specs += [here(128, both)] * 2 + [turned(128, both)] * 2
        in_specs += [states, weights, weights]
        args += [*sides[side], *seconds, prefix[side], fq[side], fk[side]]
    return pl.pallas_call(
        functools.partial(back_kernel, pairs, at, more),
        grid_spec=pltpu.PrefetchScalarGridSpec(
            num_scalar_prefetch=1,
            grid=(count,),
            in_specs=in_specs
            + [once(incoming.shape)] * 2
            + [once(ones.shape), anywhere]
            + [once((2, 128, 128))] * more,
            out_specs=[here(384, 0)] * 2 + [once(sums)] * 2 + [once((2, 128, 128))],
            scratch_shapes=[
                pltpu.VMEM((2, 2, 128, 128), f32),
                pltpu.VMEM((2, 2, 128, 128), f32),
                pltpu.VMEM((rows, 768), bf16),
                pltpu.VMEM((2, 2, 128, 256), f32),
                pltpu.VMEM((width, rows), bf16),
                pltpu.SemaphoreType.DMA((1,)),
            ],
        ),
        out_shape=[shaped((rows, 384))] * 2 + [shaped(sums)] * 2 + [shaped((2, 128, 128))],
        compiler_params=params(),
        cost_estimate=cost(17),
        name="back_pass",
    )(core, *args, incoming, later, ones, turned_h, *earlier)


def tokens_kernel(pairs, count, order, tokens, resid, gain, *refs):
    pieces = refs[: 1 + count]
    grads = refs[1 + count : 1 + count + 2 * pairs]
    out, w_own, w_oth, sems = refs[1 + count + 2 * pairs :]

    @pl.when(pl.program_id(0) == 0)
    def _():
        copies = qkv_copies(pieces[:1], order, (0, 1, 2), w_own, sems, 0)
        copies += qkv_copies(pieces[1:], order, (0, 1, 2), w_oth, sems, 3)
        run_copies(copies)

    normed, spread = norm_parts(tokens[...].astype(f32))
    total = None
    for half in range(2):
        joined = jnp.concatenate(
            [
                g[:, 128 * kind : 128 * kind + 128]
                for kind in range(3)
                for g in grads[half * pairs : half * pairs + pairs]
            ],
            axis=1,
        )
        part = dot_t(joined, (w_own, w_oth)[half][...])
        total = part if total is None else total + part
    back = norm_back(total, normed, spread, gain[...])
    out[...] = (resid[...].astype(f32) + back).astype(bf16)


def tokens_pass(order, tokens, resid, gain, w_own, pieces, grads, block, first, blocks, done=None):
    rows, width = tokens.shape
    pairs = len(grads) // 2
    cols = 3 * w_own.shape[2]
    count = len(pieces)
    cut = lambda cols: pl.BlockSpec((block, cols), lambda c: (first + c, 0))
    operands = [order, tokens, resid, gain, w_own, *pieces, *grads]
    more = [] if done is None else [done]

    def kernel(*refs):
        refs = list(refs)
        if more:
            del refs[len(operands)]
        tokens_kernel(pairs, count, *refs)

    return pl.pallas_call(
        kernel,
        grid=(blocks,),
        in_specs=[scalars]
        + [cut(width)] * 2
        + [once(gain.shape)]
        + [anywhere] * (1 + count)
        + [cut(384)] * len(grads)
        + [anywhere] * len(more),
        out_specs=cut(width),
        out_shape=shaped((rows, width)),
        input_output_aliases={len(operands): 0} if more else {},
        scratch_shapes=[
            pltpu.VMEM((width, cols), bf16),
            pltpu.VMEM((width, cols), bf16),
            pltpu.SemaphoreType.DMA((3 + 3 * count,)),
        ],
        compiler_params=params(),
        cost_estimate=cost(8),
        name="tokens_pass",
    )(*operands, *more)


def cross_to(value, axis, flip):
    count = lax.axis_size(axis)
    return lax.ppermute(value, axis, [(i, i ^ flip) for i in range(count)])


def swap(value, axis, bit):
    return cross_to(value, axis, 1 << bit)


def bit_of(axis, bit):
    return (lax.axis_index(axis) >> bit) & 1


def bits_of(axis):
    return lax.axis_size(axis).bit_length() - 1


def ordered(bit, mine, theirs, axis=0):
    return jnp.where(
        bit == 0,
        jnp.concatenate([mine, theirs], axis),
        jnp.concatenate([theirs, mine], axis),
    )


def add_low(*parts):
    total = parts[0].astype(f32)
    for part in parts[1:]:
        total = total + part.astype(f32)
    return total.astype(bf16)


class Flow:
    def __init__(self):
        self.ready = {}
        self.steps = {}
        self.done = {}

    def start(self, name, steps):
        self.steps[name] = steps
        self.ready[name] = next(steps)

    def slot(self, names, others):
        names = [n for n in names if n in self.steps]
        tied, others = lax.optimization_barrier(([self.ready[n] for n in names], others))
        for name, value in zip(names, tied):
            self.move(name, value)
        return others

    def move(self, name, value):
        try:
            self.ready[name] = self.steps[name].send(value)
        except StopIteration as end:
            self.done[name] = end.value
            del self.steps[name], self.ready[name]

    def finish(self, names):
        for name in names:
            while name in self.steps:
                self.move(name, self.ready[name])


def fetch_halves(weight, axis):
    count = weight.shape[axis] // 2
    part = yield lax.dynamic_slice_in_dim(weight, bit_of("ctx", 0) * count, count, axis)
    part = yield swap(part, "heads", 0)
    return [part, swap(part, "ctx", 0)]


def fetch_quarters(weights, across, axis):
    place = 2 * bit_of("ctx", 0) + bit_of(*across)
    parts = []
    for weight in weights:
        count = weight.shape[axis] // 4
        parts.append(lax.dynamic_slice_in_dim(weight, place * count, count, axis))
    part = yield jnp.concatenate(parts, axis)
    part = yield swap(part, "heads", 0)
    part, second = yield part, swap(part, *across)
    return [part, second, swap(part, "ctx", 0), swap(second, "ctx", 0)]


def fetch_order():
    core = bit_of("ctx", 0)
    order = [core, 1 - core]
    for across in (bit_of("ctx", 1), bit_of("batch", 0)):
        order += [
            2 * core + across,
            2 * core + 1 - across,
            2 - 2 * core + across,
            3 - 2 * core - across,
        ]
    return jnp.stack(order).astype(jnp.int32)


def reduce_sums(send, keep, ways, spread=False):
    send = yield send
    got = swap(send, "ctx", 0)
    left, oth = add_low(keep[0], got[0]), add_low(keep[1], got[1])
    return (yield from reduce_tail(left, [swap(oth, "heads", 0)], ways, spread))


def send_over(send, keep):
    send = yield send
    total = yield add_low(keep, swap(send, "ctx", 0))
    return (yield swap(total, "heads", 0))


def send_over_late(send, keep):
    send = yield send
    got = swap(send, "ctx", 0)
    count = keep.shape[0] // 2
    first, rest = yield [add_low(keep[i], got[i]) for i in (slice(0, count), slice(count, None))]
    first, rest = yield swap(first, "heads", 0), rest
    rest = yield rest
    return jnp.concatenate([first, (yield swap(rest, "heads", 0))])


def reduce_tail(left, rights, ways, spread=False):
    stages = [("ctx", b, 1) for b in range(1, bits_of("ctx"))]
    count = bits_of("batch")
    along = [("batch", b, min(ways, count - b)) for b in range(0, count, ways)]
    if not spread:
        stages += along
    for axis, low_bit, bits in stages:
        ways = 1 << bits
        place = (lax.axis_index(axis) >> low_bit) & (ways - 1)
        count = left.shape[0] // ways
        cut = lambda at: add_low(
            *[lax.dynamic_slice_in_dim(a, at * count, count, 0) for a in (left, *rights)]
        )
        sends = [cut(place ^ flip) for flip in range(1, ways)]
        left, sends = yield (cut(place), sends)
        rights = [cross_to(s, axis, (i + 1) << low_bit) for i, s in enumerate(sends)]
    whole = add_low(left, *rights)
    for axis, low_bit, bits in along if spread else []:
        whole = yield whole
        got = [cross_to(whole, axis, flip << low_bit) for flip in range(1, 1 << bits)]
        whole = add_low(whole, *got)
    for axis, low_bit, bits in reversed(stages):
        whole = yield whole
        parts = [whole] + [cross_to(whole, axis, flip << low_bit) for flip in range(1, 1 << bits)]
        for b in range(bits):
            bit = bit_of(axis, low_bit + b)
            parts = [ordered(bit, parts[i], parts[i + 1]) for i in range(0, len(parts), 2)]
        whole = parts[0]
    whole = yield whole
    return (yield (whole, swap(whole, "ctx", 0)))


def send_once(value, axis, bit):
    value = yield value
    return swap(value, axis, bit)


def scan_runs(total, boundary, rows, backward):
    place, side = lax.axis_index("ctx"), lax.axis_index("heads")
    second = lambda spot, half: (2 * spot + half) * rows >= boundary
    end = 0 if backward else 1
    total = yield total
    got = jnp.flip(swap(total, "heads", 0).astype(f32), 0)
    total = total.astype(f32)
    mine = second(place, side)
    joins = second(place, 0) == second(place, 1)
    received = jnp.where(jnp.logical_and(side == end, joins), got, 0.0)
    near = jnp.where(side == end, total, got)
    far = jnp.where(side == end, got, total)
    low = yield (near + jnp.where(joins, far, 0.0)).astype(bf16)
    for flip in range(1, lax.axis_size("ctx")):
        got = cross_to(low, "ctx", flip).astype(f32)
        spot = place ^ flip
        ahead = spot > place if backward else spot < place
        takes = jnp.logical_and(ahead, second(spot, end) == mine)
        received = received + jnp.where(takes, got, 0.0)
    received = yield received
    return received


def shards(tokens, lengths, gain_one, w_qkv, f_query, f_key, w_out, gain_two, w_up, w_down, d_out):
    rows, width = tokens.shape
    heads, size, _ = f_query.shape
    pairs = heads // 2
    wide = heads * size
    units = w_up.shape[1]
    assert size == 64 and lax.axis_size("heads") == 2 and 1536 % rows == 0
    boundary = lengths[0, 0]
    place = bit_of("ctx", 0)
    order = fetch_order()
    gain_one_row = gain_one.reshape(1, width)
    gain_two_row = gain_two.reshape(1, width)

    spots = np.arange(256) // 64
    ones = jnp.asarray(spots[:, None] == spots[None, :], bf16)
    cross = jnp.asarray((spots[:128, None] != spots[None, :128]) * (-1.0 / 64.0), bf16)
    signs = jnp.asarray(np.kron(np.array([[1, -1, 1, -1]]), np.eye(64)), bf16)

    flow = Flow()
    slot = flow.slot
    qkv_own = jnp.transpose(w_qkv, (1, 0, 2))
    flow.start("maps", send_once(jnp.stack([f_query, f_key]), "heads", 0))
    flow.start("qkv", fetch_halves(qkv_own, 1))
    flow.start("up", fetch_quarters([w_up], ("ctx", 1), 1))
    flow.start("down", fetch_quarters([w_down, w_out], ("batch", 0), 0))
    (tokens,) = slot(["maps", "qkv"], (tokens,))

    h_one, turned_h = norm_one(tokens, gain_one_row)
    maps_oth = flow.done["maps"]
    empty = jnp.zeros((wide + 16, 128), bf16)
    keys = [key_pass(h_one, [qkv_own], order, f_key, signs, empty)]
    (keys[0][6], order, maps_oth) = slot(["qkv", "up", "down"], (keys[0][6], order, maps_oth))
    qkv_oth = flow.done["qkv"]
    keys.append(key_pass(h_one, qkv_oth, order, maps_oth[1], signs, keys[0][6][1]))
    flow.start("scan", scan_runs(keys[1][6], boundary, rows, False))
    (keys[1][1], order) = slot(["scan", "up"], (keys[1][1], order))
    queries = []
    for at, weights in enumerate(([qkv_own], qkv_oth)):
        queries.append(
            query_pass(
                h_one,
                weights,
                order,
                keys[at][4],
                keys[at][1],
                keys[at][5],
                (f_query, maps_oth[0])[at],
                signs,
            )
        )
        if at == 0:
            (queries[0][0], order) = slot(["scan", "up", "down"], (queries[0][0], order))
    (queries[1][0], order) = slot(["scan", "down"], (queries[1][0], order))
    ups, downs, incoming = (flow.done[n] for n in ("up", "down", "scan"))
    q, phi_q, turned_pq, numer, _, fq = zip(*queries)
    k, v, turned_v, phi_k, turned_pk, prefix, _, _, fk = zip(*keys)

    feed_order = order[2:]
    out_order = order[6:]
    attended, turned_a, inverse, resid, h_two, turned_two = front_pass(
        out_order, tokens, numer, phi_q, incoming, gain_two_row, w_out, downs, 512
    )
    send_up, send_down, keep_up, keep_down, *parts = feed_pass(
        feed_order, h_two, turned_two, d_out, ups, downs, 768
    )
    flow.start("oth_up", send_over(send_up, keep_up))
    flow.start("oth_down", send_over_late(send_down, keep_down))
    slot(["oth_up", "oth_down"], ())
    (out_order,) = slot(["oth_up", "oth_down"], (out_order,))
    (
        act,
        grad_pre,
        mixed,
        grad_resid,
        gn,
        gd,
        turned_n,
        turned_gd,
        grad_totals,
    ) = middle_pass(
        out_order,
        resid,
        h_two,
        d_out,
        parts,
        attended,
        inverse,
        phi_q,
        gain_two_row,
        cross,
        (w_out, w_up, w_down),
        downs,
        incoming.shape,
        256,
        768,
    )
    flow.start("later", scan_runs(grad_totals, boundary, rows, True))
    near, away = place.reshape(1), (1 - place).reshape(1)
    (near, grad_pre) = slot(["later", "oth_up", "oth_down"], (near, grad_pre))
    up_sum = up_pass(near, turned_two, grad_pre, flow.done["oth_up"])
    (away, act, up_sum) = slot(["later", "oth_down"], (away, act, up_sum))
    everyone = ("batch", "ctx")
    up_sum = lax.psum_scatter(up_sum, everyone, scatter_dimension=0, tiled=True)
    send, out_send = down_pass(away, act, d_out, turned_a, grad_resid)
    flow.start("own_down", send_once(send, "ctx", 0))
    (near, out_send) = slot(["later", "own_down", "oth_down"], (near, out_send))
    keep_down, out_keep = down_pass(near, act, d_out, turned_a, grad_resid)
    got, right = flow.done["own_down"], flow.done["oth_down"]
    flow.start("down_sum", reduce_tail(keep_down, [got, right], 1))
    (near, out_keep) = slot(["down_sum"], (near, out_keep))
    later = flow.done["later"]

    grads, maps, sends, keeps = [[], []], [], [], []
    feeds = ["down_sum"]
    plan = [feeds, ["qkv0"] + feeds, ["qkv1", "qkv0"] + feeds]
    names = (q, k, v, turned_v, phi_q, turned_pq, phi_k, turned_pk)
    for at in range(pairs):
        own, oth, send, keep, map_part = back_pass(
            at,
            near,
            [[a[side] for a in names] for side in range(2)],
            [gn, gd, turned_n, turned_gd],
            prefix,
            incoming,
            later,
            fq,
            fk,
            ones,
            turned_h,
            maps if at == pairs - 1 else [],
        )
        grads[0].append(own)
        grads[1].append(oth)
        maps.append(map_part)
        sends.append(send)
        keeps.append(keep)
        if at == pairs - 2:
            flow.start(
                "qkv0",
                reduce_sums(
                    jnp.concatenate(sends + [out_send], axis=1),
                    jnp.concatenate(keeps + [out_keep], axis=1),
                    2,
                ),
            )
        if at == pairs - 1:
            flow.start("qkv1", reduce_sums(send, keep, 2))
        tied = (own, near) if at < pairs - 1 else (own, near, up_sum)
        (grads[0][at], near, *rest) = slot(plan[at], tied)
        if rest:
            (up_sum,) = rest
            up_sum = lax.all_gather(up_sum, everyone, axis=0, tiled=True)
    order = order + 0 * near[0]
    tokens_args = (tokens, grad_resid, gain_one_row, qkv_own, qkv_oth, grads[0] + grads[1], 256)
    blocks = rows // 256
    early = blocks // 2
    grad_tokens = tokens_pass(order, *tokens_args, 0, early)
    tail = ["qkv1", "qkv0"]
    (grad_tokens, order) = slot(tail + feeds, (grad_tokens, order))
    grad_tokens = tokens_pass(order, *tokens_args, early, blocks - early, grad_tokens)
    (grad_tokens,) = slot(tail + feeds, (grad_tokens,))
    (up_sum,) = slot(tail + feeds, (up_sum,))
    grad_up = up_sum.astype(f32)
    gain_two_part = jnp.sum(grad_up * w_up.astype(f32), axis=1)
    (grad_up, gain_two_part) = slot(tail + feeds, (grad_up, gain_two_part))
    flow.finish(feeds)
    grad_down = ordered(place, *flow.done["down_sum"]).astype(f32)
    (grad_down,) = slot(tail, (grad_down,))
    flow.finish(list(flow.steps))
    part = width // 2
    (mine, theirs), (mine_last, theirs_last) = flow.done["qkv0"], flow.done["qkv1"]
    join = lambda mine, theirs: ordered(place, mine, theirs)
    beside = lambda a: jnp.concatenate([a[: wide // 2], a[wide // 2 :]], axis=1)
    more = part * (pairs - 1)
    grad_out = join(beside(mine[more:]), beside(theirs[more:])).astype(f32)
    parts = [
        join(mine[part * at : part * at + part], theirs[part * at : part * at + part])
        for at in range(pairs - 1)
    ]
    parts.append(join(mine_last[:part], theirs_last[:part]))
    grad_qkv = jnp.stack(
        [
            jnp.concatenate([p[:, 128 * kind : 128 * kind + 128] for p in parts], axis=1)
            for kind in range(3)
        ]
    )
    grad_qkv = grad_qkv.astype(f32)
    gain_one_part = jnp.sum(grad_qkv * qkv_own.astype(f32), axis=(0, 2))
    gains = jnp.stack([gain_one_part, gain_two_part])
    gains = (gains + swap(gains, "heads", 0)) / jnp.stack([gain_one, gain_two])
    grad_qkv = jnp.transpose(grad_qkv, (1, 0, 2))
    maps_sum = join(mine_last[part : part + 64], theirs_last[part : part + 64]).astype(f32)
    maps_sum = maps_sum.reshape(2, 64, pairs, 2, 64).transpose(3, 2, 0, 1, 4)
    grad_maps = maps_sum.reshape(2, heads, size, size)
    return (
        mixed,
        grad_tokens,
        gains[0],
        grad_qkv,
        grad_maps[0],
        grad_maps[1],
        grad_out,
        gains[1],
        grad_up,
        grad_down,
    )


def solution(mesh):
    in_specs = (
        P(("batch", "ctx", "heads"), None),
        P("batch", None),
        P(),
        P(None, None, "heads"),
        P("heads", None, None),
        P("heads", None, None),
        P("heads", None),
        P(),
        P(None, "heads"),
        P("heads", None),
        P(("batch", "ctx", "heads"), None),
    )
    out_specs = (
        P(("batch", "ctx", "heads"), None),
        P(("batch", "ctx", "heads"), None),
        P(),
        P(None, None, "heads"),
        P("heads", None, None),
        P("heads", None, None),
        P("heads", None),
        P(),
        P(None, "heads"),
        P("heads", None),
    )
    return jax.shard_map(shards, mesh=mesh, in_specs=in_specs, out_specs=out_specs, check_vma=False)
```

```python
import functools

import jax
import jax.numpy as jnp
import numpy as np
from jax import lax
from jax.experimental import pallas as pl
from jax.experimental.pallas import tpu as pltpu
from jax.sharding import PartitionSpec as P

epsilon = 1e-05
f32 = jnp.float32
bf16 = jnp.bfloat16
CHUNK = 256
BLOCK = 512
VMEM_LIMIT = 60 * 1024 * 1024
GELU_A = 0.7978845608028654
GELU_B = 0.044715


def dot(left, right):
    return lax.dot_general(left, right, (((1,), (0,)), ((), ())), preferred_element_type=f32)


def dot_t(left, right):
    return lax.dot_general(left, right, (((1,), (1,)), ((), ())), preferred_element_type=f32)


def params():
    return pltpu.CompilerParams(
        dimension_semantics=("arbitrary",), vmem_limit_bytes=VMEM_LIMIT
    )


def cost(micros):
    return pl.CostEstimate(flops=0, bytes_accessed=micros * 3_600_000, transcendentals=0)


def shaped(shape, kind=bf16):
    return jax.ShapeDtypeStruct(shape, kind)


def once(shape):
    zeros = (0,) * len(shape)
    return pl.BlockSpec(shape, lambda *_: zeros, pipeline_mode=pl.Buffered(1))


def by_rows(count, cols, at=0):
    return pl.BlockSpec((count, cols), lambda c, *_: (c, at))


def by_cols(rows, count, at=0):
    return pl.BlockSpec((rows, count), lambda c, *_: (at, c))


def map_block(maps, kind):
    return pl.BlockSpec(
        (1, *maps.shape[1:]), lambda *_: (kind, 0, 0, 0), pipeline_mode=pl.Buffered(1)
    )


anywhere = pl.BlockSpec(memory_space=pl.ANY)
scalars = pl.BlockSpec(memory_space=pltpu.SMEM)


def first_lanes():
    return lax.broadcasted_iota(jnp.int32, (1, 128), 1) < 64


def first_sublanes():
    return lax.broadcasted_iota(jnp.int32, (128, 1), 0) < 64


def build_maps(f, signs, turned_out, plain_out, pairs):
    top = first_sublanes()
    left = lax.broadcasted_iota(jnp.int32, (1, 256), 1) < 128
    for p in range(pairs):
        both = dot(f[0, 2 * p : 2 * p + 2].reshape(128, 64), signs[...])
        plain = jnp.where(top == left, both, 0.0)
        plain_out[p] = plain.astype(bf16)
        turned_out[p] = plain.T.astype(bf16)


def soft_rows(logits):
    count, size = logits.shape
    groups = logits.reshape(count // 64, 64, size)
    grown = jnp.exp(groups - jnp.max(groups, axis=1, keepdims=True))
    soft = grown * (1.0 / jnp.sum(grown, axis=1, keepdims=True))
    return soft.reshape(count, size)


def norm_parts(values):
    centred = values - jnp.mean(values, axis=1, keepdims=True)
    spread = lax.rsqrt(jnp.mean(centred * centred, axis=1, keepdims=True) + epsilon)
    return centred * spread, spread


def norm_back(gradient, normed, spread, gain):
    scaled = gradient * gain
    return spread * (
        scaled
        - jnp.mean(scaled, axis=1, keepdims=True)
        - normed * jnp.mean(scaled * normed, axis=1, keepdims=True)
    )


def run_copies(copies):
    for copy in copies:
        copy.start()
    for copy in copies:
        copy.wait()


def qkv_copies(pieces, order, kinds, target, sems, first_sem):
    rows = pieces[0].shape[1]
    copies = []
    for i, piece in enumerate(pieces):
        where = 0 if len(pieces) == 1 else pl.multiple_of(order[i] * rows, 16)
        for at, kind in enumerate(kinds):
            wide = piece.shape[2]
            copies.append(
                pltpu.make_async_copy(
                    piece.at[kind],
                    target.at[pl.ds(where, rows), pl.ds(at * wide, wide)],
                    sems.at[first_sem + len(copies)],
                )
            )
    return copies


def norm_kernel(tokens, gain, h_out, turned_out):
    normed, _ = norm_parts(tokens[...].astype(f32))
    low = (normed * gain[...]).astype(bf16)
    h_out[...] = low
    turned_out[...] = low.T


def norm_one(tokens, gain):
    rows, width = tokens.shape
    return pl.pallas_call(
        norm_kernel,
        grid=(rows // BLOCK,),
        in_specs=[by_rows(BLOCK, width), once((1, width))],
        out_specs=[by_rows(BLOCK, width), by_cols(width, BLOCK)],
        out_shape=[shaped((rows, width)), shaped((width, rows))],
        compiler_params=params(),
        cost_estimate=cost(5),
        name="norm_one",
    )(tokens, gain)


def write_state(state, state_out, pairs):
    top = first_sublanes()
    sums = []
    for p in range(pairs):
        state_out[128 * p : 128 * p + 128] = jnp.where(
            top, state[2 * p], state[2 * p + 1]
        ).astype(bf16)
        sums.append(state[2 * p, 64:65, :])
        sums.append(state[2 * p + 1, 0:1, :])
    tail = state_out.shape[0] - 128 * pairs
    sums.append(jnp.zeros((tail - 2 * pairs, 128), f32))
    state_out[128 * pairs :] = jnp.concatenate(sums, axis=0).astype(bf16)


def read_state(packed, p, h_at, pairs):
    row = 128 * pairs + 2 * p + h_at
    whole = packed[128 * p : 128 * p + 128, :]
    sums = packed[row : row + 1, :]
    sel = first_sublanes() if h_at == 0 else jnp.logical_not(first_sublanes())
    return jnp.where(sel, whole, sums)


def keys_kernel(pairs, count, more, order, h, f, signs, *refs):
    earlier, refs = refs[:more], refs[more:]
    pieces = refs[:count]
    (k_out, v_out, turned_v_out, phi_out, turned_phi_out, prefix_out, state_out) = refs[count : count + 7]
    fext, plain_out, w_kv, state, sems = refs[count + 7 :]
    step = pl.program_id(0)
    wide = 128 * pairs

    @pl.when(step == 0)
    def _():
        copies = qkv_copies(pieces, order, (1, 2), w_kv, sems, 0)
        for copy in copies:
            copy.start()
        build_maps(f, signs, fext, plain_out, pairs)
        state[...] = jnp.zeros_like(state)
        for copy in copies:
            copy.wait()

    kv_all = dot(h[...], w_kv[...]).astype(bf16)
    turned_k_all = kv_all[:, :wide].T
    turned_v_all = kv_all[:, wide:].T
    k_out[...] = turned_k_all
    v_out[...] = kv_all[:, wide:]
    turned_v_out[...] = turned_v_all
    top = first_sublanes()
    one = jnp.ones((1, 1), bf16)
    for sub in range(h.shape[0] // CHUNK):
        run = slice(CHUNK * sub, CHUNK * sub + CHUNK)
        turned_k, turned_v = turned_k_all[:, run], turned_v_all[:, run]
        prefix_out[sub] = state[...].astype(bf16)
        for p in range(pairs):
            turned_phi = soft_rows(dot(fext[p], turned_k[128 * p : 128 * p + 128])).astype(bf16)
            phi = turned_phi.T
            turned_phi_out[256 * p : 256 * p + 256, run] = turned_phi
            phi_out[run, 256 * p : 256 * p + 256] = phi
            values = turned_v[128 * p : 128 * p + 128]
            for h_at in range(2):
                sel = top if h_at == 0 else jnp.logical_not(top)
                padded = jnp.where(sel, values, one)
                state[2 * p + h_at] += dot(padded, phi[:, 128 * h_at : 128 * h_at + 128])

    @pl.when(step == pl.num_programs(0) - 1)
    def _():
        state_out[0] = earlier[0][1] if more else jnp.zeros_like(state_out[0])
        write_state(state, state_out.at[1], pairs)


def key_pass(h, weights, order, maps, signs, earlier):
    rows, width = h.shape
    pairs = maps.shape[1] // 2
    wide = 128 * pairs
    count = rows // CHUNK
    packed = wide + 16
    return list(
        pl.pallas_call(
            functools.partial(keys_kernel, pairs, len(weights), len(earlier)),
            grid=(rows // BLOCK,),
            in_specs=[
                scalars,
                by_rows(BLOCK, width),
                map_block(maps, 1),
                once(signs.shape),
            ]
            + [once((2, packed, 128))] * len(earlier)
            + [anywhere] * len(weights),
            out_specs=[
                by_cols(wide, BLOCK),
                by_rows(BLOCK, wide),
                by_cols(wide, BLOCK),
                by_rows(BLOCK, 2 * wide),
                by_cols(2 * wide, BLOCK),
                pl.BlockSpec((BLOCK // CHUNK, 2 * pairs, 128, 128), lambda c: (c, 0, 0, 0)),
                once((2, packed, 128)),
                once((pairs, 256, 128)),
                once((pairs, 128, 256)),
            ],
            out_shape=[
                shaped((wide, rows)),
                shaped((rows, wide)),
                shaped((wide, rows)),
                shaped((rows, 2 * wide)),
                shaped((2 * wide, rows)),
                shaped((count, 2 * pairs, 128, 128)),
                shaped((2, packed, 128)),
                shaped((pairs, 256, 128)),
                shaped((pairs, 128, 256)),
            ],
            scratch_shapes=[
                pltpu.VMEM((width, 2 * wide), bf16),
                pltpu.VMEM((2 * pairs, 128, 128), f32),
                pltpu.SemaphoreType.DMA((2 * len(weights),)),
            ],
            compiler_params=params(),
            cost_estimate=cost(10),
            name="key_pass",
        )(order, h, maps, signs, *earlier, *weights)
    )


def query_kernel(pairs, count, order, h, turned_k_phi, v, prefix, f, signs, *refs):
    pieces = refs[:count]
    q_out, phi_out, turned_phi_out, numer_out, fext, plain_out, w_q, sems = refs[count:]

    @pl.when(pl.program_id(0) == 0)
    def _():
        copies = qkv_copies(pieces, order, (0,), w_q, sems, 0)
        for copy in copies:
            copy.start()
        build_maps(f, signs, fext, plain_out, pairs)
        for copy in copies:
            copy.wait()

    turned_q_all = dot(h[...], w_q[...]).astype(bf16).T
    q_out[...] = turned_q_all
    first = first_lanes()
    one = jnp.ones((1, 1), bf16)
    size = CHUNK
    past = lax.broadcasted_iota(jnp.int32, (size, size), 0) >= lax.broadcasted_iota(
        jnp.int32, (size, size), 1
    )
    for sub in range(h.shape[0] // CHUNK):
        run = slice(CHUNK * sub, CHUNK * sub + CHUNK)
        turned_q = turned_q_all[:, run]
        for p in range(pairs):
            turned_phi = soft_rows(dot(fext[p], turned_q[128 * p : 128 * p + 128])).astype(bf16)
            phi = turned_phi.T
            turned_phi_out[256 * p : 256 * p + 256, run] = turned_phi
            phi_out[run, 256 * p : 256 * p + 256] = phi
            v_two = v[run, 128 * p : 128 * p + 128]
            for h_at in range(2):
                at = 256 * p + 128 * h_at
                sel = first if h_at == 0 else jnp.logical_not(first)
                padded = jnp.where(sel, v_two, one)
                phi_q = phi[:, 128 * h_at : 128 * h_at + 128]
                scores = dot(phi_q, turned_k_phi[at : at + 128, run])
                scores = jnp.where(past, scores, 0.0).astype(bf16)
                numer_out[run, at : at + 128] = (
                    dot(scores, padded) + dot_t(phi_q, prefix[sub, 2 * p + h_at])
                ).astype(bf16)


def query_pass(h, weights, order, turned_k_phi, v, prefix, maps, signs):
    rows, width = h.shape
    pairs = maps.shape[1] // 2
    wide = 128 * pairs
    return list(
        pl.pallas_call(
            functools.partial(query_kernel, pairs, len(weights)),
            grid=(rows // BLOCK,),
            in_specs=[
                scalars,
                by_rows(BLOCK, width),
                by_cols(2 * wide, BLOCK),
                by_rows(BLOCK, wide),
                pl.BlockSpec((BLOCK // CHUNK, 2 * pairs, 128, 128), lambda c: (c, 0, 0, 0)),
                map_block(maps, 0),
                once(signs.shape),
            ]
            + [anywhere] * len(weights),
            out_specs=[
                by_cols(wide, BLOCK),
                by_rows(BLOCK, 2 * wide),
                by_cols(2 * wide, BLOCK),
                by_rows(BLOCK, 2 * wide),
                once((pairs, 256, 128)),
                once((pairs, 128, 256)),
            ],
            out_shape=[
                shaped((wide, rows)),
                shaped((rows, 2 * wide)),
                shaped((2 * wide, rows)),
                shaped((rows, 2 * wide)),
                shaped((pairs, 256, 128)),
                shaped((pairs, 128, 256)),
            ],
            scratch_shapes=[
                pltpu.VMEM((width, wide), bf16),
                pltpu.SemaphoreType.DMA((len(weights),)),
            ],
            compiler_params=params(),
            cost_estimate=cost(15),
            name="query_pass",
        )(order, h, turned_k_phi, v, prefix, maps, signs, *weights)
    )


def quarter_copies(pieces, order, target, first_row, rows, sems, first_sem):
    copies = []
    for i, piece in enumerate(pieces):
        where = pl.multiple_of(order[6 + i] * rows, 16)
        copies.append(
            pltpu.make_async_copy(
                piece.at[pl.ds(first_row, rows)],
                target.at[pl.ds(where, rows)],
                sems.at[first_sem + i],
            )
        )
    return copies


def front_kernel(pairs, units, order, tokens, *refs):
    numer, phi = refs[:2], refs[2:4]
    incoming, gain, wo_any = refs[4:7]
    pieces = refs[7:11]
    attended_out, turned_a_out, inverse_out, resid_out, h_out, turned_h_out = refs[11:17]
    held, wo_own, wo_oth, sems = refs[17:]
    first = first_lanes()
    wide = 128 * pairs
    start = pl.program_id(0) == 0

    def weight_copies():
        return [pltpu.make_async_copy(wo_any, wo_own, sems.at[0])] + quarter_copies(
            pieces, order, wo_oth, units // 4, wide // 4, sems, 1
        )

    @pl.when(start)
    def _():
        for copy in weight_copies():
            copy.start()
        for half in range(2):
            for p in range(pairs):
                for h_at in range(2):
                    held[half, 2 * p + h_at] = read_state(
                        incoming.at[half], p, h_at, pairs
                    ).astype(bf16)

    for half in range(2):
        for p in range(pairs):
            sums = []
            for h_at in range(2):
                at = 256 * p + 128 * h_at
                sums.append(
                    numer[half][:, at : at + 128].astype(f32)
                    + dot_t(phi[half][:, at : at + 128], held[half, 2 * p + h_at])
                )
            numerator = jnp.where(first, sums[0], sums[1])
            swapped = 1.0 / jnp.where(first, sums[1], sums[0])
            inv = pltpu.roll(swapped, 64, 1)
            attended = (numerator * inv).astype(bf16)
            at = wide * half + 128 * p
            inverse_out[:, at : at + 128] = inv.astype(bf16)
            attended_out[:, at : at + 128] = attended
            turned_a_out[at : at + 128, :] = attended.T

    @pl.when(start)
    def _():
        for copy in weight_copies():
            copy.wait()

    resid = (
        tokens[...].astype(f32)
        + dot(attended_out[:, :wide], wo_own[...])
        + dot(attended_out[:, wide:], wo_oth[...])
    )
    resid_out[...] = resid.astype(bf16)
    normed, _ = norm_parts(resid)
    h_two = (normed * gain[...]).astype(bf16)
    h_out[...] = h_two
    turned_h_out[...] = h_two.T


def front_pass(order, tokens, numers, phis, incoming, gain, w_out, pieces, block):
    rows, width = tokens.shape
    wide = w_out.shape[0]
    pairs = wide // 128
    units = 4 * pieces[0].shape[0] - wide
    return pl.pallas_call(
        functools.partial(front_kernel, pairs, units),
        grid=(rows // block,),
        in_specs=[scalars, by_rows(block, width)]
        + [by_rows(block, 2 * wide)] * 4
        + [once(incoming.shape), once(gain.shape)]
        + [anywhere] * 5,
        out_specs=[
            by_rows(block, 2 * wide),
            by_cols(2 * wide, block),
            by_rows(block, 2 * wide),
            by_rows(block, width),
            by_rows(block, width),
            by_cols(width, block),
        ],
        out_shape=[
            shaped((rows, 2 * wide)),
            shaped((2 * wide, rows)),
            shaped((rows, 2 * wide)),
            shaped((rows, width)),
            shaped((rows, width)),
            shaped((width, rows)),
        ],
        scratch_shapes=[
            pltpu.VMEM((2, 2 * pairs, 128, 128), bf16),
            pltpu.VMEM((wide, width), bf16),
            pltpu.VMEM((wide, width), bf16),
            pltpu.SemaphoreType.DMA((5,)),
        ],
        compiler_params=params(),
        cost_estimate=cost(13),
        name="front_pass",
    )(order, tokens, *numers, *phis, incoming, gain, w_out, *pieces)


def feed_forward(pre):
    square = pre * pre
    swing = jnp.tanh(GELU_A * pre * (1.0 + GELU_B * square))
    half_up = 0.5 + 0.5 * swing
    slope = half_up + (0.5 * GELU_A) * pre * (1.0 - swing * swing) * (
        1.0 + (3.0 * GELU_B) * square
    )
    return (pre * half_up).astype(bf16), slope


def add_to(total, part):
    return part if total is None else total + part


def feed_kernel(tile, order, h_any, turned_any, d_any, *refs):
    ups, downs = refs[:4], refs[4:8]
    sums_out = (refs[8:10], refs[10:12])
    mixed_out, grad_out = refs[12:14]
    h, turned, d, up, down, mixed, grad_h, act, grad_pre, mixed_low, grad_low = refs[14:25]
    sums, sems, out_sems = refs[25:]
    step = pl.program_id(0)
    rows = h.shape[0]
    part = up.shape[2]
    quarter = part // 2
    block = 512
    blocks = rows // block

    def chunk_copies(at):
        run = pl.ds(block * at, block)
        return [
            pltpu.make_async_copy(h_any.at[run], h.at[run], sems.at[8 + 2 * at]),
            pltpu.make_async_copy(d_any.at[run], d.at[run], sems.at[9 + 2 * at]),
        ]

    def weight_copies(spot):
        copies = []
        for i in (2, 3) if spot == 0 else (0, 1):
            where = pl.multiple_of(order[2 + i] % 2 * quarter, 128)
            copies.append(
                pltpu.make_async_copy(
                    ups[i], up.at[spot, :, pl.ds(where, quarter)], sems.at[2 * i]
                )
            )
            where = pl.multiple_of(order[6 + i] % 2 * quarter, 16)
            copies.append(
                pltpu.make_async_copy(
                    downs[i].at[pl.ds(0, quarter)],
                    down.at[spot, pl.ds(where, quarter)],
                    sems.at[2 * i + 1],
                )
            )
        return copies

    def turned_copy():
        return pltpu.make_async_copy(turned_any, turned, sems.at[8 + 2 * blocks])

    def part_copies(at):
        run = pl.ds(block * at, block)
        return [
            pltpu.make_async_copy(mixed_low.at[run], mixed_out.at[run], out_sems.at[2 * at]),
            pltpu.make_async_copy(grad_low.at[run], grad_out.at[run], out_sems.at[2 * at + 1]),
        ]

    def sum_copies(spot):
        return [
            pltpu.make_async_copy(
                sums.at[spot, i], sums_out[spot][i], out_sems.at[2 * blocks + 2 * spot + i]
            )
            for i in range(2)
        ]

    @pl.when(step == 0)
    def _():
        for copy in weight_copies(0) + chunk_copies(0):
            copy.start()
        for at in range(1, blocks):
            for copy in chunk_copies(at):
                copy.start()
        turned_copy().start()
        for copy in weight_copies(1):
            copy.start()
        for copy in weight_copies(0):
            copy.wait()

    @pl.when(step == 1)
    def _():
        for copy in weight_copies(1):
            copy.wait()

    for at in range(blocks):
        run = slice(block * at, block * at + block)

        @pl.when(step == 0)
        def _(at=at):
            for copy in chunk_copies(at):
                copy.wait()

        mixed_part = grad_part = None
        for sub in range(0, part, tile):
            up_tile = up[step, :, sub : sub + tile]
            down_tile = down[step, sub : sub + tile, :]
            low, slope = feed_forward(dot(h[run, :], up_tile))
            grad = (dot_t(d[run, :], down_tile) * slope).astype(bf16)
            act[sub : sub + tile, run] = low.T
            grad_pre[run, sub : sub + tile] = grad
            mixed_part = add_to(mixed_part, dot(low, down_tile))
            grad_part = add_to(grad_part, dot_t(grad, up_tile))

        @pl.when(step == 0)
        def _(run=run, mixed_part=mixed_part, grad_part=grad_part):
            mixed[run, :] = mixed_part
            grad_h[run, :] = grad_part

        @pl.when(step == 1)
        def _(at=at, run=run, mixed_part=mixed_part, grad_part=grad_part):
            mixed_low[run, :] = (mixed[run, :] + mixed_part).astype(bf16)
            grad_low[run, :] = (grad_h[run, :] + grad_part).astype(bf16)
            for copy in part_copies(at):
                copy.start()

    @pl.when(step == 0)
    def _():
        turned_copy().wait()

    sums[step, 1] = dot(act[...], d[...]).astype(bf16)
    sums[step, 0] = dot(turned[...], grad_pre[...]).astype(bf16)

    @pl.when(step == 0)
    def _():
        for copy in sum_copies(0):
            copy.start()

    @pl.when(step == 1)
    def _():
        for copy in sum_copies(1):
            copy.start()
        for at in range(blocks):
            for copy in part_copies(at):
                copy.wait()
        for copy in sum_copies(0) + sum_copies(1):
            copy.wait()


def feed_pass(order, h, turned_h, d_out, ups, downs, tile):
    rows, width = h.shape
    part = 2 * ups[0].shape[1]
    square = (width, part)
    blocks = rows // 512
    return pl.pallas_call(
        functools.partial(feed_kernel, tile),
        grid=(2,),
        in_specs=[scalars] + [anywhere] * 11,
        out_specs=[anywhere] * 6,
        out_shape=[shaped(square), shaped((part, width))] * 2 + [shaped((rows, width))] * 2,
        scratch_shapes=[
            pltpu.VMEM((rows, width), bf16),
            pltpu.VMEM((width, rows), bf16),
            pltpu.VMEM((rows, width), bf16),
            pltpu.VMEM((2, width, part), bf16),
            pltpu.VMEM((2, part, width), bf16),
            pltpu.VMEM((rows, width), f32),
            pltpu.VMEM((rows, width), f32),
            pltpu.VMEM((part, rows), bf16),
            pltpu.VMEM((rows, part), bf16),
            pltpu.VMEM((rows, width), bf16),
            pltpu.VMEM((rows, width), bf16),
            pltpu.VMEM((2, 2, width, part), bf16),
            pltpu.SemaphoreType.DMA((9 + 2 * blocks,)),
            pltpu.SemaphoreType.DMA((4 + 2 * blocks,)),
        ],
        compiler_params=params(),
        cost_estimate=cost(32),
        name="feed_pass",
    )(order, h, turned_h, d_out, *ups, *downs)


def middle_kernel(pairs, tile, order, resid, h, d_out, *refs):
    mixed_part, grad_part, attended, inverse = refs[:4]
    phi = refs[4:6]
    gain, cross, wo_any, up_any, down_any = refs[6:11]
    pieces = refs[11:15]
    (
        act_out,
        pre_out,
        mixed_out,
        resid_out,
        gn_out,
        gd_out,
        turned_n_out,
        turned_d_out,
        state_out,
    ) = refs[15:24]
    state, wo_own, up, down, wo_oth, sems = refs[24:]
    step = pl.program_id(0)
    top = first_sublanes()
    wide = 128 * pairs
    units = up.shape[1]

    def early_copies():
        return [
            pltpu.make_async_copy(up_any, up, sems.at[0]),
            pltpu.make_async_copy(down_any, down, sems.at[1]),
        ]

    def late_copies():
        return [pltpu.make_async_copy(wo_any, wo_own, sems.at[2])] + quarter_copies(
            pieces, order, wo_oth, units // 4, wide // 4, sems, 3
        )

    @pl.when(step == 0)
    def _():
        for copy in early_copies() + late_copies():
            copy.start()
        state[...] = jnp.zeros_like(state)
        for copy in early_copies():
            copy.wait()

    h_two = h[...]
    d_low = d_out[...]
    mixed = grad_h = None
    for at in range(0, units, tile):
        low, slope = feed_forward(dot(h_two, up[:, at : at + tile]))
        grad_pre = (dot_t(d_low, down[at : at + tile, :]) * slope).astype(bf16)
        act_out[at : at + tile, :] = low.T
        for col in range(at, at + tile, 256):
            pre_out[col // 768, :, col % 768 : col % 768 + 256] = grad_pre[
                :, col - at : col - at + 256
            ]
        mixed = add_to(mixed, dot(low, down[at : at + tile, :]))
        grad_h = add_to(grad_h, dot_t(grad_pre, up[:, at : at + tile]))
    summed = resid[...].astype(f32)
    normed, spread = norm_parts(summed)
    mixed_out[...] = (summed + mixed_part[...].astype(f32) + mixed).astype(bf16)
    grad_h = grad_part[...].astype(f32) + grad_h
    grad_resid = (d_low.astype(f32) + norm_back(grad_h, normed, spread, gain[...])).astype(bf16)
    resid_out[...] = grad_resid

    @pl.when(step == 0)
    def _():
        for copy in late_copies():
            copy.wait()

    for half in range(2):
        grad_att = dot_t(grad_resid, (wo_own, wo_oth)[half][...]).astype(bf16).astype(f32)
        for p in range(pairs):
            at = wide * half + 128 * p
            own = grad_att[:, 128 * p : 128 * p + 128]
            scaled = own * inverse[:, at : at + 128].astype(f32)
            grad_n = scaled.astype(bf16)
            exact = attended[:, at : at + 128].astype(f32)
            grad_d = dot((scaled * exact).astype(bf16), cross[...]).astype(bf16)
            gn_out[:, at : at + 128] = grad_n
            gd_out[:, at : at + 128] = grad_d
            turned_n = grad_n.T
            turned_d = grad_d.T
            turned_n_out[at : at + 128, :] = turned_n
            turned_d_out[at : at + 128, :] = turned_d
            left = jnp.concatenate([turned_n, turned_d[0:16], turned_d[64:80]], axis=0)
            sums = dot(left, phi[half][:, 256 * p : 256 * p + 256])
            state[half, 128 * p : 128 * p + 128] += jnp.where(
                top, sums[:128, :128], sums[:128, 128:]
            )
            row = wide + 2 * p
            state[half, row : row + 1] += sums[144:145, :128]
            state[half, row + 1 : row + 2] += sums[128:129, 128:]

    @pl.when(step == pl.num_programs(0) - 1)
    def _():
        state_out[...] = state[...].astype(bf16)


def middle_pass(
    order, resid, h_two, d_out, parts, attended, inverse, phis, gain, cross, owns, pieces, packed, block, tile
):
    rows, width = resid.shape
    wide = owns[0].shape[0]
    pairs = wide // 128
    units = owns[1].shape[1]
    cols_out = [width, width, 2 * wide, 2 * wide]
    spots = units // 768
    return pl.pallas_call(
        functools.partial(middle_kernel, pairs, tile),
        grid=(rows // block,),
        in_specs=[scalars]
        + [by_rows(block, width)] * 5
        + [by_rows(block, 2 * wide)] * 4
        + [once(gain.shape), once(cross.shape)]
        + [anywhere] * 7,
        out_specs=[by_cols(units, block), pl.BlockSpec((spots, block, 768), lambda c: (0, c, 0))]
        + [by_rows(block, c) for c in cols_out]
        + [by_cols(2 * wide, block)] * 2
        + [once(packed)],
        out_shape=[shaped((units, rows)), shaped((spots, rows, 768))]
        + [shaped((rows, c)) for c in cols_out]
        + [shaped((2 * wide, rows))] * 2
        + [shaped(packed)],
        scratch_shapes=[
            pltpu.VMEM(packed, f32),
            pltpu.VMEM((wide, width), bf16),
            pltpu.VMEM((width, units), bf16),
            pltpu.VMEM((units, width), bf16),
            pltpu.VMEM((wide, width), bf16),
            pltpu.SemaphoreType.DMA((7,)),
        ],
        compiler_params=params(),
        cost_estimate=cost(35),
        name="middle_pass",
    )(order, resid, h_two, d_out, *parts, attended, inverse, *phis, gain, cross, *owns, *pieces)


def up_kernel(core, left, right, got, out):
    product = dot(left[...], right[0])
    mine = pl.program_id(0) == core[0]

    @pl.when(mine)
    def _():
        out[...] = (product + got[...].astype(f32)).astype(bf16)

    @pl.when(jnp.logical_not(mine))
    def _():
        out[...] = product.astype(bf16)


def up_pass(core, left, right, got):
    width, rows = left.shape
    count, _, part = right.shape
    return pl.pallas_call(
        up_kernel,
        grid_spec=pltpu.PrefetchScalarGridSpec(
            num_scalar_prefetch=1,
            grid=(count,),
            in_specs=[
                once((width, rows)),
                pl.BlockSpec((1, rows, part), lambda s, c: (s, 0, 0)),
                once((width, part)),
            ],
            out_specs=pl.BlockSpec((width, part), lambda s, c: (0, s)),
        ),
        out_shape=shaped((width, count * part)),
        compiler_params=params(),
        cost_estimate=cost(8),
        name="up_pass",
    )(core, left, right, got)


def down_kernel(core, left, right, own_left, oth_left, right_more, out, more_out):
    out[...] = dot(left[...], right[...]).astype(bf16)
    for side, rows in enumerate((own_left, oth_left)):
        more_out[side] = dot(rows[...], right_more[...]).astype(bf16)


def down_pass(half, left, right, left_more, right_more):
    rows, width = right.shape
    part = left.shape[0] // 2
    more = left_more.shape[0] // 4
    tile = width // 2
    cols = pl.BlockSpec((rows, tile), lambda s, half: (0, s))
    mine = lambda count, first: pl.BlockSpec((count, rows), lambda s, half: (first + half[0], 0))
    return pl.pallas_call(
        down_kernel,
        grid_spec=pltpu.PrefetchScalarGridSpec(
            num_scalar_prefetch=1,
            grid=(2,),
            in_specs=[mine(part, 0), cols, mine(more, 0), mine(more, 2), cols],
            out_specs=[
                pl.BlockSpec((part, tile), lambda s, half: (0, s)),
                pl.BlockSpec((2, more, tile), lambda s, half: (0, s, 0)),
            ],
        ),
        out_shape=[shaped((part, width)), shaped((2, 2 * more, tile))],
        compiler_params=params(),
        cost_estimate=cost(8),
        name="down_pass",
    )(half, left, right, left_more, left_more, right_more)


def back_kernel(pairs, at_pair, more, core, *refs):
    sides = (refs[:15], refs[15:30])
    incoming, later, ones, h_any = refs[30:34]
    earlier = refs[34 : 34 + more]
    grad_outs = refs[34 + more : 36 + more]
    send_out, keep_out, map_out = refs[36 + more : 39 + more]
    held, state, grads, maps, turned_h, sem = refs[39 + more :]
    step = pl.program_id(0)
    last = pl.num_programs(0) - 1
    first = first_lanes()
    top = first_sublanes()
    size = CHUNK
    inner = refs[2].shape[0] // CHUNK
    past = lax.broadcasted_iota(jnp.int32, (size, size), 0) >= lax.broadcasted_iota(
        jnp.int32, (size, size), 1
    )
    one = jnp.ones((1, 1), bf16)

    @pl.when(step == 0)
    def _():
        pltpu.make_async_copy(h_any, turned_h, sem.at[0]).start()
        maps[...] = jnp.zeros_like(maps)
        for side in range(2):
            for h_at in range(2):
                held[side, h_at] = read_state(incoming.at[side], at_pair, h_at, pairs)
                state[side, h_at] = read_state(later.at[side], at_pair, h_at, pairs)

    for sub in reversed(range(inner)):
        run = slice(CHUNK * sub, CHUNK * sub + CHUNK)
        for side in range(2):
            (q, k, v, turned_v, pq, turned_pq, pk, turned_pk) = sides[side][:8]
            (gn, gd, turned_n, turned_d, prefix, fq, fk) = sides[side][8:]
            grads_q, grads_k, grads_v = [], [], []
            for h_at in range(2):
                sel = first if h_at == 0 else jnp.logical_not(first)
                sel_top = top if h_at == 0 else jnp.logical_not(top)
                lanes = slice(128 * h_at, 128 * h_at + 128)
                padded_v = jnp.where(sel, v[run, :], one)
                padded_vt = jnp.where(sel_top, turned_v[:, run], one)
                padded_g = jnp.where(sel, gn[run, :], gd[run, :])
                padded_gt = jnp.where(sel_top, turned_n[:, run], turned_d[:, run])
                before = (prefix[sub, h_at].astype(f32) + held[side, h_at]).astype(bf16)
                after = state[side, h_at].astype(bf16)
                e = jnp.where(past, dot_t(padded_g, padded_v), 0.0).astype(bf16)
                s = jnp.where(past, dot(pq[run, lanes], turned_pk[lanes, run]), 0.0).astype(bf16)
                grads_q.append(dot(e, pk[run, lanes]) + dot(padded_g, before))
                grads_k.append(dot(turned_pq[lanes, run], e) + dot(after.T, padded_vt))
                grads_v.append(dot(padded_gt, s) + dot(after, turned_pk[lanes, run]))
                state[side, h_at] += dot(padded_gt, pq[run, lanes])

            grad_phi = jnp.concatenate(grads_q, axis=1)
            phi = pq[run, :].astype(f32)
            shared = dot((phi * grad_phi).astype(bf16), ones[...])
            grad_u = (phi * (grad_phi - shared)).astype(bf16)
            maps[side, 0] += dot(q[:, run], grad_u)
            grad_q = dot_t(grad_u, fq[0]).astype(bf16)

            grad_phi = jnp.concatenate(grads_k, axis=0).reshape(4, 64, size)
            phi = turned_pk[:, run].astype(f32).reshape(4, 64, size)
            shared = jnp.sum(phi * grad_phi, axis=1, keepdims=True)
            grad_u = (phi * (grad_phi - shared)).reshape(256, size).astype(bf16)
            maps[side, 1] += dot_t(k[:, run], grad_u)
            grad_k = dot(fk[0], grad_u).astype(bf16).T
            grad_v = jnp.where(top, grads_v[0], grads_v[1]).astype(bf16).T

            joined = jnp.concatenate([grad_q, grad_k, grad_v], axis=1)
            grad_outs[side][run, :] = joined
            where = pl.multiple_of(((last - step) * inner + sub) * size, size)
            grads[pl.ds(where, size), 384 * side : 384 * side + 384] = joined

    @pl.when(step == last)
    def _():
        pltpu.make_async_copy(h_any, turned_h, sem.at[0]).wait()
        product = dot(turned_h[...], grads[...]).astype(bf16)
        part = product.shape[0] // 2
        mine = core[0] == 0
        for side in range(2):
            cols = slice(384 * side, 384 * side + 384)
            low, high = product[:part, cols], product[part:, cols]
            send_out[side, 0:part] = jnp.where(mine, high, low)
            keep_out[side, 0:part] = jnp.where(mine, low, high)
            joins = [
                jnp.where(top, maps[side, i][:, :128], maps[side, i][:, 128:]) for i in range(2)
            ]
            turns = [pltpu.roll(j, 64, 1) for j in joins]
            own_map = jnp.where(first, joins[0] - turns[0], turns[1] - joins[1]).astype(bf16)
            map_out[side] = own_map
            if more:
                whole = jnp.concatenate([m[side] for m in earlier] + [own_map], axis=1)
                low, high = whole[:64], whole[64:]
                send_out[side, part : part + 64] = jnp.where(mine, high, low)
                keep_out[side, part : part + 64] = jnp.where(mine, low, high)
                send_out[side, part + 64 :] = jnp.zeros_like(low)
                keep_out[side, part + 64 :] = jnp.zeros_like(low)


def back_pass(at, core, sides, seconds, prefix, incoming, later, fq, fk, ones, turned_h, earlier):
    rows = sides[0][2].shape[0]
    pairs = fq[0].shape[0]
    width = turned_h.shape[0]
    count = rows // BLOCK
    here = lambda cols, spot: pl.BlockSpec((BLOCK, cols), lambda c, core: (count - 1 - c, spot))
    turned = lambda cols, spot: pl.BlockSpec((cols, BLOCK), lambda c, core: (spot, count - 1 - c))
    weights = pl.BlockSpec((1, 128, 256), lambda c, core: (at, 0, 0))
    states = pl.BlockSpec(
        (BLOCK // CHUNK, 2, 128, 128), lambda c, core: (count - 1 - c, at, 0, 0)
    )
    more = len(earlier)
    sums = (2, width // 2 + (128 if more else 0), 384)
    in_specs, args = [], []
    for side in range(2):
        both = pairs * side + at
        in_specs += [turned(128, at), turned(128, at), here(128, at), turned(128, at)]
        in_specs += [here(256, at), turned(256, at)] * 2
        in_specs += [here(128, both)] * 2 + [turned(128, both)] * 2
        in_specs += [states, weights, weights]
        args += [*sides[side], *seconds, prefix[side], fq[side], fk[side]]
    return pl.pallas_call(
        functools.partial(back_kernel, pairs, at, more),
        grid_spec=pltpu.PrefetchScalarGridSpec(
            num_scalar_prefetch=1,
            grid=(count,),
            in_specs=in_specs
            + [once(incoming.shape)] * 2
            + [once(ones.shape), anywhere]
            + [once((2, 128, 128))] * more,
            out_specs=[here(384, 0)] * 2 + [once(sums)] * 2 + [once((2, 128, 128))],
            scratch_shapes=[
                pltpu.VMEM((2, 2, 128, 128), f32),
                pltpu.VMEM((2, 2, 128, 128), f32),
                pltpu.VMEM((rows, 768), bf16),
                pltpu.VMEM((2, 2, 128, 256), f32),
                pltpu.VMEM((width, rows), bf16),
                pltpu.SemaphoreType.DMA((1,)),
            ],
        ),
        out_shape=[shaped((rows, 384))] * 2 + [shaped(sums)] * 2 + [shaped((2, 128, 128))],
        compiler_params=params(),
        cost_estimate=cost(17),
        name="back_pass",
    )(core, *args, incoming, later, ones, turned_h, *earlier)


def tokens_kernel(pairs, count, order, tokens, resid, gain, *refs):
    pieces = refs[: 1 + count]
    grads = refs[1 + count : 1 + count + 2 * pairs]
    out, w_own, w_oth, sems = refs[1 + count + 2 * pairs :]

    @pl.when(pl.program_id(0) == 0)
    def _():
        copies = qkv_copies(pieces[:1], order, (0, 1, 2), w_own, sems, 0)
        copies += qkv_copies(pieces[1:], order, (0, 1, 2), w_oth, sems, 3)
        run_copies(copies)

    normed, spread = norm_parts(tokens[...].astype(f32))
    total = None
    for half in range(2):
        joined = jnp.concatenate(
            [
                g[:, 128 * kind : 128 * kind + 128]
                for kind in range(3)
                for g in grads[half * pairs : half * pairs + pairs]
            ],
            axis=1,
        )
        part = dot_t(joined, (w_own, w_oth)[half][...])
        total = part if total is None else total + part
    back = norm_back(total, normed, spread, gain[...])
    out[...] = (resid[...].astype(f32) + back).astype(bf16)


def tokens_pass(order, tokens, resid, gain, w_own, pieces, grads, block, first, blocks, done=None):
    rows, width = tokens.shape
    pairs = len(grads) // 2
    cols = 3 * w_own.shape[2]
    count = len(pieces)
    cut = lambda cols: pl.BlockSpec((block, cols), lambda c: (first + c, 0))
    operands = [order, tokens, resid, gain, w_own, *pieces, *grads]
    more = [] if done is None else [done]

    def kernel(*refs):
        refs = list(refs)
        if more:
            del refs[len(operands)]
        tokens_kernel(pairs, count, *refs)

    return pl.pallas_call(
        kernel,
        grid=(blocks,),
        in_specs=[scalars]
        + [cut(width)] * 2
        + [once(gain.shape)]
        + [anywhere] * (1 + count)
        + [cut(384)] * len(grads)
        + [anywhere] * len(more),
        out_specs=cut(width),
        out_shape=shaped((rows, width)),
        input_output_aliases={len(operands): 0} if more else {},
        scratch_shapes=[
            pltpu.VMEM((width, cols), bf16),
            pltpu.VMEM((width, cols), bf16),
            pltpu.SemaphoreType.DMA((3 + 3 * count,)),
        ],
        compiler_params=params(),
        cost_estimate=cost(8),
        name="tokens_pass",
    )(*operands, *more)


def cross_to(value, axis, flip):
    count = lax.axis_size(axis)
    return lax.ppermute(value, axis, [(i, i ^ flip) for i in range(count)])


def swap(value, axis, bit):
    return cross_to(value, axis, 1 << bit)


def bit_of(axis, bit):
    return (lax.axis_index(axis) >> bit) & 1


def bits_of(axis):
    return lax.axis_size(axis).bit_length() - 1


def ordered(bit, mine, theirs, axis=0):
    return jnp.where(
        bit == 0,
        jnp.concatenate([mine, theirs], axis),
        jnp.concatenate([theirs, mine], axis),
    )


def add_low(*parts):
    total = parts[0].astype(f32)
    for part in parts[1:]:
        total = total + part.astype(f32)
    return total.astype(bf16)


class Flow:
    def __init__(self):
        self.ready = {}
        self.steps = {}
        self.done = {}

    def start(self, name, steps):
        self.steps[name] = steps
        self.ready[name] = next(steps)

    def slot(self, names, others):
        names = [n for n in names if n in self.steps]
        tied, others = lax.optimization_barrier(([self.ready[n] for n in names], others))
        for name, value in zip(names, tied):
            self.move(name, value)
        return others

    def move(self, name, value):
        try:
            self.ready[name] = self.steps[name].send(value)
        except StopIteration as end:
            self.done[name] = end.value
            del self.steps[name], self.ready[name]

    def finish(self, names):
        for name in names:
            while name in self.steps:
                self.move(name, self.ready[name])


def fetch_halves(weight, axis):
    count = weight.shape[axis] // 2
    part = yield lax.dynamic_slice_in_dim(weight, bit_of("ctx", 0) * count, count, axis)
    part = yield swap(part, "heads", 0)
    return [part, swap(part, "ctx", 0)]


def fetch_quarters(weights, across, axis):
    place = 2 * bit_of("ctx", 0) + bit_of(*across)
    parts = []
    for weight in weights:
        count = weight.shape[axis] // 4
        parts.append(lax.dynamic_slice_in_dim(weight, place * count, count, axis))
    part = yield jnp.concatenate(parts, axis)
    part = yield swap(part, "heads", 0)
    part, second, third = yield part, swap(part, *across), swap(part, "ctx", 0)
    return [part, second, third, swap(second, "ctx", 0)]


def fetch_order():
    core = bit_of("ctx", 0)
    order = [core, 1 - core]
    for across in (bit_of("ctx", 1), bit_of("batch", 0)):
        order += [
            2 * core + across,
            2 * core + 1 - across,
            2 - 2 * core + across,
            3 - 2 * core - across,
        ]
    return jnp.stack(order).astype(jnp.int32)


def reduce_sums(send, keep, ways, spread=False):
    send = yield send
    got = swap(send, "ctx", 0)
    left, oth = add_low(keep[0], got[0]), add_low(keep[1], got[1])
    return (yield from reduce_tail(left, [swap(oth, "heads", 0)], ways, spread))


def send_over(send, keep):
    send = yield send
    total = yield add_low(keep, swap(send, "ctx", 0))
    return (yield swap(total, "heads", 0))


def send_over_late(send, keep):
    send = yield send
    got = swap(send, "ctx", 0)
    count = keep.shape[0] // 2
    first, rest = yield [add_low(keep[i], got[i]) for i in (slice(0, count), slice(count, None))]
    first, rest = yield swap(first, "heads", 0), rest
    rest = yield rest
    return jnp.concatenate([first, (yield swap(rest, "heads", 0))])


def reduce_tail(left, rights, ways, spread=False):
    stages = [("ctx", b, 1) for b in range(1, bits_of("ctx"))]
    count = bits_of("batch")
    along = [("batch", b, min(ways, count - b)) for b in range(0, count, ways)]
    if not spread:
        stages += along
    for axis, low_bit, bits in stages:
        ways = 1 << bits
        place = (lax.axis_index(axis) >> low_bit) & (ways - 1)
        count = left.shape[0] // ways
        cut = lambda at: add_low(
            *[lax.dynamic_slice_in_dim(a, at * count, count, 0) for a in (left, *rights)]
        )
        sends = [cut(place ^ flip) for flip in range(1, ways)]
        left, sends = yield (cut(place), sends)
        rights = [cross_to(s, axis, (i + 1) << low_bit) for i, s in enumerate(sends)]
    whole = add_low(left, *rights)
    for axis, low_bit, bits in along if spread else []:
        whole = yield whole
        got = [cross_to(whole, axis, flip << low_bit) for flip in range(1, 1 << bits)]
        whole = add_low(whole, *got)
    for axis, low_bit, bits in reversed(stages):
        whole = yield whole
        parts = [whole] + [cross_to(whole, axis, flip << low_bit) for flip in range(1, 1 << bits)]
        for b in range(bits):
            bit = bit_of(axis, low_bit + b)
            parts = [ordered(bit, parts[i], parts[i + 1]) for i in range(0, len(parts), 2)]
        whole = parts[0]
    whole = yield whole
    return (yield (whole, swap(whole, "ctx", 0)))


def send_once(value, axis, bit):
    value = yield value
    return swap(value, axis, bit)


def scan_runs(total, boundary, rows, backward):
    place, side = lax.axis_index("ctx"), lax.axis_index("heads")
    second = lambda spot, half: (2 * spot + half) * rows >= boundary
    end = 0 if backward else 1
    total = yield total
    got = jnp.flip(swap(total, "heads", 0).astype(f32), 0)
    total = total.astype(f32)
    mine = second(place, side)
    joins = second(place, 0) == second(place, 1)
    received = jnp.where(jnp.logical_and(side == end, joins), got, 0.0)
    near = jnp.where(side == end, total, got)
    far = jnp.where(side == end, got, total)
    low = yield (near + jnp.where(joins, far, 0.0)).astype(bf16)
    for flip in range(1, lax.axis_size("ctx")):
        got = cross_to(low, "ctx", flip).astype(f32)
        spot = place ^ flip
        ahead = spot > place if backward else spot < place
        takes = jnp.logical_and(ahead, second(spot, end) == mine)
        received = received + jnp.where(takes, got, 0.0)
    received = yield received
    return received


def shards(tokens, lengths, gain_one, w_qkv, f_query, f_key, w_out, gain_two, w_up, w_down, d_out):
    rows, width = tokens.shape
    heads, size, _ = f_query.shape
    pairs = heads // 2
    wide = heads * size
    units = w_up.shape[1]
    assert size == 64 and lax.axis_size("heads") == 2 and 1536 % rows == 0
    boundary = lengths[0, 0]
    place = bit_of("ctx", 0)
    order = fetch_order()
    gain_one_row = gain_one.reshape(1, width)
    gain_two_row = gain_two.reshape(1, width)

    spots = np.arange(256) // 64
    ones = jnp.asarray(spots[:, None] == spots[None, :], bf16)
    cross = jnp.asarray((spots[:128, None] != spots[None, :128]) * (-1.0 / 64.0), bf16)
    signs = jnp.asarray(np.kron(np.array([[1, -1, 1, -1]]), np.eye(64)), bf16)

    flow = Flow()
    slot = flow.slot
    qkv_own = jnp.transpose(w_qkv, (1, 0, 2))
    maps_own = jnp.stack([f_query, f_key])
    flow.start("maps", send_once(maps_own, "heads", 0))
    flow.start("qkv", fetch_halves(qkv_own, 1))
    flow.start("up", fetch_quarters([w_up], ("ctx", 1), 1))
    flow.start("down", fetch_quarters([w_down, w_out], ("batch", 0), 0))
    (tokens,) = slot(["maps", "qkv"], (tokens,))

    h_one, turned_h = norm_one(tokens, gain_one_row)
    maps_oth = flow.done["maps"]
    keys = [key_pass(h_one, [qkv_own], order, maps_own, signs, [])]
    (keys[0][6], order, maps_oth, gain_two_row) = slot(
        ["qkv", "up", "down"], (keys[0][6], order, maps_oth, gain_two_row)
    )
    qkv_oth = flow.done["qkv"]
    keys.append(key_pass(h_one, qkv_oth, order, maps_oth, signs, [keys[0][6]]))
    flow.start("scan", scan_runs(keys[1][6], boundary, rows, False))
    (keys[1][1], order) = slot(["scan", "up"], (keys[1][1], order))
    queries = []
    for at, weights in enumerate(([qkv_own], qkv_oth)):
        queries.append(
            query_pass(
                h_one,
                weights,
                order,
                keys[at][4],
                keys[at][1],
                keys[at][5],
                (maps_own, maps_oth)[at],
                signs,
            )
        )
        if at == 0:
            (queries[0][0], order) = slot(["scan", "up", "down"], (queries[0][0], order))
    (queries[1][0], order) = slot(["scan", "down"], (queries[1][0], order))
    ups, downs, incoming = (flow.done[n] for n in ("up", "down", "scan"))
    q, phi_q, turned_pq, numer, _, fq = zip(*queries)
    k, v, turned_v, phi_k, turned_pk, prefix, _, _, fk = zip(*keys)

    attended, turned_a, inverse, resid, h_two, turned_two = front_pass(
        order, tokens, numer, phi_q, incoming, gain_two_row, w_out, downs, 512
    )
    send_up, send_down, keep_up, keep_down, *parts = feed_pass(
        order, h_two, turned_two, d_out, ups, downs, 768
    )
    flow.start("oth_up", send_over(send_up, keep_up))
    flow.start("oth_down", send_over_late(send_down, keep_down))
    slot(["oth_up", "oth_down"], ())
    (order,) = slot(["oth_up", "oth_down"], (order,))
    (
        act,
        grad_pre,
        mixed,
        grad_resid,
        gn,
        gd,
        turned_n,
        turned_gd,
        grad_totals,
    ) = middle_pass(
        order,
        resid,
        h_two,
        d_out,
        parts,
        attended,
        inverse,
        phi_q,
        gain_two_row,
        cross,
        (w_out, w_up, w_down),
        downs,
        incoming.shape,
        256,
        768,
    )
    flow.start("later", scan_runs(grad_totals, boundary, rows, True))
    near, away = place.reshape(1), (1 - place).reshape(1)
    (near, grad_pre) = slot(["later", "oth_up", "oth_down"], (near, grad_pre))
    up_sum = up_pass(near, turned_two, grad_pre, flow.done["oth_up"])
    (away, act, up_sum) = slot(["later", "oth_down"], (away, act, up_sum))
    everyone = ("batch", "ctx")
    up_sum = lax.psum_scatter(up_sum, everyone, scatter_dimension=0, tiled=True)
    send, out_send = down_pass(away, act, d_out, turned_a, grad_resid)
    flow.start("own_down", send_once(send, "ctx", 0))
    (near, out_send) = slot(["later", "own_down", "oth_down"], (near, out_send))
    keep_down, out_keep = down_pass(near, act, d_out, turned_a, grad_resid)
    got, right = flow.done["own_down"], flow.done["oth_down"]
    flow.start("down_sum", reduce_tail(keep_down, [got, right], 1))
    (near, out_keep) = slot(["down_sum"], (near, out_keep))
    later = flow.done["later"]

    grads, maps, sends, keeps = [[], []], [], [], []
    feeds = ["down_sum"]
    plan = [feeds, ["qkv0"] + feeds, ["qkv1", "qkv0"] + feeds]
    names = (q, k, v, turned_v, phi_q, turned_pq, phi_k, turned_pk)
    for at in range(pairs):
        own, oth, send, keep, map_part = back_pass(
            at,
            near,
            [[a[side] for a in names] for side in range(2)],
            [gn, gd, turned_n, turned_gd],
            prefix,
            incoming,
            later,
            fq,
            fk,
            ones,
            turned_h,
            maps if at == pairs - 1 else [],
        )
        grads[0].append(own)
        grads[1].append(oth)
        maps.append(map_part)
        sends.append(send)
        keeps.append(keep)
        if at == pairs - 2:
            flow.start(
                "qkv0",
                reduce_sums(
                    jnp.concatenate(sends + [out_send], axis=1),
                    jnp.concatenate(keeps + [out_keep], axis=1),
                    2,
                ),
            )
        if at == pairs - 1:
            flow.start("qkv1", reduce_sums(send, keep, 2))
        tied = (own, near) if at < pairs - 1 else (own, near, up_sum)
        (grads[0][at], near, *rest) = slot(plan[at], tied)
        if rest:
            (up_sum,) = rest
            up_sum = lax.all_gather(up_sum, everyone, axis=0, tiled=True)
    order = order + 0 * near[0]
    tokens_args = (tokens, grad_resid, gain_one_row, qkv_own, qkv_oth, grads[0] + grads[1], 256)
    blocks = rows // 256
    early = blocks // 2
    grad_tokens = tokens_pass(order, *tokens_args, 0, early)
    tail = ["qkv1", "qkv0"]
    (grad_tokens, order) = slot(tail + feeds, (grad_tokens, order))
    grad_tokens = tokens_pass(order, *tokens_args, early, blocks - early, grad_tokens)
    (grad_tokens,) = slot(tail + feeds, (grad_tokens,))
    (up_sum,) = slot(tail + feeds, (up_sum,))
    grad_up = up_sum.astype(f32)
    gain_two_part = jnp.sum(grad_up * w_up.astype(f32), axis=1)
    (grad_up, gain_two_part) = slot(tail + feeds, (grad_up, gain_two_part))
    flow.finish(feeds)
    grad_down = ordered(place, *flow.done["down_sum"]).astype(f32)
    (grad_down,) = slot(tail, (grad_down,))
    flow.finish(list(flow.steps))
    part = width // 2
    (mine, theirs), (mine_last, theirs_last) = flow.done["qkv0"], flow.done["qkv1"]
    join = lambda mine, theirs: ordered(place, mine, theirs)
    beside = lambda a: jnp.concatenate([a[: wide // 2], a[wide // 2 :]], axis=1)
    more = part * (pairs - 1)
    grad_out = join(beside(mine[more:]), beside(theirs[more:])).astype(f32)
    parts = [
        join(mine[part * at : part * at + part], theirs[part * at : part * at + part])
        for at in range(pairs - 1)
    ]
    parts.append(join(mine_last[:part], theirs_last[:part]))
    grad_qkv = jnp.stack(
        [
            jnp.concatenate([p[:, 128 * kind : 128 * kind + 128] for p in parts], axis=1)
            for kind in range(3)
        ]
    )
    grad_qkv = grad_qkv.astype(f32)
    gain_one_part = jnp.sum(grad_qkv * qkv_own.astype(f32), axis=(0, 2))
    gains = jnp.stack([gain_one_part, gain_two_part])
    gains = (gains + swap(gains, "heads", 0)) / jnp.stack([gain_one, gain_two])
    grad_qkv = jnp.transpose(grad_qkv, (1, 0, 2))
    maps_sum = join(mine_last[part : part + 64], theirs_last[part : part + 64]).astype(f32)
    maps_sum = maps_sum.reshape(2, 64, pairs, 2, 64).transpose(3, 2, 0, 1, 4)
    grad_maps = maps_sum.reshape(2, heads, size, size)
    return (
        mixed,
        grad_tokens,
        gains[0],
        grad_qkv,
        grad_maps[0],
        grad_maps[1],
        grad_out,
        gains[1],
        grad_up,
        grad_down,
    )


def solution(mesh):
    in_specs = (
        P(("batch", "ctx", "heads"), None),
        P("batch", None),
        P(),
        P(None, None, "heads"),
        P("heads", None, None),
        P("heads", None, None),
        P("heads", None),
        P(),
        P(None, "heads"),
        P("heads", None),
        P(("batch", "ctx", "heads"), None),
    )
    out_specs = (
        P(("batch", "ctx", "heads"), None),
        P(("batch", "ctx", "heads"), None),
        P(),
        P(None, None, "heads"),
        P("heads", None, None),
        P("heads", None, None),
        P("heads", None),
        P(),
        P(None, "heads"),
        P("heads", None),
    )
    return jax.shard_map(shards, mesh=mesh, in_specs=in_specs, out_specs=out_specs, check_vma=False)
```

```python
import functools

import jax
import jax.numpy as jnp
import numpy as np
from jax import lax
from jax.experimental import pallas as pl
from jax.experimental.pallas import tpu as pltpu
from jax.sharding import PartitionSpec as P

epsilon = 1e-05
f32 = jnp.float32
bf16 = jnp.bfloat16
CHUNK = 256
BLOCK = 512
VMEM_LIMIT = 60 * 1024 * 1024
GELU_A = 0.7978845608028654
GELU_B = 0.044715


def dot(left, right):
    return lax.dot_general(left, right, (((1,), (0,)), ((), ())), preferred_element_type=f32)


def dot_t(left, right):
    return lax.dot_general(left, right, (((1,), (1,)), ((), ())), preferred_element_type=f32)


def params():
    return pltpu.CompilerParams(
        dimension_semantics=("arbitrary",), vmem_limit_bytes=VMEM_LIMIT
    )


def cost(micros):
    return pl.CostEstimate(flops=0, bytes_accessed=micros * 3_600_000, transcendentals=0)


def shaped(shape, kind=bf16):
    return jax.ShapeDtypeStruct(shape, kind)


def once(shape):
    zeros = (0,) * len(shape)
    return pl.BlockSpec(shape, lambda *_: zeros, pipeline_mode=pl.Buffered(1))


def by_rows(count, cols, at=0):
    return pl.BlockSpec((count, cols), lambda c, *_: (c, at))


def by_cols(rows, count, at=0):
    return pl.BlockSpec((rows, count), lambda c, *_: (at, c))


def map_block(maps, kind):
    return pl.BlockSpec(
        (1, *maps.shape[1:]), lambda *_: (kind, 0, 0, 0), pipeline_mode=pl.Buffered(1)
    )


anywhere = pl.BlockSpec(memory_space=pl.ANY)
scalars = pl.BlockSpec(memory_space=pltpu.SMEM)


def first_lanes():
    return lax.broadcasted_iota(jnp.int32, (1, 128), 1) < 64


def first_sublanes():
    return lax.broadcasted_iota(jnp.int32, (128, 1), 0) < 64


def build_maps(f, signs, turned_out, plain_out, pairs):
    top = first_sublanes()
    left = lax.broadcasted_iota(jnp.int32, (1, 256), 1) < 128
    for p in range(pairs):
        both = dot(f[0, 2 * p : 2 * p + 2].reshape(128, 64), signs[...])
        plain = jnp.where(top == left, both, 0.0)
        plain_out[p] = plain.astype(bf16)
        turned_out[p] = plain.T.astype(bf16)


def soft_rows(logits):
    count, size = logits.shape
    groups = logits.reshape(count // 64, 64, size)
    grown = jnp.exp(groups - jnp.max(groups, axis=1, keepdims=True))
    soft = grown * (1.0 / jnp.sum(grown, axis=1, keepdims=True))
    return soft.reshape(count, size)


def norm_parts(values):
    centred = values - jnp.mean(values, axis=1, keepdims=True)
    spread = lax.rsqrt(jnp.mean(centred * centred, axis=1, keepdims=True) + epsilon)
    return centred * spread, spread


def norm_back(gradient, normed, spread, gain):
    scaled = gradient * gain
    return spread * (
        scaled
        - jnp.mean(scaled, axis=1, keepdims=True)
        - normed * jnp.mean(scaled * normed, axis=1, keepdims=True)
    )


def run_copies(copies):
    for copy in copies:
        copy.start()
    for copy in copies:
        copy.wait()


def qkv_copies(pieces, order, kinds, target, sems, first_sem):
    rows = pieces[0].shape[1]
    copies = []
    for i, piece in enumerate(pieces):
        where = 0 if len(pieces) == 1 else pl.multiple_of(order[i] * rows, 16)
        for at, kind in enumerate(kinds):
            wide = piece.shape[2]
            copies.append(
                pltpu.make_async_copy(
                    piece.at[kind],
                    target.at[pl.ds(where, rows), pl.ds(at * wide, wide)],
                    sems.at[first_sem + len(copies)],
                )
            )
    return copies


def norm_kernel(tokens, gain, h_out, turned_out):
    normed, _ = norm_parts(tokens[...].astype(f32))
    low = (normed * gain[...]).astype(bf16)
    h_out[...] = low
    turned_out[...] = low.T


def norm_one(tokens, gain):
    rows, width = tokens.shape
    return pl.pallas_call(
        norm_kernel,
        grid=(rows // BLOCK,),
        in_specs=[by_rows(BLOCK, width), once((1, width))],
        out_specs=[by_rows(BLOCK, width), by_cols(width, BLOCK)],
        out_shape=[shaped((rows, width)), shaped((width, rows))],
        compiler_params=params(),
        cost_estimate=cost(5),
        name="norm_one",
    )(tokens, gain)


def write_state(state, state_out, pairs):
    top = first_sublanes()
    sums = []
    for p in range(pairs):
        state_out[128 * p : 128 * p + 128] = jnp.where(
            top, state[2 * p], state[2 * p + 1]
        ).astype(bf16)
        sums.append(state[2 * p, 64:65, :])
        sums.append(state[2 * p + 1, 0:1, :])
    tail = state_out.shape[0] - 128 * pairs
    sums.append(jnp.zeros((tail - 2 * pairs, 128), f32))
    state_out[128 * pairs :] = jnp.concatenate(sums, axis=0).astype(bf16)


def read_state(packed, p, h_at, pairs):
    row = 128 * pairs + 2 * p + h_at
    whole = packed[128 * p : 128 * p + 128, :]
    sums = packed[row : row + 1, :]
    sel = first_sublanes() if h_at == 0 else jnp.logical_not(first_sublanes())
    return jnp.where(sel, whole, sums)


def keys_kernel(pairs, count, more, order, h, f, signs, *refs):
    earlier, refs = refs[:more], refs[more:]
    pieces = refs[:count]
    (k_out, v_out, turned_v_out, phi_out, turned_phi_out, prefix_out, state_out) = refs[count : count + 7]
    fext, plain_out, w_kv, state, sems = refs[count + 7 :]
    step = pl.program_id(0)
    wide = 128 * pairs

    @pl.when(step == 0)
    def _():
        copies = qkv_copies(pieces, order, (1, 2), w_kv, sems, 0)
        for copy in copies:
            copy.start()
        build_maps(f, signs, fext, plain_out, pairs)
        state[...] = jnp.zeros_like(state)
        for copy in copies:
            copy.wait()

    kv_all = dot(h[...], w_kv[...]).astype(bf16)
    turned_k_all = kv_all[:, :wide].T
    turned_v_all = kv_all[:, wide:].T
    k_out[...] = turned_k_all
    v_out[...] = kv_all[:, wide:]
    turned_v_out[...] = turned_v_all
    top = first_sublanes()
    one = jnp.ones((1, 1), bf16)
    for sub in range(h.shape[0] // CHUNK):
        run = slice(CHUNK * sub, CHUNK * sub + CHUNK)
        turned_k, turned_v = turned_k_all[:, run], turned_v_all[:, run]
        prefix_out[sub] = state[...].astype(bf16)
        for p in range(pairs):
            turned_phi = soft_rows(dot(fext[p], turned_k[128 * p : 128 * p + 128])).astype(bf16)
            phi = turned_phi.T
            turned_phi_out[256 * p : 256 * p + 256, run] = turned_phi
            phi_out[run, 256 * p : 256 * p + 256] = phi
            values = turned_v[128 * p : 128 * p + 128]
            for h_at in range(2):
                sel = top if h_at == 0 else jnp.logical_not(top)
                padded = jnp.where(sel, values, one)
                state[2 * p + h_at] += dot(padded, phi[:, 128 * h_at : 128 * h_at + 128])

    @pl.when(step == pl.num_programs(0) - 1)
    def _():
        state_out[0] = earlier[0][1] if more else jnp.zeros_like(state_out[0])
        write_state(state, state_out.at[1], pairs)


def key_pass(h, weights, order, maps, signs, earlier):
    rows, width = h.shape
    pairs = maps.shape[1] // 2
    wide = 128 * pairs
    count = rows // CHUNK
    packed = wide + 16
    return list(
        pl.pallas_call(
            functools.partial(keys_kernel, pairs, len(weights), len(earlier)),
            grid=(rows // BLOCK,),
            in_specs=[
                scalars,
                by_rows(BLOCK, width),
                map_block(maps, 1),
                once(signs.shape),
            ]
            + [once((2, packed, 128))] * len(earlier)
            + [anywhere] * len(weights),
            out_specs=[
                by_cols(wide, BLOCK),
                by_rows(BLOCK, wide),
                by_cols(wide, BLOCK),
                by_rows(BLOCK, 2 * wide),
                by_cols(2 * wide, BLOCK),
                pl.BlockSpec((BLOCK // CHUNK, 2 * pairs, 128, 128), lambda c: (c, 0, 0, 0)),
                once((2, packed, 128)),
                once((pairs, 256, 128)),
                once((pairs, 128, 256)),
            ],
            out_shape=[
                shaped((wide, rows)),
                shaped((rows, wide)),
                shaped((wide, rows)),
                shaped((rows, 2 * wide)),
                shaped((2 * wide, rows)),
                shaped((count, 2 * pairs, 128, 128)),
                shaped((2, packed, 128)),
                shaped((pairs, 256, 128)),
                shaped((pairs, 128, 256)),
            ],
            scratch_shapes=[
                pltpu.VMEM((width, 2 * wide), bf16),
                pltpu.VMEM((2 * pairs, 128, 128), f32),
                pltpu.SemaphoreType.DMA((2 * len(weights),)),
            ],
            compiler_params=params(),
            cost_estimate=cost(10),
            name="key_pass",
        )(order, h, maps, signs, *earlier, *weights)
    )


def query_kernel(pairs, count, order, h, turned_k_phi, v, prefix, f, signs, *refs):
    pieces = refs[:count]
    q_out, phi_out, turned_phi_out, numer_out, fext, plain_out, w_q, sems = refs[count:]

    @pl.when(pl.program_id(0) == 0)
    def _():
        copies = qkv_copies(pieces, order, (0,), w_q, sems, 0)
        for copy in copies:
            copy.start()
        build_maps(f, signs, fext, plain_out, pairs)
        for copy in copies:
            copy.wait()

    turned_q_all = dot(h[...], w_q[...]).astype(bf16).T
    q_out[...] = turned_q_all
    first = first_lanes()
    one = jnp.ones((1, 1), bf16)
    size = CHUNK
    past = lax.broadcasted_iota(jnp.int32, (size, size), 0) >= lax.broadcasted_iota(
        jnp.int32, (size, size), 1
    )
    for sub in range(h.shape[0] // CHUNK):
        run = slice(CHUNK * sub, CHUNK * sub + CHUNK)
        turned_q = turned_q_all[:, run]
        for p in range(pairs):
            turned_phi = soft_rows(dot(fext[p], turned_q[128 * p : 128 * p + 128])).astype(bf16)
            phi = turned_phi.T
            turned_phi_out[256 * p : 256 * p + 256, run] = turned_phi
            phi_out[run, 256 * p : 256 * p + 256] = phi
            v_two = v[run, 128 * p : 128 * p + 128]
            for h_at in range(2):
                at = 256 * p + 128 * h_at
                sel = first if h_at == 0 else jnp.logical_not(first)
                padded = jnp.where(sel, v_two, one)
                phi_q = phi[:, 128 * h_at : 128 * h_at + 128]
                scores = dot(phi_q, turned_k_phi[at : at + 128, run])
                scores = jnp.where(past, scores, 0.0).astype(bf16)
                numer_out[run, at : at + 128] = (
                    dot(scores, padded) + dot_t(phi_q, prefix[sub, 2 * p + h_at])
                ).astype(bf16)


def query_pass(h, weights, order, turned_k_phi, v, prefix, maps, signs):
    rows, width = h.shape
    pairs = maps.shape[1] // 2
    wide = 128 * pairs
    return list(
        pl.pallas_call(
            functools.partial(query_kernel, pairs, len(weights)),
            grid=(rows // BLOCK,),
            in_specs=[
                scalars,
                by_rows(BLOCK, width),
                by_cols(2 * wide, BLOCK),
                by_rows(BLOCK, wide),
                pl.BlockSpec((BLOCK // CHUNK, 2 * pairs, 128, 128), lambda c: (c, 0, 0, 0)),
                map_block(maps, 0),
                once(signs.shape),
            ]
            + [anywhere] * len(weights),
            out_specs=[
                by_cols(wide, BLOCK),
                by_rows(BLOCK, 2 * wide),
                by_cols(2 * wide, BLOCK),
                by_rows(BLOCK, 2 * wide),
                once((pairs, 256, 128)),
                once((pairs, 128, 256)),
            ],
            out_shape=[
                shaped((wide, rows)),
                shaped((rows, 2 * wide)),
                shaped((2 * wide, rows)),
                shaped((rows, 2 * wide)),
                shaped((pairs, 256, 128)),
                shaped((pairs, 128, 256)),
            ],
            scratch_shapes=[
                pltpu.VMEM((width, wide), bf16),
                pltpu.SemaphoreType.DMA((len(weights),)),
            ],
            compiler_params=params(),
            cost_estimate=cost(15),
            name="query_pass",
        )(order, h, turned_k_phi, v, prefix, maps, signs, *weights)
    )


def quarter_copies(pieces, order, target, first_row, rows, sems, first_sem):
    copies = []
    for i, piece in enumerate(pieces):
        where = pl.multiple_of(order[6 + i] * rows, 16)
        copies.append(
            pltpu.make_async_copy(
                piece.at[pl.ds(first_row, rows)],
                target.at[pl.ds(where, rows)],
                sems.at[first_sem + i],
            )
        )
    return copies


def front_kernel(pairs, units, order, tokens, *refs):
    numer, phi = refs[:2], refs[2:4]
    incoming, gain, wo_any = refs[4:7]
    pieces = refs[7:11]
    attended_out, turned_a_out, inverse_out, resid_out, h_out, turned_h_out = refs[11:17]
    held, wo_own, wo_oth, sems = refs[17:]
    first = first_lanes()
    wide = 128 * pairs
    start = pl.program_id(0) == 0

    def weight_copies():
        return [pltpu.make_async_copy(wo_any, wo_own, sems.at[0])] + quarter_copies(
            pieces, order, wo_oth, units // 4, wide // 4, sems, 1
        )

    @pl.when(start)
    def _():
        for copy in weight_copies():
            copy.start()
        for half in range(2):
            for p in range(pairs):
                for h_at in range(2):
                    held[half, 2 * p + h_at] = read_state(
                        incoming.at[half], p, h_at, pairs
                    ).astype(bf16)

    for half in range(2):
        for p in range(pairs):
            sums = []
            for h_at in range(2):
                at = 256 * p + 128 * h_at
                sums.append(
                    numer[half][:, at : at + 128].astype(f32)
                    + dot_t(phi[half][:, at : at + 128], held[half, 2 * p + h_at])
                )
            numerator = jnp.where(first, sums[0], sums[1])
            swapped = 1.0 / jnp.where(first, sums[1], sums[0])
            inv = pltpu.roll(swapped, 64, 1)
            attended = (numerator * inv).astype(bf16)
            at = wide * half + 128 * p
            inverse_out[:, at : at + 128] = inv.astype(bf16)
            attended_out[:, at : at + 128] = attended
            turned_a_out[at : at + 128, :] = attended.T

    @pl.when(start)
    def _():
        for copy in weight_copies():
            copy.wait()

    resid = (
        tokens[...].astype(f32)
        + dot(attended_out[:, :wide], wo_own[...])
        + dot(attended_out[:, wide:], wo_oth[...])
    )
    resid_out[...] = resid.astype(bf16)
    normed, _ = norm_parts(resid)
    h_two = (normed * gain[...]).astype(bf16)
    h_out[...] = h_two
    turned_h_out[...] = h_two.T


def front_pass(order, tokens, numers, phis, incoming, gain, w_out, pieces, block):
    rows, width = tokens.shape
    wide = w_out.shape[0]
    pairs = wide // 128
    units = 4 * pieces[0].shape[0] - wide
    return pl.pallas_call(
        functools.partial(front_kernel, pairs, units),
        grid=(rows // block,),
        in_specs=[scalars, by_rows(block, width)]
        + [by_rows(block, 2 * wide)] * 4
        + [once(incoming.shape), once(gain.shape)]
        + [anywhere] * 5,
        out_specs=[
            by_rows(block, 2 * wide),
            by_cols(2 * wide, block),
            by_rows(block, 2 * wide),
            by_rows(block, width),
            by_rows(block, width),
            by_cols(width, block),
        ],
        out_shape=[
            shaped((rows, 2 * wide)),
            shaped((2 * wide, rows)),
            shaped((rows, 2 * wide)),
            shaped((rows, width)),
            shaped((rows, width)),
            shaped((width, rows)),
        ],
        scratch_shapes=[
            pltpu.VMEM((2, 2 * pairs, 128, 128), bf16),
            pltpu.VMEM((wide, width), bf16),
            pltpu.VMEM((wide, width), bf16),
            pltpu.SemaphoreType.DMA((5,)),
        ],
        compiler_params=params(),
        cost_estimate=cost(13),
        name="front_pass",
    )(order, tokens, *numers, *phis, incoming, gain, w_out, *pieces)


def feed_forward(pre):
    square = pre * pre
    swing = jnp.tanh(GELU_A * pre * (1.0 + GELU_B * square))
    half_up = 0.5 + 0.5 * swing
    slope = half_up + (0.5 * GELU_A) * pre * (1.0 - swing * swing) * (
        1.0 + (3.0 * GELU_B) * square
    )
    return (pre * half_up).astype(bf16), slope


def add_to(total, part):
    return part if total is None else total + part


def feed_kernel(tile, order, h_any, turned_any, d_any, *refs):
    ups, downs = refs[:4], refs[4:8]
    sums_out = (refs[8:10], refs[10:12])
    mixed_out, grad_out = refs[12:14]
    h, turned, d, up, down, mixed, grad_h, act, grad_pre, mixed_low, grad_low = refs[14:25]
    sums, sems, out_sems = refs[25:]
    step = pl.program_id(0)
    rows = h.shape[0]
    part = up.shape[2]
    quarter = part // 2
    block = 512
    blocks = rows // block

    def chunk_copies(at):
        run = pl.ds(block * at, block)
        return [
            pltpu.make_async_copy(h_any.at[run], h.at[run], sems.at[8 + 2 * at]),
            pltpu.make_async_copy(d_any.at[run], d.at[run], sems.at[9 + 2 * at]),
        ]

    def weight_copies(spot):
        copies = []
        for i in (2, 3) if spot == 0 else (0, 1):
            where = pl.multiple_of(order[2 + i] % 2 * quarter, 128)
            copies.append(
                pltpu.make_async_copy(
                    ups[i], up.at[spot, :, pl.ds(where, quarter)], sems.at[2 * i]
                )
            )
            where = pl.multiple_of(order[6 + i] % 2 * quarter, 16)
            copies.append(
                pltpu.make_async_copy(
                    downs[i].at[pl.ds(0, quarter)],
                    down.at[spot, pl.ds(where, quarter)],
                    sems.at[2 * i + 1],
                )
            )
        return copies

    def turned_copy():
        return pltpu.make_async_copy(turned_any, turned, sems.at[8 + 2 * blocks])

    def part_copies(at):
        run = pl.ds(block * at, block)
        return [
            pltpu.make_async_copy(mixed_low.at[run], mixed_out.at[run], out_sems.at[2 * at]),
            pltpu.make_async_copy(grad_low.at[run], grad_out.at[run], out_sems.at[2 * at + 1]),
        ]

    def sum_copies(spot):
        return [
            pltpu.make_async_copy(
                sums.at[spot, i], sums_out[spot][i], out_sems.at[2 * blocks + 2 * spot + i]
            )
            for i in range(2)
        ]

    @pl.when(step == 0)
    def _():
        for copy in weight_copies(0) + chunk_copies(0):
            copy.start()
        for at in range(1, blocks):
            for copy in chunk_copies(at):
                copy.start()
        turned_copy().start()
        for copy in weight_copies(1):
            copy.start()
        for copy in weight_copies(0):
            copy.wait()

    @pl.when(step == 1)
    def _():
        for copy in weight_copies(1):
            copy.wait()

    for at in range(blocks):
        run = slice(block * at, block * at + block)

        @pl.when(step == 0)
        def _(at=at):
            for copy in chunk_copies(at):
                copy.wait()

        mixed_part = grad_part = None
        for sub in range(0, part, tile):
            up_tile = up[step, :, sub : sub + tile]
            down_tile = down[step, sub : sub + tile, :]
            low, slope = feed_forward(dot(h[run, :], up_tile))
            grad = (dot_t(d[run, :], down_tile) * slope).astype(bf16)
            act[sub : sub + tile, run] = low.T
            grad_pre[run, sub : sub + tile] = grad
            mixed_part = add_to(mixed_part, dot(low, down_tile))
            grad_part = add_to(grad_part, dot_t(grad, up_tile))

        @pl.when(step == 0)
        def _(run=run, mixed_part=mixed_part, grad_part=grad_part):
            mixed[run, :] = mixed_part
            grad_h[run, :] = grad_part

        @pl.when(step == 1)
        def _(at=at, run=run, mixed_part=mixed_part, grad_part=grad_part):
            mixed_low[run, :] = (mixed[run, :] + mixed_part).astype(bf16)
            grad_low[run, :] = (grad_h[run, :] + grad_part).astype(bf16)
            for copy in part_copies(at):
                copy.start()

    @pl.when(step == 0)
    def _():
        turned_copy().wait()

    sums[step, 1] = dot(act[...], d[...]).astype(bf16)
    sums[step, 0] = dot(turned[...], grad_pre[...]).astype(bf16)

    @pl.when(step == 0)
    def _():
        for copy in sum_copies(0):
            copy.start()

    @pl.when(step == 1)
    def _():
        for copy in sum_copies(1):
            copy.start()
        for at in range(blocks):
            for copy in part_copies(at):
                copy.wait()
        for copy in sum_copies(0) + sum_copies(1):
            copy.wait()


def feed_pass(order, h, turned_h, d_out, ups, downs, tile):
    rows, width = h.shape
    part = 2 * ups[0].shape[1]
    square = (width, part)
    blocks = rows // 512
    return pl.pallas_call(
        functools.partial(feed_kernel, tile),
        grid=(2,),
        in_specs=[scalars] + [anywhere] * 11,
        out_specs=[anywhere] * 6,
        out_shape=[shaped(square), shaped((part, width))] * 2 + [shaped((rows, width))] * 2,
        scratch_shapes=[
            pltpu.VMEM((rows, width), bf16),
            pltpu.VMEM((width, rows), bf16),
            pltpu.VMEM((rows, width), bf16),
            pltpu.VMEM((2, width, part), bf16),
            pltpu.VMEM((2, part, width), bf16),
            pltpu.VMEM((rows, width), f32),
            pltpu.VMEM((rows, width), f32),
            pltpu.VMEM((part, rows), bf16),
            pltpu.VMEM((rows, part), bf16),
            pltpu.VMEM((rows, width), bf16),
            pltpu.VMEM((rows, width), bf16),
            pltpu.VMEM((2, 2, width, part), bf16),
            pltpu.SemaphoreType.DMA((9 + 2 * blocks,)),
            pltpu.SemaphoreType.DMA((4 + 2 * blocks,)),
        ],
        compiler_params=params(),
        cost_estimate=cost(32),
        name="feed_pass",
    )(order, h, turned_h, d_out, *ups, *downs)


def middle_kernel(pairs, tile, order, resid, h, d_out, *refs):
    mixed_part, grad_part, attended, inverse = refs[:4]
    phi = refs[4:6]
    gain, cross, wo_any, up_any, down_any = refs[6:11]
    pieces = refs[11:15]
    (
        act_out,
        pre_out,
        mixed_out,
        resid_out,
        gn_out,
        gd_out,
        turned_n_out,
        turned_d_out,
        state_out,
    ) = refs[15:24]
    state, wo_own, up, down, wo_oth, sems = refs[24:]
    step = pl.program_id(0)
    top = first_sublanes()
    wide = 128 * pairs
    units = up.shape[1]

    def early_copies():
        return [
            pltpu.make_async_copy(up_any, up, sems.at[0]),
            pltpu.make_async_copy(down_any, down, sems.at[1]),
        ]

    def late_copies():
        return [pltpu.make_async_copy(wo_any, wo_own, sems.at[2])] + quarter_copies(
            pieces, order, wo_oth, units // 4, wide // 4, sems, 3
        )

    @pl.when(step == 0)
    def _():
        for copy in early_copies() + late_copies():
            copy.start()
        state[...] = jnp.zeros_like(state)
        for copy in early_copies():
            copy.wait()

    h_two = h[...]
    d_low = d_out[...]
    mixed = grad_h = None
    for at in range(0, units, tile):
        low, slope = feed_forward(dot(h_two, up[:, at : at + tile]))
        grad_pre = (dot_t(d_low, down[at : at + tile, :]) * slope).astype(bf16)
        act_out[at : at + tile, :] = low.T
        for col in range(at, at + tile, 256):
            pre_out[col // 768, :, col % 768 : col % 768 + 256] = grad_pre[
                :, col - at : col - at + 256
            ]
        mixed = add_to(mixed, dot(low, down[at : at + tile, :]))
        grad_h = add_to(grad_h, dot_t(grad_pre, up[:, at : at + tile]))
    summed = resid[...].astype(f32)
    normed, spread = norm_parts(summed)
    mixed_out[...] = (summed + mixed_part[...].astype(f32) + mixed).astype(bf16)
    grad_h = grad_part[...].astype(f32) + grad_h
    grad_resid = (d_low.astype(f32) + norm_back(grad_h, normed, spread, gain[...])).astype(bf16)
    resid_out[...] = grad_resid

    @pl.when(step == 0)
    def _():
        for copy in late_copies():
            copy.wait()

    for half in range(2):
        grad_att = dot_t(grad_resid, (wo_own, wo_oth)[half][...]).astype(bf16).astype(f32)
        for p in range(pairs):
            at = wide * half + 128 * p
            own = grad_att[:, 128 * p : 128 * p + 128]
            scaled = own * inverse[:, at : at + 128].astype(f32)
            grad_n = scaled.astype(bf16)
            exact = attended[:, at : at + 128].astype(f32)
            grad_d = dot((scaled * exact).astype(bf16), cross[...]).astype(bf16)
            gn_out[:, at : at + 128] = grad_n
            gd_out[:, at : at + 128] = grad_d
            turned_n = grad_n.T
            turned_d = grad_d.T
            turned_n_out[at : at + 128, :] = turned_n
            turned_d_out[at : at + 128, :] = turned_d
            left = jnp.concatenate([turned_n, turned_d[0:16], turned_d[64:80]], axis=0)
            sums = dot(left, phi[half][:, 256 * p : 256 * p + 256])
            state[half, 128 * p : 128 * p + 128] += jnp.where(
                top, sums[:128, :128], sums[:128, 128:]
            )
            row = wide + 2 * p
            state[half, row : row + 1] += sums[144:145, :128]
            state[half, row + 1 : row + 2] += sums[128:129, 128:]

    @pl.when(step == pl.num_programs(0) - 1)
    def _():
        state_out[...] = state[...].astype(bf16)


def middle_pass(
    order, resid, h_two, d_out, parts, attended, inverse, phis, gain, cross, owns, pieces, packed, block, tile
):
    rows, width = resid.shape
    wide = owns[0].shape[0]
    pairs = wide // 128
    units = owns[1].shape[1]
    cols_out = [width, width, 2 * wide, 2 * wide]
    spots = units // 768
    return pl.pallas_call(
        functools.partial(middle_kernel, pairs, tile),
        grid=(rows // block,),
        in_specs=[scalars]
        + [by_rows(block, width)] * 5
        + [by_rows(block, 2 * wide)] * 4
        + [once(gain.shape), once(cross.shape)]
        + [anywhere] * 7,
        out_specs=[by_cols(units, block), pl.BlockSpec((spots, block, 768), lambda c: (0, c, 0))]
        + [by_rows(block, c) for c in cols_out]
        + [by_cols(2 * wide, block)] * 2
        + [once(packed)],
        out_shape=[shaped((units, rows)), shaped((spots, rows, 768))]
        + [shaped((rows, c)) for c in cols_out]
        + [shaped((2 * wide, rows))] * 2
        + [shaped(packed)],
        scratch_shapes=[
            pltpu.VMEM(packed, f32),
            pltpu.VMEM((wide, width), bf16),
            pltpu.VMEM((width, units), bf16),
            pltpu.VMEM((units, width), bf16),
            pltpu.VMEM((wide, width), bf16),
            pltpu.SemaphoreType.DMA((7,)),
        ],
        compiler_params=params(),
        cost_estimate=cost(35),
        name="middle_pass",
    )(order, resid, h_two, d_out, *parts, attended, inverse, *phis, gain, cross, *owns, *pieces)


def up_kernel(core, left, right, got, out):
    product = dot(left[...], right[0])
    mine = pl.program_id(0) == core[0]

    @pl.when(mine)
    def _():
        out[...] = (product + got[...].astype(f32)).astype(bf16)

    @pl.when(jnp.logical_not(mine))
    def _():
        out[...] = product.astype(bf16)


def up_pass(core, left, right, got):
    width, rows = left.shape
    count, _, part = right.shape
    return pl.pallas_call(
        up_kernel,
        grid_spec=pltpu.PrefetchScalarGridSpec(
            num_scalar_prefetch=1,
            grid=(count,),
            in_specs=[
                once((width, rows)),
                pl.BlockSpec((1, rows, part), lambda s, c: (s, 0, 0)),
                once((width, part)),
            ],
            out_specs=pl.BlockSpec((width, part), lambda s, c: (0, s)),
        ),
        out_shape=shaped((width, count * part)),
        compiler_params=params(),
        cost_estimate=cost(8),
        name="up_pass",
    )(core, left, right, got)


def down_kernel(core, left, right, own_left, oth_left, right_more, out, more_out):
    out[...] = dot(left[...], right[...]).astype(bf16)
    for side, rows in enumerate((own_left, oth_left)):
        more_out[side] = dot(rows[...], right_more[...]).astype(bf16)


def down_pass(half, left, right, left_more, right_more):
    rows, width = right.shape
    part = left.shape[0] // 2
    more = left_more.shape[0] // 4
    tile = width // 2
    cols = pl.BlockSpec((rows, tile), lambda s, half: (0, s))
    mine = lambda count, first: pl.BlockSpec((count, rows), lambda s, half: (first + half[0], 0))
    return pl.pallas_call(
        down_kernel,
        grid_spec=pltpu.PrefetchScalarGridSpec(
            num_scalar_prefetch=1,
            grid=(2,),
            in_specs=[mine(part, 0), cols, mine(more, 0), mine(more, 2), cols],
            out_specs=[
                pl.BlockSpec((part, tile), lambda s, half: (0, s)),
                pl.BlockSpec((2, more, tile), lambda s, half: (0, s, 0)),
            ],
        ),
        out_shape=[shaped((part, width)), shaped((2, 2 * more, tile))],
        compiler_params=params(),
        cost_estimate=cost(8),
        name="down_pass",
    )(half, left, right, left_more, left_more, right_more)


def back_kernel(pairs, at_pair, more, core, *refs):
    sides = (refs[:15], refs[15:30])
    incoming, later, ones, h_any = refs[30:34]
    earlier = refs[34 : 34 + more]
    grad_outs = refs[34 + more : 36 + more]
    send_out, keep_out, map_out = refs[36 + more : 39 + more]
    held, state, grads, maps, turned_h, sem = refs[39 + more :]
    step = pl.program_id(0)
    last = pl.num_programs(0) - 1
    first = first_lanes()
    top = first_sublanes()
    size = CHUNK
    inner = refs[2].shape[0] // CHUNK
    past = lax.broadcasted_iota(jnp.int32, (size, size), 0) >= lax.broadcasted_iota(
        jnp.int32, (size, size), 1
    )
    one = jnp.ones((1, 1), bf16)

    @pl.when(step == 0)
    def _():
        pltpu.make_async_copy(h_any, turned_h, sem.at[0]).start()
        maps[...] = jnp.zeros_like(maps)
        for side in range(2):
            for h_at in range(2):
                held[side, h_at] = read_state(incoming.at[side], at_pair, h_at, pairs)
                state[side, h_at] = read_state(later.at[side], at_pair, h_at, pairs)

    for sub in reversed(range(inner)):
        run = slice(CHUNK * sub, CHUNK * sub + CHUNK)
        for side in range(2):
            (q, k, v, turned_v, pq, turned_pq, pk, turned_pk) = sides[side][:8]
            (gn, gd, turned_n, turned_d, prefix, fq, fk) = sides[side][8:]
            grads_q, grads_k, grads_v = [], [], []
            for h_at in range(2):
                sel = first if h_at == 0 else jnp.logical_not(first)
                sel_top = top if h_at == 0 else jnp.logical_not(top)
                lanes = slice(128 * h_at, 128 * h_at + 128)
                padded_v = jnp.where(sel, v[run, :], one)
                padded_vt = jnp.where(sel_top, turned_v[:, run], one)
                padded_g = jnp.where(sel, gn[run, :], gd[run, :])
                padded_gt = jnp.where(sel_top, turned_n[:, run], turned_d[:, run])
                before = (prefix[sub, h_at].astype(f32) + held[side, h_at]).astype(bf16)
                after = state[side, h_at].astype(bf16)
                e = jnp.where(past, dot_t(padded_g, padded_v), 0.0).astype(bf16)
                s = jnp.where(past, dot(pq[run, lanes], turned_pk[lanes, run]), 0.0).astype(bf16)
                grads_q.append(dot(e, pk[run, lanes]) + dot(padded_g, before))
                grads_k.append(dot(turned_pq[lanes, run], e) + dot(after.T, padded_vt))
                grads_v.append(dot(padded_gt, s) + dot(after, turned_pk[lanes, run]))
                state[side, h_at] += dot(padded_gt, pq[run, lanes])

            grad_phi = jnp.concatenate(grads_q, axis=1)
            phi = pq[run, :].astype(f32)
            shared = dot((phi * grad_phi).astype(bf16), ones[...])
            grad_u = (phi * (grad_phi - shared)).astype(bf16)
            maps[side, 0] += dot(q[:, run], grad_u)
            grad_q = dot_t(grad_u, fq[0]).astype(bf16)

            grad_phi = jnp.concatenate(grads_k, axis=0).reshape(4, 64, size)
            phi = turned_pk[:, run].astype(f32).reshape(4, 64, size)
            shared = jnp.sum(phi * grad_phi, axis=1, keepdims=True)
            grad_u = (phi * (grad_phi - shared)).reshape(256, size).astype(bf16)
            maps[side, 1] += dot_t(k[:, run], grad_u)
            grad_k = dot(fk[0], grad_u).astype(bf16).T
            grad_v = jnp.where(top, grads_v[0], grads_v[1]).astype(bf16).T

            joined = jnp.concatenate([grad_q, grad_k, grad_v], axis=1)
            grad_outs[side][run, :] = joined
            where = pl.multiple_of(((last - step) * inner + sub) * size, size)
            grads[pl.ds(where, size), 384 * side : 384 * side + 384] = joined

    @pl.when(step == last)
    def _():
        pltpu.make_async_copy(h_any, turned_h, sem.at[0]).wait()
        product = dot(turned_h[...], grads[...]).astype(bf16)
        part = product.shape[0] // 2
        mine = core[0] == 0
        for side in range(2):
            cols = slice(384 * side, 384 * side + 384)
            low, high = product[:part, cols], product[part:, cols]
            send_out[side, 0:part] = jnp.where(mine, high, low)
            keep_out[side, 0:part] = jnp.where(mine, low, high)
            joins = [
                jnp.where(top, maps[side, i][:, :128], maps[side, i][:, 128:]) for i in range(2)
            ]
            turns = [pltpu.roll(j, 64, 1) for j in joins]
            own_map = jnp.where(first, joins[0] - turns[0], turns[1] - joins[1]).astype(bf16)
            map_out[side] = own_map
            if more:
                whole = jnp.concatenate([m[side] for m in earlier] + [own_map], axis=1)
                low, high = whole[:64], whole[64:]
                send_out[side, part : part + 64] = jnp.where(mine, high, low)
                keep_out[side, part : part + 64] = jnp.where(mine, low, high)
                send_out[side, part + 64 :] = jnp.zeros_like(low)
                keep_out[side, part + 64 :] = jnp.zeros_like(low)


def back_pass(at, core, sides, seconds, prefix, incoming, later, fq, fk, ones, turned_h, earlier):
    rows = sides[0][2].shape[0]
    pairs = fq[0].shape[0]
    width = turned_h.shape[0]
    count = rows // BLOCK
    here = lambda cols, spot: pl.BlockSpec((BLOCK, cols), lambda c, core: (count - 1 - c, spot))
    turned = lambda cols, spot: pl.BlockSpec((cols, BLOCK), lambda c, core: (spot, count - 1 - c))
    weights = pl.BlockSpec((1, 128, 256), lambda c, core: (at, 0, 0))
    states = pl.BlockSpec(
        (BLOCK // CHUNK, 2, 128, 128), lambda c, core: (count - 1 - c, at, 0, 0)
    )
    more = len(earlier)
    sums = (2, width // 2 + (128 if more else 0), 384)
    in_specs, args = [], []
    for side in range(2):
        both = pairs * side + at
        in_specs += [turned(128, at), turned(128, at), here(128, at), turned(128, at)]
        in_specs += [here(256, at), turned(256, at)] * 2
        in_specs += [here(128, both)] * 2 + [turned(128, both)] * 2
        in_specs += [states, weights, weights]
        args += [*sides[side], *seconds, prefix[side], fq[side], fk[side]]
    return pl.pallas_call(
        functools.partial(back_kernel, pairs, at, more),
        grid_spec=pltpu.PrefetchScalarGridSpec(
            num_scalar_prefetch=1,
            grid=(count,),
            in_specs=in_specs
            + [once(incoming.shape)] * 2
            + [once(ones.shape), anywhere]
            + [once((2, 128, 128))] * more,
            out_specs=[here(384, 0)] * 2 + [once(sums)] * 2 + [once((2, 128, 128))],
            scratch_shapes=[
                pltpu.VMEM((2, 2, 128, 128), f32),
                pltpu.VMEM((2, 2, 128, 128), f32),
                pltpu.VMEM((rows, 768), bf16),
                pltpu.VMEM((2, 2, 128, 256), f32),
                pltpu.VMEM((width, rows), bf16),
                pltpu.SemaphoreType.DMA((1,)),
            ],
        ),
        out_shape=[shaped((rows, 384))] * 2 + [shaped(sums)] * 2 + [shaped((2, 128, 128))],
        compiler_params=params(),
        cost_estimate=cost(17),
        name="back_pass",
    )(core, *args, incoming, later, ones, turned_h, *earlier)


def tokens_kernel(pairs, count, order, tokens, resid, gain, *refs):
    pieces = refs[: 1 + count]
    grads = refs[1 + count : 1 + count + 2 * pairs]
    out, w_own, w_oth, sems = refs[1 + count + 2 * pairs :]

    @pl.when(pl.program_id(0) == 0)
    def _():
        copies = qkv_copies(pieces[:1], order, (0, 1, 2), w_own, sems, 0)
        copies += qkv_copies(pieces[1:], order, (0, 1, 2), w_oth, sems, 3)
        run_copies(copies)

    normed, spread = norm_parts(tokens[...].astype(f32))
    total = None
    for half in range(2):
        joined = jnp.concatenate(
            [
                g[:, 128 * kind : 128 * kind + 128]
                for kind in range(3)
                for g in grads[half * pairs : half * pairs + pairs]
            ],
            axis=1,
        )
        part = dot_t(joined, (w_own, w_oth)[half][...])
        total = part if total is None else total + part
    back = norm_back(total, normed, spread, gain[...])
    out[...] = (resid[...].astype(f32) + back).astype(bf16)


def tokens_pass(order, tokens, resid, gain, w_own, pieces, grads, block, first, blocks, done=None):
    rows, width = tokens.shape
    pairs = len(grads) // 2
    cols = 3 * w_own.shape[2]
    count = len(pieces)
    cut = lambda cols: pl.BlockSpec((block, cols), lambda c: (first + c, 0))
    operands = [order, tokens, resid, gain, w_own, *pieces, *grads]
    more = [] if done is None else [done]

    def kernel(*refs):
        refs = list(refs)
        if more:
            del refs[len(operands)]
        tokens_kernel(pairs, count, *refs)

    return pl.pallas_call(
        kernel,
        grid=(blocks,),
        in_specs=[scalars]
        + [cut(width)] * 2
        + [once(gain.shape)]
        + [anywhere] * (1 + count)
        + [cut(384)] * len(grads)
        + [anywhere] * len(more),
        out_specs=cut(width),
        out_shape=shaped((rows, width)),
        input_output_aliases={len(operands): 0} if more else {},
        scratch_shapes=[
            pltpu.VMEM((width, cols), bf16),
            pltpu.VMEM((width, cols), bf16),
            pltpu.SemaphoreType.DMA((3 + 3 * count,)),
        ],
        compiler_params=params(),
        cost_estimate=cost(8),
        name="tokens_pass",
    )(*operands, *more)


def cross_to(value, axis, flip):
    count = lax.axis_size(axis)
    return lax.ppermute(value, axis, [(i, i ^ flip) for i in range(count)])


def swap(value, axis, bit):
    return cross_to(value, axis, 1 << bit)


def bit_of(axis, bit):
    return (lax.axis_index(axis) >> bit) & 1


def bits_of(axis):
    return lax.axis_size(axis).bit_length() - 1


def ordered(bit, mine, theirs, axis=0):
    return jnp.where(
        bit == 0,
        jnp.concatenate([mine, theirs], axis),
        jnp.concatenate([theirs, mine], axis),
    )


def add_low(*parts):
    total = parts[0].astype(f32)
    for part in parts[1:]:
        total = total + part.astype(f32)
    return total.astype(bf16)


class Flow:
    def __init__(self):
        self.ready = {}
        self.steps = {}
        self.done = {}

    def start(self, name, steps):
        self.steps[name] = steps
        self.ready[name] = next(steps)

    def slot(self, names, others):
        names = [n for n in names if n in self.steps]
        tied, others = lax.optimization_barrier(([self.ready[n] for n in names], others))
        for name, value in zip(names, tied):
            self.move(name, value)
        return others

    def move(self, name, value):
        try:
            self.ready[name] = self.steps[name].send(value)
        except StopIteration as end:
            self.done[name] = end.value
            del self.steps[name], self.ready[name]

    def finish(self, names):
        for name in names:
            while name in self.steps:
                self.move(name, self.ready[name])


def fetch_halves(weight, axis):
    count = weight.shape[axis] // 2
    part = yield lax.dynamic_slice_in_dim(weight, bit_of("ctx", 0) * count, count, axis)
    part = yield swap(part, "heads", 0)
    return [part, swap(part, "ctx", 0)]


def fetch_quarters(weights, across, axis):
    place = 2 * bit_of("ctx", 0) + bit_of(*across)
    parts = []
    for weight in weights:
        count = weight.shape[axis] // 4
        parts.append(lax.dynamic_slice_in_dim(weight, place * count, count, axis))
    part = yield jnp.concatenate(parts, axis)
    part = yield swap(part, "heads", 0)
    part, second, third = yield part, swap(part, *across), swap(part, "ctx", 0)
    return [part, second, third, swap(second, "ctx", 0)]


def fetch_order():
    core = bit_of("ctx", 0)
    order = [core, 1 - core]
    for across in (bit_of("ctx", 1), bit_of("batch", 0)):
        order += [
            2 * core + across,
            2 * core + 1 - across,
            2 - 2 * core + across,
            3 - 2 * core - across,
        ]
    return jnp.stack(order).astype(jnp.int32)


def reduce_sums(send, keep, ways, spread=False):
    send = yield send
    got = swap(send, "ctx", 0)
    left, oth = add_low(keep[0], got[0]), add_low(keep[1], got[1])
    return (yield from reduce_tail(left, [swap(oth, "heads", 0)], ways, spread))


def send_over(send, keep):
    send = yield send
    total = yield add_low(keep, swap(send, "ctx", 0))
    return (yield swap(total, "heads", 0))


def send_over_late(send, keep):
    send = yield send
    got = swap(send, "ctx", 0)
    count = keep.shape[0] // 2
    first, rest = yield [add_low(keep[i], got[i]) for i in (slice(0, count), slice(count, None))]
    first, rest = yield swap(first, "heads", 0), rest
    rest = yield rest
    return jnp.concatenate([first, (yield swap(rest, "heads", 0))])


def reduce_tail(left, rights, ways, spread=False):
    stages = [("ctx", b, 1) for b in range(1, bits_of("ctx"))]
    count = bits_of("batch")
    along = [("batch", b, min(ways, count - b)) for b in range(0, count, ways)]
    if not spread:
        stages += along
    for axis, low_bit, bits in stages:
        ways = 1 << bits
        place = (lax.axis_index(axis) >> low_bit) & (ways - 1)
        count = left.shape[0] // ways
        cut = lambda at: add_low(
            *[lax.dynamic_slice_in_dim(a, at * count, count, 0) for a in (left, *rights)]
        )
        sends = [cut(place ^ flip) for flip in range(1, ways)]
        left, sends = yield (cut(place), sends)
        rights = [cross_to(s, axis, (i + 1) << low_bit) for i, s in enumerate(sends)]
    whole = add_low(left, *rights)
    for axis, low_bit, bits in along if spread else []:
        whole = yield whole
        got = [cross_to(whole, axis, flip << low_bit) for flip in range(1, 1 << bits)]
        whole = add_low(whole, *got)
    for axis, low_bit, bits in reversed(stages):
        whole = yield whole
        parts = [whole] + [cross_to(whole, axis, flip << low_bit) for flip in range(1, 1 << bits)]
        for b in range(bits):
            bit = bit_of(axis, low_bit + b)
            parts = [ordered(bit, parts[i], parts[i + 1]) for i in range(0, len(parts), 2)]
        whole = parts[0]
    whole = yield whole
    return (yield (whole, swap(whole, "ctx", 0)))


def send_once(value, axis, bit):
    value = yield value
    return swap(value, axis, bit)


def scan_runs(total, boundary, rows, backward):
    place, side = lax.axis_index("ctx"), lax.axis_index("heads")
    second = lambda spot, half: (2 * spot + half) * rows >= boundary
    end = 0 if backward else 1
    total = yield total
    got = jnp.flip(swap(total, "heads", 0).astype(f32), 0)
    total = total.astype(f32)
    mine = second(place, side)
    joins = second(place, 0) == second(place, 1)
    received = jnp.where(jnp.logical_and(side == end, joins), got, 0.0)
    near = jnp.where(side == end, total, got)
    far = jnp.where(side == end, got, total)
    low = yield (near + jnp.where(joins, far, 0.0)).astype(bf16)
    for flip in range(1, lax.axis_size("ctx")):
        got = cross_to(low, "ctx", flip).astype(f32)
        spot = place ^ flip
        ahead = spot > place if backward else spot < place
        takes = jnp.logical_and(ahead, second(spot, end) == mine)
        received = received + jnp.where(takes, got, 0.0)
    received = yield received
    return received


def shards(tokens, lengths, gain_one, w_qkv, f_query, f_key, w_out, gain_two, w_up, w_down, d_out):
    rows, width = tokens.shape
    heads, size, _ = f_query.shape
    pairs = heads // 2
    wide = heads * size
    units = w_up.shape[1]
    assert size == 64 and lax.axis_size("heads") == 2 and 1536 % rows == 0
    boundary = lengths[0, 0]
    place = bit_of("ctx", 0)
    order = fetch_order()
    gain_one_row = gain_one.reshape(1, width)
    gain_two_row = gain_two.reshape(1, width)

    spots = np.arange(256) // 64
    ones = jnp.asarray(spots[:, None] == spots[None, :], bf16)
    cross = jnp.asarray((spots[:128, None] != spots[None, :128]) * (-1.0 / 64.0), bf16)
    signs = jnp.asarray(np.kron(np.array([[1, -1, 1, -1]]), np.eye(64)), bf16)

    flow = Flow()
    slot = flow.slot
    qkv_own = jnp.transpose(w_qkv, (1, 0, 2))
    maps_own = jnp.stack([f_query, f_key])
    flow.start("maps", send_once(maps_own, "heads", 0))
    flow.start("qkv", fetch_halves(qkv_own, 1))
    flow.start("up", fetch_quarters([w_up], ("ctx", 1), 1))
    flow.start("down", fetch_quarters([w_down, w_out], ("batch", 0), 0))
    (tokens,) = slot(["maps", "qkv"], (tokens,))

    h_one, turned_h = norm_one(tokens, gain_one_row)
    maps_oth = flow.done["maps"]
    keys = [key_pass(h_one, [qkv_own], order, maps_own, signs, [])]
    (keys[0][6], order, maps_oth, gain_two_row) = slot(
        ["qkv", "up", "down"], (keys[0][6], order, maps_oth, gain_two_row)
    )
    qkv_oth = flow.done["qkv"]
    keys.append(key_pass(h_one, qkv_oth, order, maps_oth, signs, [keys[0][6]]))
    flow.start("scan", scan_runs(keys[1][6], boundary, rows, False))
    (keys[1][1], order) = slot(["scan", "up"], (keys[1][1], order))
    queries = []
    for at, weights in enumerate(([qkv_own], qkv_oth)):
        queries.append(
            query_pass(
                h_one,
                weights,
                order,
                keys[at][4],
                keys[at][1],
                keys[at][5],
                (maps_own, maps_oth)[at],
                signs,
            )
        )
        if at == 0:
            (queries[0][0], order) = slot(["scan", "up", "down"], (queries[0][0], order))
    (queries[1][0], order) = slot(["scan", "down"], (queries[1][0], order))
    ups, downs, incoming = (flow.done[n] for n in ("up", "down", "scan"))
    q, phi_q, turned_pq, numer, _, fq = zip(*queries)
    k, v, turned_v, phi_k, turned_pk, prefix, _, _, fk = zip(*keys)

    attended, turned_a, inverse, resid, h_two, turned_two = front_pass(
        order, tokens, numer, phi_q, incoming, gain_two_row, w_out, downs, 512
    )
    send_up, send_down, keep_up, keep_down, *parts = feed_pass(
        order, h_two, turned_two, d_out, ups, downs, 768
    )
    flow.start("oth_up", send_over(send_up, keep_up))
    flow.start("oth_down", send_over_late(send_down, keep_down))
    slot(["oth_up", "oth_down"], ())
    (order,) = slot(["oth_up", "oth_down"], (order,))
    (
        act,
        grad_pre,
        mixed,
        grad_resid,
        gn,
        gd,
        turned_n,
        turned_gd,
        grad_totals,
    ) = middle_pass(
        order,
        resid,
        h_two,
        d_out,
        parts,
        attended,
        inverse,
        phi_q,
        gain_two_row,
        cross,
        (w_out, w_up, w_down),
        downs,
        incoming.shape,
        256,
        768,
    )
    flow.start("later", scan_runs(grad_totals, boundary, rows, True))
    near, away = place.reshape(1), (1 - place).reshape(1)
    (near, grad_pre) = slot(["later", "oth_up", "oth_down"], (near, grad_pre))
    up_sum = up_pass(near, turned_two, grad_pre, flow.done["oth_up"])
    (away, act, up_sum) = slot(["later", "oth_down"], (away, act, up_sum))
    everyone = ("batch", "ctx")
    up_sum = lax.psum_scatter(up_sum, everyone, scatter_dimension=0, tiled=True)
    send, out_send = down_pass(away, act, d_out, turned_a, grad_resid)
    flow.start("own_down", send_once(send, "ctx", 0))
    (near, out_send) = slot(["later", "own_down", "oth_down"], (near, out_send))
    keep_down, out_keep = down_pass(near, act, d_out, turned_a, grad_resid)
    got, right = flow.done["own_down"], flow.done["oth_down"]
    flow.start("down_sum", reduce_tail(keep_down, [got, right], 1))
    (near, out_keep) = slot(["down_sum"], (near, out_keep))
    later = flow.done["later"]

    grads, maps, sends, keeps = [[], []], [], [], []
    feeds = ["down_sum"]
    plan = [feeds, ["qkv0"] + feeds, ["qkv1", "qkv0"] + feeds]
    names = (q, k, v, turned_v, phi_q, turned_pq, phi_k, turned_pk)
    for at in range(pairs):
        own, oth, send, keep, map_part = back_pass(
            at,
            near,
            [[a[side] for a in names] for side in range(2)],
            [gn, gd, turned_n, turned_gd],
            prefix,
            incoming,
            later,
            fq,
            fk,
            ones,
            turned_h,
            maps if at == pairs - 1 else [],
        )
        grads[0].append(own)
        grads[1].append(oth)
        maps.append(map_part)
        sends.append(send)
        keeps.append(keep)
        if at == pairs - 2:
            flow.start(
                "qkv0",
                reduce_sums(
                    jnp.concatenate(sends + [out_send], axis=1),
                    jnp.concatenate(keeps + [out_keep], axis=1),
                    2,
                ),
            )
        if at == pairs - 1:
            flow.start("qkv1", reduce_sums(send, keep, 2))
        tied = (own, near) if at < pairs - 1 else (own, near, up_sum)
        (grads[0][at], near, *rest) = slot(plan[at], tied)
        if rest:
            (up_sum,) = rest
            up_sum = lax.all_gather(up_sum, everyone, axis=0, tiled=True)
    order = order + 0 * near[0]
    tokens_args = (tokens, grad_resid, gain_one_row, qkv_own, qkv_oth, grads[0] + grads[1], 384)
    blocks = rows // 384
    early = blocks // 2
    grad_tokens = tokens_pass(order, *tokens_args, 0, early)
    tail = ["qkv1", "qkv0"]
    (grad_tokens, order) = slot(tail + feeds, (grad_tokens, order))
    grad_tokens = tokens_pass(order, *tokens_args, early, blocks - early, grad_tokens)
    (grad_tokens,) = slot(tail + feeds, (grad_tokens,))
    (up_sum,) = slot(tail + feeds, (up_sum,))
    grad_up = up_sum.astype(f32)
    gain_two_part = jnp.sum(grad_up * w_up.astype(f32), axis=1)
    (grad_up, gain_two_part) = slot(tail + feeds, (grad_up, gain_two_part))
    flow.finish(feeds)
    grad_down = ordered(place, *flow.done["down_sum"]).astype(f32)
    (grad_down,) = slot(tail, (grad_down,))
    flow.finish(list(flow.steps))
    part = width // 2
    (mine, theirs), (mine_last, theirs_last) = flow.done["qkv0"], flow.done["qkv1"]
    join = lambda mine, theirs: ordered(place, mine, theirs)
    beside = lambda a: jnp.concatenate([a[: wide // 2], a[wide // 2 :]], axis=1)
    more = part * (pairs - 1)
    grad_out = join(beside(mine[more:]), beside(theirs[more:])).astype(f32)
    parts = [
        join(mine[part * at : part * at + part], theirs[part * at : part * at + part])
        for at in range(pairs - 1)
    ]
    parts.append(join(mine_last[:part], theirs_last[:part]))
    grad_qkv = jnp.stack(
        [
            jnp.concatenate([p[:, 128 * kind : 128 * kind + 128] for p in parts], axis=1)
            for kind in range(3)
        ]
    )
    grad_qkv = grad_qkv.astype(f32)
    gain_one_part = jnp.sum(grad_qkv * qkv_own.astype(f32), axis=(0, 2))
    gains = jnp.stack([gain_one_part, gain_two_part])
    gains = (gains + swap(gains, "heads", 0)) / jnp.stack([gain_one, gain_two])
    grad_qkv = jnp.transpose(grad_qkv, (1, 0, 2))
    maps_sum = join(mine_last[part : part + 64], theirs_last[part : part + 64]).astype(f32)
    maps_sum = maps_sum.reshape(2, 64, pairs, 2, 64).transpose(3, 2, 0, 1, 4)
    grad_maps = maps_sum.reshape(2, heads, size, size)
    return (
        mixed,
        grad_tokens,
        gains[0],
        grad_qkv,
        grad_maps[0],
        grad_maps[1],
        grad_out,
        gains[1],
        grad_up,
        grad_down,
    )


def solution(mesh):
    in_specs = (
        P(("batch", "ctx", "heads"), None),
        P("batch", None),
        P(),
        P(None, None, "heads"),
        P("heads", None, None),
        P("heads", None, None),
        P("heads", None),
        P(),
        P(None, "heads"),
        P("heads", None),
        P(("batch", "ctx", "heads"), None),
    )
    out_specs = (
        P(("batch", "ctx", "heads"), None),
        P(("batch", "ctx", "heads"), None),
        P(),
        P(None, None, "heads"),
        P("heads", None, None),
        P("heads", None, None),
        P("heads", None),
        P(),
        P(None, "heads"),
        P("heads", None),
    )
    return jax.shard_map(shards, mesh=mesh, in_specs=in_specs, out_specs=out_specs, check_vma=False)
```
